512 devices in a mesh: blk: 64 (over y_hi, x, z), group: 8 (over y_lo, core).
Axes of the slice: x: 4, y: 8 (y_hi: 2, y_lo: 4; y = y_hi * 4 + y_lo), z: 8, core: 2. Of those that a mesh axis runs over, the one named last changes fastest.
Arguments:
- images: bfloat16 [65536, 1152], P(('blk', 'group')), may hold values from -0.1875 to 0.1875
- captions: bfloat16 [65536, 1152], P(('blk', 'group')), may hold values from -0.1875 to 0.1875
- labels: int32 [65536], P(('blk', 'group')), may hold values from 0 to 1023
- logit_scale: float32 [1], replicated, may hold values from 4 to 12
- logit_bias: float32 [1], replicated, may hold values from -6 to -3
Outputs:
- loss_rows: float32 [65536], P(('blk', 'group'))
- image_grad: float32 [65536, 1152], P(('blk', 'group'))
- text_grad: float32 [65536, 1152], P(('blk', 'group'))
The draws below stay inside these ranges and needn't reach their ends.
Inputs may be any that keep to these rules, and one draw needn't show every extreme that they name: `labels`: the positive caption of an image in block b is caption row b * 1024 + label.
All inputs are finite; a program needn't handle non-finite values.
Results may differ from the reference program's by a relative error of at most 0.015.
Values may be sent and summed in bfloat16 or wider, within the bound.
A program may use at most 64 MiB of HBM per device.

```python
import jax
import jax.numpy as jnp
from jax import lax

D = 1152
I_DEV = 128
GROUP_TEXTS = 1024
IMAGES = 65536
TEXTS = 65536
N_BLK = 64
N_GROUP = 8


def with_ends(array, own_key, least, top_value):
    extent = array.shape
    index_at = [jax.random.randint(jax.random.fold_in(own_key, axis), (), 0, extent[axis]) for axis in range(len(extent))]
    array = array.at[tuple(index_at)].set(least)
    longest = extent.index(max(extent))
    index_at[longest] = (index_at[longest] + 1) % extent[longest]
    return array.at[tuple(index_at)].set(top_value)


def levels(stream_key, extent, pieces, low, top_value):
    factor_of = 1.0
    for position, parts in pieces:
        heights = jax.random.uniform(jax.random.fold_in(jax.random.fold_in(stream_key, 6), position), (parts,), jnp.float32, low / len(pieces), top_value / len(pieces))
        factor_of = factor_of * jnp.repeat(jnp.exp(heights), extent[position] // parts).reshape((-1,) + (1,) * (len(extent) - 1 - position))
    return factor_of


def gaussian(own_key, dims, scale, reach, split=(), kind=jnp.bfloat16):
    result = jax.random.normal(own_key, dims, jnp.float32) * scale
    if len(split) > 0:
        result = levels(own_key, dims, split, -0.22, 0.18) * result
    return jnp.clip(result, min=-reach, max=reach).astype(kind)


def setup_inputs(seed: int = 0) -> dict:
    keys = jax.random.split(jax.random.key(seed), 6)
    images = gaussian(keys[0], (IMAGES, D), (D ** -0.5), 0.1875, ((0, 512),))
    captions = gaussian(keys[1], (TEXTS, D), (D ** -0.5), 0.1875, ((0, 512),))
    labels = with_ends(jax.random.randint(keys[2], (IMAGES,), 0, GROUP_TEXTS), jax.random.fold_in(keys[2], 1), 0, GROUP_TEXTS - 1).astype(jnp.int32)
    logit_scale = jnp.clip(jax.random.uniform(keys[3], (1,), jnp.float32, 4.0, 12.0), 4.0, 12.0)
    logit_bias = jnp.clip(jax.random.uniform(keys[4], (1,), jnp.float32, -6.0, -3.0), -6.0, -3.0)
    return {"images": images, "captions": captions, "labels": labels, "logit_scale": logit_scale, "logit_bias": logit_bias}


EPSILON = 1e-06

def unit_rows(values):
    wide = values.astype(jnp.float32)
    length = jnp.sqrt(lax.optimization_barrier(jnp.sum(wide * wide, axis=-1, keepdims=True)) + EPSILON)
    return (wide / length, length)

def pair_tile(image_block, text_block, label_block, diagonal, scale_value, bias_value):
    raw = lax.dot_general(image_block, text_block, (((1,), (1,)), ((), ())), preferred_element_type=jnp.float32)
    logits = scale_value * raw + bias_value
    columns = lax.broadcasted_iota(jnp.int32, logits.shape, 1)
    positive = jnp.logical_and(diagonal, columns == label_block[:, None])
    signed = jnp.where(positive, logits, -logits)
    row_loss = -lax.optimization_barrier(jnp.sum(jax.nn.log_sigmoid(signed), axis=1))
    slope = jnp.where(positive, -1.0, 1.0) * jax.nn.sigmoid(-signed)
    weights = (scale_value * slope).astype(jnp.bfloat16)
    image_part = jnp.dot(weights, text_block, preferred_element_type=jnp.float32)
    grouped_weights = weights.astype(jnp.float32).reshape(N_GROUP, I_DEV, weights.shape[1])
    grouped_images = image_block.astype(jnp.float32).reshape(N_GROUP, I_DEV, image_block.shape[1])
    text_parts = jnp.einsum('gic,gid->gcd', grouped_weights, grouped_images, precision=lax.Precision.HIGHEST)
    return (row_loss, image_part, text_parts.astype(jnp.bfloat16))

def through_norm(sums, unit_float, length):
    return (sums - unit_float * lax.optimization_barrier(jnp.sum(unit_float * sums, axis=-1, keepdims=True))) / length

def reference(images, captions, labels, logit_scale, logit_bias):
    scale_value = logit_scale[0]
    bias_value = logit_bias[0]
    width = images.shape[1]
    image_float, image_length = unit_rows(images)
    image_unit = image_float.astype(jnp.bfloat16)
    text_float, text_length = unit_rows(captions)
    text_unit = text_float.astype(jnp.bfloat16)
    image_blocks = image_unit.reshape(N_BLK, GROUP_TEXTS, width)
    label_blocks = labels.reshape(N_BLK, GROUP_TEXTS)
    text_blocks = text_unit.reshape(N_BLK, GROUP_TEXTS, width)

    def visit(carry, target):
        loss_all, image_all = carry
        text_block = lax.dynamic_index_in_dim(text_blocks, target, 0, keepdims=False)
        partial_value = jnp.zeros((N_GROUP, GROUP_TEXTS, width), jnp.float32)
        for offset in (-1, 0, 1):
            source = ((target - offset) % N_BLK).astype(jnp.int32)
            image_block = lax.dynamic_index_in_dim(image_blocks, source, 0, keepdims=False)
            label_block = lax.dynamic_index_in_dim(label_blocks, source, 0, keepdims=False)
            row_loss, image_part, text_bits = pair_tile(image_block, text_block, label_block, offset == 0, scale_value, bias_value)
            old_loss = lax.dynamic_index_in_dim(loss_all, source, 0, keepdims=False)
            loss_all = lax.dynamic_update_index_in_dim(loss_all, old_loss + row_loss, source, 0)
            old_image = lax.dynamic_index_in_dim(image_all, source, 0, keepdims=False)
            image_all = lax.dynamic_update_index_in_dim(image_all, old_image + image_part, source, 0)
            partial_value = partial_value + lax.optimization_barrier(text_bits).astype(jnp.float32)
        rounded = lax.optimization_barrier(partial_value.astype(jnp.bfloat16)).astype(jnp.float32)
        return ((loss_all, image_all), lax.optimization_barrier(jnp.sum(rounded, axis=0)))
    start = (jnp.zeros((N_BLK, GROUP_TEXTS), jnp.float32), jnp.zeros((N_BLK, GROUP_TEXTS, width), jnp.float32))
    indices = jnp.arange(N_BLK, dtype=jnp.int32)
    (loss_all, image_all), text_sums = lax.scan(visit, start, indices)
    image_grad = through_norm(image_all.reshape(-1, width), image_float, image_length)
    text_grad = through_norm(text_sums.reshape(-1, width), text_float, text_length)
    return (loss_all.reshape(-1), image_grad, text_grad)
```

```python
import jax
import jax.numpy as jnp
from jax import lax
from jax.sharding import PartitionSpec as P

EPSILON = 1e-06


def unit_rows(values):
    wide = values.astype(jnp.float32)
    length = jnp.sqrt(jnp.sum(wide * wide, axis=-1, keepdims=True) + EPSILON)
    return (wide / length, length)


def through_norm(sums, unit_float, length):
    return (sums - unit_float * jnp.sum(unit_float * sums, axis=-1, keepdims=True)) / length


def block_pairs(blocks, members):
    half = blocks // 2
    pairs = []
    for block in range(blocks):
        for member in range(members):
            partner = member
            if block % half == half - 1:
                chip, core = divmod(member, 2)
                partner = (members // 2 - 1 - chip) * 2 + core
            pairs.append((block * members + member, ((block + 1) % blocks) * members + partner))
    return pairs


def per_device(blocks, members, images, captions, labels, logit_scale, logit_bias):
    scale_value = logit_scale[0]
    bias_value = logit_bias[0]
    up = block_pairs(blocks, members)
    down = [(target, source) for source, target in up]
    image_float, image_length = unit_rows(images)
    image_unit = image_float.astype(jnp.bfloat16)
    text_float, text_length = unit_rows(captions)
    text_unit = text_float.astype(jnp.bfloat16)
    all_labels = lax.all_gather(labels, "group", axis=0, tiled=True)
    all_images = lax.all_gather(image_unit, "group", axis=0, tiled=True)
    lower = lax.ppermute(text_unit, ("blk", "group"), up)
    upper = lax.ppermute(text_unit, ("blk", "group"), down)
    texts = jnp.concatenate([text_unit, lower, upper], axis=0)
    raw = lax.dot_general(
        all_images, texts, (((1,), (1,)), ((), ())), preferred_element_type=jnp.float32
    )
    logits = scale_value * raw + bias_value
    rows = labels.shape[0]
    columns = lax.broadcasted_iota(jnp.int32, logits.shape, 1)
    wanted = all_labels - lax.axis_index("group") * rows
    positive = jnp.logical_and(columns < rows, columns == wanted[:, None])
    signed = jnp.where(positive, logits, -logits)
    row_loss = -jnp.sum(jax.nn.log_sigmoid(signed), axis=1)
    slope = jnp.where(positive, -1.0, 1.0) * jax.nn.sigmoid(-signed)
    weights = (scale_value * slope).astype(jnp.bfloat16)
    text_part = lax.dot_general(
        weights, all_images, (((0,), (0,)), ((), ())), preferred_element_type=jnp.float32
    )
    from_above = lax.ppermute(text_part[rows : 2 * rows].astype(jnp.bfloat16), ("blk", "group"), down)
    from_below = lax.ppermute(text_part[2 * rows :].astype(jnp.bfloat16), ("blk", "group"), up)
    image_part = jnp.dot(weights, texts, preferred_element_type=jnp.float32)
    image_sums = lax.psum_scatter(
        image_part.astype(jnp.bfloat16), "group", scatter_dimension=0, tiled=True
    ).astype(jnp.float32)
    loss_rows = lax.psum_scatter(row_loss, "group", scatter_dimension=0, tiled=True)
    text_sums = text_part[:rows] + from_above.astype(jnp.float32) + from_below.astype(jnp.float32)
    image_grad = through_norm(image_sums, image_float, image_length)
    text_grad = through_norm(text_sums, text_float, text_length)
    return (loss_rows, image_grad, text_grad)


def solution(mesh):
    blocks, members = mesh.shape["blk"], mesh.shape["group"]

    def body(*arrays):
        return per_device(blocks, members, *arrays)

    in_specs = (P(("blk", "group"), None), P(("blk", "group"), None), P(("blk", "group")), P(), P())
    out_specs = (P(("blk", "group")), P(("blk", "group"), None), P(("blk", "group"), None))
    return jax.shard_map(body, mesh=mesh, in_specs=in_specs, out_specs=out_specs, check_vma=False)
```

```python
import functools

import jax
import jax.numpy as jnp
from jax import lax
from jax.experimental import pallas as pl
from jax.experimental.pallas import tpu as pltpu
from jax.sharding import PartitionSpec as P

EPSILON = 1e-06
CHIPS = 4
AG_CHUNKS = 2
RS_CHUNKS = 4
MESH = pl.DeviceIdType.MESH
F32 = jnp.float32
BF16 = jnp.bfloat16


def unit_rows(values):
    wide = values.astype(F32)
    length = jnp.sqrt(jnp.sum(wide * wide, axis=-1, keepdims=True) + EPSILON)
    return (wide / length, length)


def through_norm(sums, unit_float, length):
    return (sums - unit_float * jnp.sum(unit_float * sums, axis=-1, keepdims=True)) / length


def pair_weights(raw, positive, scale, bias):
    turned = scale * raw + bias
    if positive is not None:
        turned = jnp.where(positive, -turned, turned)
    decay = jnp.exp(-jnp.abs(turned))
    loss = jnp.maximum(turned, 0.0) + jnp.log1p(decay)
    share = jnp.where(turned >= 0, 1.0, decay) / (1.0 + decay)
    if positive is not None:
        share = jnp.where(positive, -share, share)
    return (jnp.sum(loss, axis=0, keepdims=True), (scale * share).astype(BF16))


def kernel(
    blocks,
    images,
    captions,
    labels,
    scale_ref,
    bias_ref,
    loss_out,
    image_out,
    text_out,
    imgs,
    texts,
    labs,
    loss_part,
    loss_in,
    parts,
    parts_out,
    parts_in,
    sums,
    sums_out,
    sums_in,
    back_out,
    back_in,
    ag_own_send,
    ag_fwd_send,
    ag_recv,
    lab_send,
    lab_recv,
    loss_send,
    loss_recv,
    core_send,
    core_recv,
    next_send,
    next_recv,
    rs_send,
    rs_recv,
    sum_send,
    sum_recv,
    back_send,
    back_recv,
):
    rows = images.shape[0]
    ag_rows = rows // AG_CHUNKS
    rs_rows = rows // RS_CHUNKS
    blk = lax.axis_index("blk")
    group = lax.axis_index("group")
    y = group // 2
    core = group % 2
    other = group + 1 - 2 * core
    half = blocks // 2
    mirror = 2 * (CHIPS - 1 - 2 * y)
    up_dev = {
        "blk": (blk + 1) % blocks,
        "group": group + ((blk % half) // (half - 1)) * mirror,
    }
    down_dev = {
        "blk": (blk + blocks - 1) % blocks,
        "group": group + ((half - 1 - blk % half) // (half - 1)) * mirror,
    }
    other_dev = {"blk": blk, "group": other}

    def chip(position):
        return {"blk": blk, "group": (position + CHIPS) % CHIPS * 2 + core}

    def remote(src, dst, send, recv, device):
        return pltpu.make_async_remote_copy(
            src_ref=src, dst_ref=dst, send_sem=send, recv_sem=recv, device_id=device, device_id_type=MESH
        )

    is_end = (y == 0) | (y == CHIPS - 1)
    is_middle = (y == 1) | (y == 2)

    barrier = pltpu.get_barrier_semaphore()
    for device in [up_dev, down_dev, other_dev] + [chip((y + d) % CHIPS) for d in (1, 2, 3)]:
        pl.semaphore_signal(barrier, inc=1, device_id=device, device_id_type=MESH)

    image_float, _ = unit_rows(images[...])
    imgs[y] = image_float.astype(BF16)
    text_float, _ = unit_rows(captions[...])
    texts[0:rows, :] = text_float.astype(BF16)
    labs[y] = labels[...]

    pl.semaphore_wait(barrier, 6)

    def own_copy(c, direction):
        part = imgs.at[y, pl.ds(c * ag_rows, ag_rows)]
        return remote(
            part, part, ag_own_send.at[direction, c], ag_recv.at[y, c], chip(y + 1 - 2 * direction)
        )

    def fwd_copy(s, c):
        part = imgs.at[s, pl.ds(c * ag_rows, ag_rows)]
        target = jnp.where(s < y, y + 1, y - 1)
        return remote(part, part, ag_fwd_send.at[s, c], ag_recv.at[s, c], chip(target))

    def slot(i):
        return texts.at[pl.ds(i * rows, rows)]

    next_up = remote(slot(0), slot(2), next_send.at[0], next_recv.at[0], up_dev)
    next_down = remote(slot(0), slot(4), next_send.at[1], next_recv.at[1], down_dev)
    core_copies = [
        remote(slot(2 * i), slot(2 * i + 1), core_send.at[i], core_recv.at[i], other_dev) for i in range(3)
    ]

    for c in range(AG_CHUNKS):

        @pl.when(y < CHIPS - 1)
        def _():
            own_copy(c, 0).start()

        @pl.when(y > 0)
        def _():
            own_copy(c, 1).start()

    next_up.start()
    next_down.start()
    core_copies[0].start()
    lab_copies = [
        remote(labs.at[y], labs.at[y], lab_send.at[d - 1], lab_recv.at[y], chip((y + d) % CHIPS))
        for d in (1, 2, 3)
    ]
    for copy in lab_copies:
        copy.start()

    next_up.wait_recv()
    core_copies[1].start()
    next_down.wait_recv()
    core_copies[2].start()
    for copy in core_copies:
        copy.wait_recv()

    scale = scale_ref[0]
    bias = bias_ref[0]

    def arrive(s):
        for c in range(AG_CHUNKS):
            fwd = fwd_copy(s, c)
            fwd.wait_recv()

            @pl.when(is_middle)
            def _():
                fwd.start()

        remote(labs.at[s], labs.at[s], lab_send.at[0], lab_recv.at[s], chip(y + 1)).wait_recv()

    def compute(s, first):
        image = imgs[s]
        label = labs[s]
        loss = None
        part = None
        for i in range(3):
            text = texts[2 * i * rows : 2 * (i + 1) * rows, :]
            raw = lax.dot_general(text, image, (((1,), (1,)), ((), ())), preferred_element_type=F32)
            positive = None
            if i == 0:
                index = lax.broadcasted_iota(jnp.int32, raw.shape, 0)
                column = jnp.where(index < rows, group * rows + index, other * rows + index - rows)
                positive = column == label
            loss_i, weights = pair_weights(raw, positive, scale, bias)
            part_i = lax.dot_general(
                weights, text, (((0,), (0,)), ((), ())), preferred_element_type=F32
            )
            sum_i = jnp.dot(weights, image, preferred_element_type=F32)
            where = pl.ds(2 * i * rows, 2 * rows)
            if first:
                sums[where, :] = sum_i
            else:
                sums[where, :] += sum_i
            loss = loss_i if i == 0 else loss + loss_i
            part = part_i if i == 0 else part + part_i
        parts[s] = part
        loss_part[s] = loss

    def rs_copy(t, c, direction):
        where = pl.ds(c * rs_rows, rs_rows)
        return remote(
            parts_out.at[t, where],
            parts_in.at[direction, t, where],
            rs_send.at[t, c],
            rs_recv.at[direction, t, c],
            chip(y + 1 - 2 * direction),
        )

    end_direction = y // (CHIPS - 1)
    compute(y, True)

    def step(k, carry):
        ascending = jnp.where((y == 1) & (k == 1), 0, k)
        s = jnp.where(y < 2, ascending, CHIPS - 1 - jnp.where((y == 2) & (k == 1), 0, k))

        @pl.when((k == 1) | (k == 3) | is_end)
        def _():
            arrive(s)

        @pl.when((k == 1) & is_middle)
        def _():
            arrive(jnp.where(y == 1, 2, 1))

        compute(s, False)

        @pl.when(is_end)
        def _():
            parts_out[s] = parts[s].astype(BF16)
            for c in range(RS_CHUNKS):
                rs_copy(s, c, end_direction).start()

        return carry

    lax.fori_loop(1, CHIPS, step, 0)

    loss_copies = [
        remote(
            loss_part.at[(y + d) % CHIPS],
            loss_in.at[y],
            loss_send.at[d - 1],
            loss_recv.at[y],
            chip((y + d) % CHIPS),
        )
        for d in (1, 2, 3)
    ]
    for copy in loss_copies:
        copy.start()

    sum_copies = [
        remote(sums_out.at[i], sums_in.at[i], sum_send.at[i], sum_recv.at[i], other_dev) for i in range(3)
    ]
    back_copies = [
        remote(back_out.at[0], back_in.at[1], back_send.at[0], back_recv.at[1], down_dev),
        remote(back_out.at[1], back_in.at[0], back_send.at[1], back_recv.at[0], up_dev),
    ]
    for i in (1, 2, 0):
        sums_out[i] = sums[(2 * i + 1) * rows : (2 * i + 2) * rows, :].astype(BF16)
        sum_copies[i].start()
    for i in (1, 2):
        sum_copies[i].wait_recv()
        total = sums[2 * i * rows : (2 * i + 1) * rows, :] + sums_in[i].astype(F32)
        back_out[i - 1] = total.astype(BF16)
        back_copies[i - 1].start()

    def pass_on(t, c, direction):
        copy = rs_copy(t, c, direction)
        where = pl.ds(c * rs_rows, rs_rows)
        copy.wait_recv()
        total = parts[t, where, :] + parts_in[direction, t, where, :].astype(F32)
        parts_out[t, where, :] = total.astype(BF16)
        copy.start()

    @pl.when(is_middle)
    def _():
        inner = 3 - y
        outer = jnp.where(y == 1, 0, 3)
        far = 3 - outer
        inward = y - 1
        outward = 2 - y

        def near(c, carry):
            pass_on(inner, c, inward)
            return carry

        lax.fori_loop(0, RS_CHUNKS, near, 0)

        def ends(c, carry):
            pass_on(far, c, inward)
            pass_on(outer, c, outward)
            return carry

        lax.fori_loop(0, RS_CHUNKS, ends, 0)

    sum_copies[0].wait_recv()
    text_sums = sums[0:rows, :] + sums_in[0].astype(F32)
    for i in range(2):
        back_copies[1 - i].wait_recv()
        text_sums = text_sums + back_in[i].astype(F32)
    text_float, text_length = unit_rows(captions[...])
    text_out[...] = through_norm(text_sums, text_float, text_length)

    loss_total = loss_part[y]
    for d in (1, 2, 3):
        s = (y + d) % CHIPS
        remote(loss_part.at[s], loss_in.at[s], loss_send.at[0], loss_recv.at[s], chip(y + 1)).wait_recv()
        loss_total = loss_total + loss_in[s]
    loss_out[...] = loss_total

    for direction in (0, 1):

        @pl.when((y > 0) if direction == 0 else (y < CHIPS - 1))
        def _():
            for c in range(RS_CHUNKS):
                rs_copy(y, c, direction).wait_recv()
            parts[y] += parts_in[direction, y].astype(F32)

    image_float, image_length = unit_rows(images[...])
    image_out[...] = through_norm(parts[y], image_float, image_length)

    for c in range(AG_CHUNKS):

        @pl.when(y < CHIPS - 1)
        def _():
            own_copy(c, 0).wait_send()

        @pl.when(y > 0)
        def _():
            own_copy(c, 1).wait_send()

    for d in (1, 2, 3):
        s = (y + d) % CHIPS

        @pl.when(is_middle)
        def _():
            for c in range(AG_CHUNKS):
                fwd_copy(s, c).wait_send()

        for c in range(RS_CHUNKS):
            rs_copy(s, c, 0).wait_send()
    for copy in [next_up, next_down] + core_copies + lab_copies + loss_copies + sum_copies + back_copies:
        copy.wait_send()


def per_device(blocks, images, captions, labels, logit_scale, logit_bias):
    rows, width = images.shape
    vmem = pl.BlockSpec(memory_space=pltpu.VMEM)
    smem = pl.BlockSpec(memory_space=pltpu.SMEM)
    dma = pltpu.SemaphoreType.DMA
    loss, image_grad, text_grad = pl.pallas_call(
        functools.partial(kernel, blocks),
        out_shape=[
            jax.ShapeDtypeStruct((1, rows), F32),
            jax.ShapeDtypeStruct((rows, width), F32),
            jax.ShapeDtypeStruct((rows, width), F32),
        ],
        in_specs=[vmem, vmem, vmem, smem, smem],
        out_specs=[vmem, vmem, vmem],
        scratch_shapes=[
            pltpu.VMEM((CHIPS, rows, width), BF16),
            pltpu.VMEM((6 * rows, width), BF16),
            pltpu.VMEM((CHIPS, 1, rows), jnp.int32),
            pltpu.VMEM((CHIPS, 1, rows), F32),
            pltpu.VMEM((CHIPS, 1, rows), F32),
            pltpu.VMEM((CHIPS, rows, width), F32),
            pltpu.VMEM((CHIPS, rows, width), BF16),
            pltpu.VMEM((2, CHIPS, rows, width), BF16),
            pltpu.VMEM((6 * rows, width), F32),
            pltpu.VMEM((3, rows, width), BF16),
            pltpu.VMEM((3, rows, width), BF16),
            pltpu.VMEM((2, rows, width), BF16),
            pltpu.VMEM((2, rows, width), BF16),
            dma((2, AG_CHUNKS)),
            dma((CHIPS, AG_CHUNKS)),
            dma((CHIPS, AG_CHUNKS)),
            dma((3,)),
            dma((CHIPS,)),
            dma((3,)),
            dma((CHIPS,)),
            dma((3,)),
            dma((3,)),
            dma((2,)),
            dma((2,)),
            dma((CHIPS, RS_CHUNKS)),
            dma((2, CHIPS, RS_CHUNKS)),
            dma((3,)),
            dma((3,)),
            dma((2,)),
            dma((2,)),
        ],
        compiler_params=pltpu.CompilerParams(
            collective_id=0, has_side_effects=True, vmem_limit_bytes=48 * 1024 * 1024
        ),
    )(images, captions, labels.reshape(1, rows), logit_scale, logit_bias)
    return (loss.reshape(rows), image_grad, text_grad)


def solution(mesh):
    body = functools.partial(per_device, mesh.shape["blk"])
    in_specs = (P(("blk", "group"), None), P(("blk", "group"), None), P(("blk", "group")), P(), P())
    out_specs = (P(("blk", "group")), P(("blk", "group"), None), P(("blk", "group"), None))
    return jax.shard_map(body, mesh=mesh, in_specs=in_specs, out_specs=out_specs, check_vma=False)
```

```python
import functools

import jax
import jax.numpy as jnp
from jax import lax
from jax.experimental import pallas as pl
from jax.experimental.pallas import tpu as pltpu
from jax.sharding import PartitionSpec as P

EPSILON = 1e-06
CHIPS = 4
LINE = 8
AG_CHUNKS = 2
RS_CHUNKS = 8
RELAY_CHUNKS = 2
MESH = pl.DeviceIdType.MESH
F32 = jnp.float32
BF16 = jnp.bfloat16


def unit_rows(values):
    wide = values.astype(F32)
    length = jnp.sqrt(jnp.sum(wide * wide, axis=-1, keepdims=True) + EPSILON)
    return (wide / length, length)


def through_norm(sums, unit_float, length):
    return (sums - unit_float * jnp.sum(unit_float * sums, axis=-1, keepdims=True)) / length


def depth_part(a, b, start, stop):
    return lax.dot_general(
        a[:, start:stop], b[:, start:stop], (((1,), (1,)), ((), ())), preferred_element_type=F32
    )


def summed_log(decay):
    pieces = [decay[i : i + 8, :] for i in range(0, decay.shape[0], 8)]
    while len(pieces) > 1:
        pieces = [a + b + a * b for a, b in zip(pieces[::2], pieces[1::2])]
    return jnp.sum(jnp.log1p(pieces[0]), axis=0, keepdims=True)


def pair_weights(raw, positive, scale, bias):
    logits = scale * raw + bias
    turned = jnp.where(positive, -logits, logits)
    decay = jnp.exp(-jnp.abs(turned))
    loss = jnp.sum(jnp.maximum(turned, 0.0), axis=0, keepdims=True) + summed_log(decay)
    share = jnp.where(turned >= 0, 1.0, decay) / (1.0 + decay)
    weights = jnp.where(positive, -scale, scale) * share
    return (loss, weights.astype(BF16))


def kernel(
    blocks,
    images_hbm,
    captions_hbm,
    labels_hbm,
    scale_ref,
    bias_ref,
    loss_out,
    image_out,
    text_out,
    images,
    captions,
    imgs,
    texts,
    labs,
    loss_part,
    loss_in,
    parts,
    parts_out,
    end_in,
    mid_in,
    sums,
    sums_out,
    sums_in,
    back_out,
    back_in,
    relay_in,
    load_sem,
    ag_own_send,
    ag_fwd_send,
    ag_recv,
    lab_send,
    lab_recv,
    loss_send,
    loss_recv,
    core_send,
    core_recv,
    next_send,
    next_recv,
    end_send,
    end_recv,
    mid_send,
    mid_recv,
    sum_send,
    sum_recv,
    back_send,
    back_recv,
    relay_src_send,
    relay_recv,
    relay_fwd_send,
):
    rows = images.shape[0]
    ag_rows = rows // AG_CHUNKS
    rs_rows = rows // RS_CHUNKS
    relay_rows = rows // RELAY_CHUNKS
    blk = lax.axis_index("blk")
    group = lax.axis_index("group")
    y = group // 2
    core = group % 2
    other = group + 1 - 2 * core
    half = blocks // 2
    mirrored = 2 * (CHIPS - 1 - y) + core
    up_edge = (blk % half) // (half - 1)
    down_edge = (half - 1 - blk % half) // (half - 1)
    up_dev = {"blk": (blk + 1) % blocks, "group": group + up_edge * (mirrored - group)}
    down_dev = {"blk": (blk + blocks - 1) % blocks, "group": group + down_edge * (mirrored - group)}
    on_up = jnp.where(blk % half == LINE - 1, 1, 0)
    on_down = jnp.where(blk % half == half - LINE, 1, 0)
    shift = half - LINE
    via_dev = {"blk": blk + shift * (down_edge - up_edge), "group": group}
    from_dev = {"blk": (blk + blocks + (shift + 1) * (up_edge - down_edge)) % blocks, "group": mirrored}
    source_dev = {"blk": blk + shift * (on_up - on_down), "group": group}
    target_dev = {"blk": (blk + blocks + (shift + 1) * (on_up - on_down)) % blocks, "group": mirrored}
    other_dev = {"blk": blk, "group": other}

    def chip(position):
        return {"blk": blk, "group": (position + CHIPS) % CHIPS * 2 + core}

    def remote(src, dst, send, recv, device):
        return pltpu.make_async_remote_copy(
            src_ref=src, dst_ref=dst, send_sem=send, recv_sem=recv, device_id=device, device_id_type=MESH
        )

    is_end = (y == 0) | (y == CHIPS - 1)
    is_middle = (y == 1) | (y == 2)
    relayed_up = is_middle & (up_edge == 1)
    relayed_down = is_middle & (down_edge == 1)
    relayed = is_middle & (up_edge + down_edge == 1)
    relays = is_middle & (on_up + on_down == 1)

    loads = [
        pltpu.make_async_copy(captions_hbm, captions, load_sem.at[0]),
        pltpu.make_async_copy(images_hbm, images, load_sem.at[1]),
        pltpu.make_async_copy(labels_hbm, labs.at[y], load_sem.at[2]),
    ]
    for load in loads:
        load.start()

    barrier = pltpu.get_barrier_semaphore()

    def greet(device):
        pl.semaphore_signal(barrier, inc=1, device_id=device, device_id_type=MESH)

    for device in [up_dev, down_dev, other_dev] + [chip(y + d) for d in (1, 2, 3)]:
        greet(device)

    @pl.when(relayed)
    def _():
        greet(via_dev)
        greet(from_dev)

    @pl.when(relays)
    def _():
        greet(source_dev)
        greet(target_dev)

    loads[0].wait()
    text_float, _ = unit_rows(captions[...])
    texts[0:rows, :] = text_float.astype(BF16)
    loads[1].wait()
    image_float, _ = unit_rows(images[...])
    imgs[y] = image_float.astype(BF16)
    loads[2].wait()

    relay_peers = 2 * ((y * (3 - y)) // 2) * (up_edge + down_edge + on_up + on_down)
    pl.semaphore_wait(barrier, 6 + relay_peers)

    def own_copy(c, direction):
        part = imgs.at[y, pl.ds(c * ag_rows, ag_rows)]
        return remote(
            part, part, ag_own_send.at[direction, c], ag_recv.at[y, c], chip(y + 1 - 2 * direction)
        )

    def fwd_copy(s, c):
        part = imgs.at[s, pl.ds(c * ag_rows, ag_rows)]
        target = jnp.where(s < y, y + 1, y - 1)
        return remote(part, part, ag_fwd_send.at[s, c], ag_recv.at[s, c], chip(target))

    def slot(i):
        return texts.at[pl.ds(i * rows, rows)]

    def relay_source(kind, source, c):
        where = pl.ds(c * relay_rows, relay_rows)
        return remote(
            source.at[where],
            relay_in.at[kind, where],
            relay_src_send.at[kind, c],
            relay_recv.at[kind, c],
            via_dev,
        )

    def relay_on(kind, target, start, sem, c):
        where = pl.ds(c * relay_rows, relay_rows)
        return remote(
            relay_in.at[kind, where],
            target.at[pl.ds(start + c * relay_rows, relay_rows)],
            relay_fwd_send.at[kind, c],
            sem,
            target_dev,
        )

    def captions_on(c):
        return relay_on(0, texts, (2 * on_up + 4 * on_down) * rows, next_recv.at[on_down], c)

    def sums_on(c):
        return relay_on(1, back_in.at[on_down], 0, back_recv.at[on_down], c)

    next_up = remote(slot(0), slot(2), next_send.at[0], next_recv.at[0], up_dev)
    next_down = remote(slot(0), slot(4), next_send.at[1], next_recv.at[1], down_dev)
    core_copies = [
        remote(slot(2 * i), slot(2 * i + 1), core_send.at[i], core_recv.at[i], other_dev) for i in range(3)
    ]
    lab_copies = [
        remote(labs.at[y], labs.at[y], lab_send.at[d - 1], lab_recv.at[y], chip(y + d)) for d in (1, 2, 3)
    ]

    @pl.when(relayed)
    def _():
        for c in range(RELAY_CHUNKS):
            relay_source(0, slot(0), c).start()

    for c in range(AG_CHUNKS):

        @pl.when(y < CHIPS - 1)
        def _():
            own_copy(c, 0).start()

        @pl.when(y > 0)
        def _():
            own_copy(c, 1).start()

    core_copies[0].start()

    @pl.when(jnp.logical_not(relayed_up))
    def _():
        next_up.start()

    @pl.when(jnp.logical_not(relayed_down))
    def _():
        next_down.start()

    for copy in lab_copies:
        copy.start()

    parts[...] = jnp.zeros_like(parts)
    sums[...] = jnp.zeros_like(sums)
    loss_part[...] = jnp.zeros_like(loss_part)

    near = jnp.where(y == 0, 1, jnp.where(y == 1, 0, jnp.where(y == 2, 3, 2)))
    next_near = jnp.where(y == 0, 2, jnp.where(y == 1, 2, 1))
    far = jnp.where(y < 2, 3, 0)

    def take(s, c):
        copy = fwd_copy(s, c)
        copy.wait_recv()

        @pl.when(is_middle)
        def _():
            copy.start()

    def take_labels(s):
        remote(labs.at[s], labs.at[s], lab_send.at[0], lab_recv.at[s], chip(y + 1)).wait_recv()

    scale = scale_ref[0]
    bias = bias_ref[0]

    def compute(s, i):
        image = imgs[s]
        where = pl.ds(pl.multiple_of(2 * i * rows, 2 * rows), 2 * rows)
        text = texts[where, :]
        raw = depth_part(text, image, 0, 512) + depth_part(text, image, 512, text.shape[1])
        label = labs[s]
        mine = label - group * rows
        theirs = label - other * rows
        theirs = jnp.where((theirs >= 0) & (theirs < rows), theirs + rows, -1)
        place = jnp.where((mine >= 0) & (mine < rows), mine, theirs)
        place = jnp.where(i == 0, place, -1)
        positive = lax.broadcasted_iota(jnp.int32, raw.shape, 0) == place
        loss, weights = pair_weights(raw, positive, scale, bias)
        sums[where, :] += jnp.dot(weights, image, preferred_element_type=F32)
        parts[s] += lax.dot_general(weights, text, (((0,), (0,)), ((), ())), preferred_element_type=F32)
        loss_part[s] += loss

    def end_copy(t, c):
        where = pl.ds(c * rs_rows, rs_rows)
        return remote(
            parts_out.at[t, where],
            end_in.at[t, where],
            end_send.at[t, c],
            end_recv.at[t, c],
            chip(1 + y // (CHIPS - 1)),
        )

    def mid_copy(t, c):
        where = pl.ds(c * rs_rows, rs_rows)
        sender = (y + 1) % 2
        return remote(
            parts_out.at[t, where], mid_in.at[sender, where], mid_send.at[t, c], mid_recv.at[sender, c], chip(t)
        )

    def sum_copy(i):
        return remote(sums_out.at[i], sums_in.at[i], sum_send.at[i], sum_recv.at[i], other_dev)

    def step(u, carry):
        s = jnp.where(u < 9, jnp.where((u == 0) | (u == 4) | (u == 5), y, jnp.where(u < 4, near, next_near)), far)
        i = jnp.where(u < 4, jnp.where(u == 0, 0, u - 1), jnp.where(u < 6, u - 3, u % 3))
        i = jnp.where(u > 8, (u + 1) % 3, i)

        @pl.when(u == 0)
        def _():
            core_copies[0].wait_recv()

        @pl.when((u == 1) & is_middle)
        def _():
            for c in range(AG_CHUNKS):
                take(near, c)
                take(next_near, c)

        @pl.when((u == 1) & relays)
        def _():
            for c in range(RELAY_CHUNKS):
                relay_source(0, slot(0), c).wait_recv()
                captions_on(c).start()

        @pl.when((u == 1) & is_end)
        def _():
            for c in range(AG_CHUNKS):
                take(near, c)

        @pl.when(u == 1)
        def _():
            for other_slot in (near, next_near, far):
                take_labels(other_slot)

        @pl.when((u == 2) & is_middle)
        def _():
            take(far, 0)

        @pl.when(u == 2)
        def _():
            next_up.wait_recv()
            core_copies[1].start()
            next_down.wait_recv()
            core_copies[2].start()

        @pl.when((u == 2) & is_middle)
        def _():
            for c in range(1, AG_CHUNKS):
                take(far, c)

        @pl.when(u == 2)
        def _():
            core_copies[1].wait_recv()
            core_copies[2].wait_recv()

        @pl.when((u == 6) & is_end)
        def _():
            for c in range(AG_CHUNKS):
                take(next_near, c)

        @pl.when((u == 9) & is_end)
        def _():
            for c in range(AG_CHUNKS):
                take(far, c)

        compute(s, i)

        @pl.when(u > 8)
        def _():
            start = pl.multiple_of((2 * i + 1) * rows, rows)
            sums_out[i] = sums[pl.ds(start, rows), :].astype(BF16)
            sum_copy(i).start()

        @pl.when(((u == 3) | (u == 8) | (u == 11)) & is_end)
        def _():
            parts_out[s] = parts[s].astype(BF16)
            for c in range(RS_CHUNKS):
                end_copy(s, c).start()

        return carry

    lax.fori_loop(0, 3 * CHIPS, step, 0)

    back_down = remote(back_out.at[0], back_in.at[1], back_send.at[0], back_recv.at[1], down_dev)
    back_up = remote(back_out.at[1], back_in.at[0], back_send.at[1], back_recv.at[0], up_dev)
    for i in (1, 2):
        sum_copy(i).wait_recv()
        total = sums[2 * i * rows : (2 * i + 1) * rows, :] + sums_in[i].astype(F32)
        back_out[i - 1] = total.astype(BF16)

        @pl.when(jnp.logical_not(relayed_down if i == 1 else relayed_up))
        def _():
            (back_down if i == 1 else back_up).start()

    @pl.when(relayed)
    def _():
        for c in range(RELAY_CHUNKS):
            relay_source(1, back_out.at[up_edge], c).start()

    loss_copies = [
        remote(
            loss_part.at[(y + d) % CHIPS], loss_in.at[y], loss_send.at[d - 1], loss_recv.at[y], chip(y + d)
        )
        for d in (1, 2, 3)
    ]
    for copy in loss_copies:
        copy.start()

    def pass_on(t, c):
        where = pl.ds(pl.multiple_of(c * rs_rows, rs_rows), rs_rows)
        end_copy(t, c).wait_recv()
        total = parts[t, where, :] + end_in[t, where, :].astype(F32)
        parts_out[t, where, :] = total.astype(BF16)
        mid_copy(t, c).start()

    @pl.when(is_middle)
    def _():
        parts_out[near] = parts[near].astype(BF16)
        for c in range(RS_CHUNKS):
            mid_copy(near, c).start()

        def inner(c, carry):
            pass_on(next_near, c)
            return carry

        lax.fori_loop(0, RS_CHUNKS, inner, 0)

        def outer(c, carry):
            pass_on(far, c)

            @pl.when(relays & (c % (RS_CHUNKS // RELAY_CHUNKS) == RS_CHUNKS // RELAY_CHUNKS - 1))
            def _():
                part = c // (RS_CHUNKS // RELAY_CHUNKS)
                relay_source(1, back_out.at[up_edge], part).wait_recv()
                sums_on(part).start()

            return carry

        lax.fori_loop(0, RS_CHUNKS, outer, 0)

    sum_copy(0).wait_recv()
    text_sums = sums[0:rows, :] + sums_in[0].astype(F32)
    back_down.wait_recv()
    text_sums = text_sums + back_in[1].astype(F32)
    back_up.wait_recv()
    text_sums = text_sums + back_in[0].astype(F32)
    text_float, text_length = unit_rows(captions[...])
    text_out[...] = through_norm(text_sums, text_float, text_length)

    loss_total = loss_part[y]
    for d in (1, 2, 3):
        s = (y + d) % CHIPS
        remote(loss_part.at[s], loss_in.at[s], loss_send.at[0], loss_recv.at[s], chip(y + 1)).wait_recv()
        loss_total = loss_total + loss_in[s]
    loss_out[...] = loss_total

    for sender in (0, 1):

        @pl.when(y != sender + 1)
        def _():
            for c in range(RS_CHUNKS):
                where = pl.ds(c * rs_rows, rs_rows)
                part = mid_in.at[sender, where]
                remote(part, part, mid_send.at[0, c], mid_recv.at[sender, c], chip(y + 1)).wait_recv()
            parts[y] += mid_in[sender].astype(F32)

    @pl.when(is_middle)
    def _():
        for c in range(RS_CHUNKS):
            end_copy(y, c).wait_recv()
        parts[y] += end_in[y].astype(F32)

    image_float, image_length = unit_rows(images[...])
    image_out[...] = through_norm(parts[y], image_float, image_length)

    for c in range(AG_CHUNKS):

        @pl.when(y < CHIPS - 1)
        def _():
            own_copy(c, 0).wait_send()

        @pl.when(y > 0)
        def _():
            own_copy(c, 1).wait_send()

    def sent(d, carry):
        s = (y + d) % CHIPS

        @pl.when(is_middle)
        def _():
            for c in range(AG_CHUNKS):
                fwd_copy(s, c).wait_send()
            for c in range(RS_CHUNKS):
                mid_copy(s, c).wait_send()

        @pl.when(is_end)
        def _():
            for c in range(RS_CHUNKS):
                end_copy(s, c).wait_send()

        return carry

    lax.fori_loop(1, CHIPS, sent, 0)

    @pl.when(jnp.logical_not(relayed_up))
    def _():
        next_up.wait_send()
        back_up.wait_send()

    @pl.when(jnp.logical_not(relayed_down))
    def _():
        next_down.wait_send()
        back_down.wait_send()

    @pl.when(relayed)
    def _():
        for c in range(RELAY_CHUNKS):
            relay_source(0, slot(0), c).wait_send()
            relay_source(1, back_out.at[up_edge], c).wait_send()

    @pl.when(relays)
    def _():
        for c in range(RELAY_CHUNKS):
            captions_on(c).wait_send()
            sums_on(c).wait_send()

    for copy in core_copies + lab_copies + loss_copies + [sum_copy(i) for i in range(3)]:
        copy.wait_send()


def per_device(blocks, images, captions, labels, logit_scale, logit_bias):
    rows, width = images.shape
    vmem = pl.BlockSpec(memory_space=pltpu.VMEM)
    smem = pl.BlockSpec(memory_space=pltpu.SMEM)
    hbm = pl.BlockSpec(memory_space=pl.ANY)
    dma = pltpu.SemaphoreType.DMA
    loss, image_grad, text_grad = pl.pallas_call(
        functools.partial(kernel, blocks),
        out_shape=[
            jax.ShapeDtypeStruct((1, rows), F32),
            jax.ShapeDtypeStruct((rows, width), F32),
            jax.ShapeDtypeStruct((rows, width), F32),
        ],
        in_specs=[hbm, hbm, hbm, smem, smem],
        out_specs=[vmem, vmem, vmem],
        scratch_shapes=[
            pltpu.VMEM((rows, width), BF16),
            pltpu.VMEM((rows, width), BF16),
            pltpu.VMEM((CHIPS, rows, width), BF16),
            pltpu.VMEM((6 * rows, width), BF16),
            pltpu.VMEM((CHIPS, 1, rows), jnp.int32),
            pltpu.VMEM((CHIPS, 1, rows), F32),
            pltpu.VMEM((CHIPS, 1, rows), F32),
            pltpu.VMEM((CHIPS, rows, width), F32),
            pltpu.VMEM((CHIPS, rows, width), BF16),
            pltpu.VMEM((CHIPS, rows, width), BF16),
            pltpu.VMEM((2, rows, width), BF16),
            pltpu.VMEM((6 * rows, width), F32),
            pltpu.VMEM((3, rows, width), BF16),
            pltpu.VMEM((3, rows, width), BF16),
            pltpu.VMEM((2, rows, width), BF16),
            pltpu.VMEM((2, rows, width), BF16),
            pltpu.VMEM((2, rows, width), BF16),
            dma((3,)),
            dma((2, AG_CHUNKS)),
            dma((CHIPS, AG_CHUNKS)),
            dma((CHIPS, AG_CHUNKS)),
            dma((3,)),
            dma((CHIPS,)),
            dma((3,)),
            dma((CHIPS,)),
            dma((3,)),
            dma((3,)),
            dma((2,)),
            dma((2,)),
            dma((CHIPS, RS_CHUNKS)),
            dma((CHIPS, RS_CHUNKS)),
            dma((CHIPS, RS_CHUNKS)),
            dma((2, RS_CHUNKS)),
            dma((3,)),
            dma((3,)),
            dma((2,)),
            dma((2,)),
            dma((2, RELAY_CHUNKS)),
            dma((2, RELAY_CHUNKS)),
            dma((2, RELAY_CHUNKS)),
        ],
        compiler_params=pltpu.CompilerParams(
            collective_id=0, has_side_effects=True, vmem_limit_bytes=48 * 1024 * 1024
        ),
    )(images, captions, labels.reshape(1, rows), logit_scale, logit_bias)
    return (loss.reshape(rows), image_grad, text_grad)


def solution(mesh):
    body = functools.partial(per_device, mesh.shape["blk"])
    in_specs = (P(("blk", "group"), None), P(("blk", "group"), None), P(("blk", "group")), P(), P())
    out_specs = (P(("blk", "group")), P(("blk", "group"), None), P(("blk", "group"), None))
    return jax.shard_map(body, mesh=mesh, in_specs=in_specs, out_specs=out_specs, check_vma=False)
```

```python
import functools

import jax
import jax.numpy as jnp
from jax import lax
from jax.experimental import pallas as pl
from jax.experimental.pallas import tpu as pltpu
from jax.sharding import PartitionSpec as P

EPSILON = 1e-06
CHIPS = 4
LINE = 8
AG_CHUNKS = 2
RS_CHUNKS = 8
RELAY_CHUNKS = 2
MESH = pl.DeviceIdType.MESH
F32 = jnp.float32
BF16 = jnp.bfloat16


def unit_rows(values):
    wide = values.astype(F32)
    length = jnp.sqrt(jnp.sum(wide * wide, axis=-1, keepdims=True) + EPSILON)
    return (wide / length, length)


def through_norm(sums, unit_float, length):
    return (sums - unit_float * jnp.sum(unit_float * sums, axis=-1, keepdims=True)) / length


def depth_part(a, b, start, stop):
    return lax.dot_general(
        a[:, start:stop], b[:, start:stop], (((1,), (1,)), ((), ())), preferred_element_type=F32
    )


def summed_log(decay):
    pieces = [decay[i : i + 8, :] for i in range(0, decay.shape[0], 8)]
    while len(pieces) > 1:
        pieces = [a + b + a * b for a, b in zip(pieces[::2], pieces[1::2])]
    return jnp.sum(jnp.log1p(pieces[0]), axis=0, keepdims=True)


def pair_weights(raw, positive, scale, bias):
    logits = scale * raw + bias
    turned = jnp.where(positive, -logits, logits)
    decay = jnp.exp(-jnp.abs(turned))
    loss = jnp.sum(jnp.maximum(turned, 0.0), axis=0, keepdims=True) + summed_log(decay)
    share = jnp.where(turned >= 0, 1.0, decay) / (1.0 + decay)
    weights = jnp.where(positive, -scale, scale) * share
    return (loss, weights.astype(BF16))


def kernel(
    blocks,
    images_hbm,
    captions_hbm,
    labels_hbm,
    scale_ref,
    bias_ref,
    loss_out,
    image_out,
    text_out,
    images,
    captions,
    imgs,
    texts,
    labs,
    loss_part,
    loss_in,
    parts,
    parts_out,
    end_in,
    mid_in,
    sums,
    sums_out,
    sums_in,
    back_out,
    back_in,
    relay_in,
    load_sem,
    ag_own_send,
    ag_fwd_send,
    ag_recv,
    lab_send,
    lab_recv,
    loss_send,
    loss_recv,
    core_send,
    core_recv,
    next_send,
    next_recv,
    end_send,
    end_recv,
    mid_send,
    mid_recv,
    sum_send,
    sum_recv,
    back_send,
    back_recv,
    relay_src_send,
    relay_recv,
    relay_fwd_send,
    ready,
):
    rows = images.shape[0]
    ag_rows = rows // AG_CHUNKS
    rs_rows = rows // RS_CHUNKS
    relay_rows = rows // RELAY_CHUNKS
    blk = lax.axis_index("blk")
    group = lax.axis_index("group")
    y = group // 2
    core = group % 2
    other = group + 1 - 2 * core
    half = blocks // 2
    mirrored = 2 * (CHIPS - 1 - y) + core
    up_edge = (blk % half) // (half - 1)
    down_edge = (half - 1 - blk % half) // (half - 1)
    up_dev = {"blk": (blk + 1) % blocks, "group": group + up_edge * (mirrored - group)}
    down_dev = {"blk": (blk + blocks - 1) % blocks, "group": group + down_edge * (mirrored - group)}
    on_up = down_edge
    on_down = jnp.where(blk % half == half - LINE, 1, 0)
    shift = half - LINE
    via_dev = {"blk": blk + shift * down_edge - (half - 1) * up_edge, "group": group}
    from_dev = {"blk": (blk + shift + 1) % blocks, "group": mirrored}
    source_dev = {"blk": blk + (half - 1) * on_up - shift * on_down, "group": group}
    target_dev = {"blk": (blk + blocks + half * on_up - (shift + 1) * on_down) % blocks, "group": mirrored}
    other_dev = {"blk": blk, "group": other}

    def chip(position):
        return {"blk": blk, "group": (position + CHIPS) % CHIPS * 2 + core}

    def remote(src, dst, send, recv, device):
        return pltpu.make_async_remote_copy(
            src_ref=src, dst_ref=dst, send_sem=send, recv_sem=recv, device_id=device, device_id_type=MESH
        )

    is_end = (y == 0) | (y == CHIPS - 1)
    is_middle = (y == 1) | (y == 2)
    relayed_up = is_middle & (up_edge == 1)
    relayed_down = is_middle & (down_edge == 1)
    relayed = is_middle & (up_edge + down_edge == 1)
    relays = is_middle & (on_up + on_down == 1)
    is_first = blk % LINE == 0
    is_last = blk % LINE == LINE - 1
    not_first = jnp.logical_not(is_first)
    not_last = jnp.logical_not(is_last)

    loads = [
        pltpu.make_async_copy(captions_hbm, captions, load_sem.at[0]),
        pltpu.make_async_copy(images_hbm, images, load_sem.at[1]),
        pltpu.make_async_copy(labels_hbm, labs.at[y], load_sem.at[2]),
    ]
    for load in loads:
        load.start()

    barrier = pltpu.get_barrier_semaphore()

    def greet(device):
        pl.semaphore_signal(barrier, inc=1, device_id=device, device_id_type=MESH)

    for device in [other_dev] + [chip(y + d) for d in (1, 2, 3)]:
        greet(device)

    @pl.when(not_last)
    def _():
        greet(up_dev)

    @pl.when(is_first)
    def _():
        greet(down_dev)

    @pl.when(relayed & is_first)
    def _():
        greet(via_dev)

    @pl.when(relays)
    def _():
        greet(source_dev)
        greet(target_dev)

    loads[0].wait()
    text_float, _ = unit_rows(captions[...])
    texts[0:rows, :] = text_float.astype(BF16)
    loads[1].wait()
    image_float, _ = unit_rows(images[...])
    imgs[y] = image_float.astype(BF16)
    loads[2].wait()

    inner = (y * (3 - y)) // 2
    peers = 4 + jnp.where(is_first, 0, 1) + jnp.where(is_last, 1, 0)
    peers = peers + inner * (2 * (up_edge + down_edge) + on_down)
    pl.semaphore_wait(barrier, peers)

    def answer(index, device):
        pl.semaphore_signal(ready.at[index], inc=1, device_id=device, device_id_type=MESH)

    @pl.when(not_first)
    def _():
        answer(0, down_dev)

    @pl.when(is_last)
    def _():
        answer(1, up_dev)

    @pl.when(relayed & is_last)
    def _():
        answer(2, from_dev)

    def own_copy(c, direction):
        part = imgs.at[y, pl.ds(c * ag_rows, ag_rows)]
        return remote(
            part, part, ag_own_send.at[direction, c], ag_recv.at[y, c], chip(y + 1 - 2 * direction)
        )

    def fwd_copy(s, c):
        part = imgs.at[s, pl.ds(c * ag_rows, ag_rows)]
        target = jnp.where(s < y, y + 1, y - 1)
        return remote(part, part, ag_fwd_send.at[s, c], ag_recv.at[s, c], chip(target))

    def slot(i):
        return texts.at[pl.ds(i * rows, rows)]

    def relay_source(kind, source, c):
        where = pl.ds(c * relay_rows, relay_rows)
        return remote(
            source.at[where],
            relay_in.at[kind, where],
            relay_src_send.at[kind, c],
            relay_recv.at[kind, c],
            via_dev,
        )

    def relay_on(kind, target, start, sem, c):
        where = pl.ds(c * relay_rows, relay_rows)
        return remote(
            relay_in.at[kind, where],
            target.at[pl.ds(start + c * relay_rows, relay_rows)],
            relay_fwd_send.at[kind, c],
            sem,
            target_dev,
        )

    def captions_on(c):
        return relay_on(0, texts, (2 * on_up + 4 * on_down) * rows, next_recv.at[on_down], c)

    def sums_on(c):
        return relay_on(1, back_in.at[on_down], 0, back_recv.at[on_down], c)

    next_up = remote(slot(0), slot(2), next_send.at[0], next_recv.at[0], up_dev)
    next_down = remote(slot(0), slot(4), next_send.at[1], next_recv.at[1], down_dev)
    core_copies = [
        remote(slot(2 * i), slot(2 * i + 1), core_send.at[i], core_recv.at[i], other_dev) for i in range(3)
    ]
    lab_copies = [
        remote(labs.at[y], labs.at[y], lab_send.at[d - 1], lab_recv.at[y], chip(y + d)) for d in (1, 2, 3)
    ]

    @pl.when(relayed)
    def _():
        for c in range(RELAY_CHUNKS):
            relay_source(0, slot(0), c).start()

    for c in range(AG_CHUNKS):

        @pl.when(y < CHIPS - 1)
        def _():
            own_copy(c, 0).start()

        @pl.when(y > 0)
        def _():
            own_copy(c, 1).start()

    core_copies[0].start()

    @pl.when(not_first)
    def _():
        next_down.start()

    for copy in lab_copies:
        copy.start()

    @pl.when(not_last)
    def _():
        pl.semaphore_wait(ready.at[0], 1)

    @pl.when(jnp.logical_not(relayed_up))
    def _():
        next_up.start()

    parts[...] = jnp.zeros_like(parts)
    sums[...] = jnp.zeros_like(sums)
    loss_part[...] = jnp.zeros_like(loss_part)

    near = jnp.where(y == 0, 1, jnp.where(y == 1, 0, jnp.where(y == 2, 3, 2)))
    next_near = jnp.where(y == 0, 2, jnp.where(y == 1, 2, 1))
    far = jnp.where(y < 2, 3, 0)

    def take(s, c):
        copy = fwd_copy(s, c)
        copy.wait_recv()

        @pl.when(is_middle)
        def _():
            copy.start()

    def take_labels(s):
        remote(labs.at[s], labs.at[s], lab_send.at[0], lab_recv.at[s], chip(y + 1)).wait_recv()

    scale = scale_ref[0]
    bias = bias_ref[0]

    def compute(s, i):
        image = imgs[s]
        where = pl.ds(pl.multiple_of(2 * i * rows, 2 * rows), 2 * rows)
        text = texts[where, :]
        raw = depth_part(text, image, 0, 512) + depth_part(text, image, 512, text.shape[1])
        label = labs[s]
        mine = label - group * rows
        theirs = label - other * rows
        theirs = jnp.where((theirs >= 0) & (theirs < rows), theirs + rows, -1)
        place = jnp.where((mine >= 0) & (mine < rows), mine, theirs)
        place = jnp.where(i == 0, place, -1)
        positive = lax.broadcasted_iota(jnp.int32, raw.shape, 0) == place
        loss, weights = pair_weights(raw, positive, scale, bias)
        sums[where, :] += jnp.dot(weights, image, preferred_element_type=F32)
        parts[s] += lax.dot_general(weights, text, (((0,), (0,)), ((), ())), preferred_element_type=F32)
        loss_part[s] += loss

    def end_copy(t, c):
        where = pl.ds(c * rs_rows, rs_rows)
        return remote(
            parts_out.at[t, where],
            end_in.at[t, where],
            end_send.at[t, c],
            end_recv.at[t, c],
            chip(1 + y // (CHIPS - 1)),
        )

    def mid_copy(t, c):
        where = pl.ds(c * rs_rows, rs_rows)
        sender = (y + 1) % 2
        return remote(
            parts_out.at[t, where], mid_in.at[sender, where], mid_send.at[t, c], mid_recv.at[sender, c], chip(t)
        )

    def sum_copy(i):
        return remote(sums_out.at[i], sums_in.at[i], sum_send.at[i], sum_recv.at[i], other_dev)

    def finish(i):
        sum_copy(i).wait_recv()
        total = sums[2 * i * rows : (2 * i + 1) * rows, :] + sums_in[i].astype(F32)
        back_out[i - 1] = total.astype(BF16)
        direct = back_down if i == 1 else back_up
        edge = relayed_down if i == 1 else relayed_up

        @pl.when(jnp.logical_not(edge))
        def _():
            direct.start()

        @pl.when(edge)
        def _():
            for c in range(RELAY_CHUNKS):
                relay_source(1, back_out.at[i - 1], c).start()

    back_down = remote(back_out.at[0], back_in.at[1], back_send.at[0], back_recv.at[1], down_dev)
    back_up = remote(back_out.at[1], back_in.at[0], back_send.at[1], back_recv.at[0], up_dev)

    def chosen(u, usual, first):
        value = usual[0]
        for k in range(len(usual)):
            value = jnp.where(u == k, jnp.where(is_first, first[k], usual[k]), value)
        return value

    def pass_captions(c):
        relay_source(0, slot(0), c).wait_recv()
        captions_on(c).start()

    usual_order = [y, near, near, near, y, y, next_near, next_near, next_near, far, far, far]
    first_order = [y, near, near, y, next_near, next_near, far, far, far, next_near, near, y]

    def step(u, carry):
        s = chosen(u, usual_order, first_order)
        i = chosen(u, [0, 0, 1, 2, 1, 2, 0, 1, 2, 2, 1, 0], [0, 0, 2, 2, 0, 2, 2, 0, 1, 1, 1, 1])

        @pl.when(u == 0)
        def _():
            core_copies[0].wait_recv()

        @pl.when((u == 1) & is_middle)
        def _():
            for c in range(AG_CHUNKS):
                take(near, c)
                take(next_near, c)

        @pl.when((u == 1) & is_end)
        def _():
            for c in range(AG_CHUNKS):
                take(near, c)

        @pl.when(u == 1)
        def _():
            for other_slot in (near, next_near, far):
                take_labels(other_slot)

        @pl.when((u == 2) & is_first)
        def _():
            next_down.wait_recv()
            core_copies[2].start()

        @pl.when((u == 2) & not_first)
        def _():
            next_up.wait_recv()
            core_copies[1].start()

        @pl.when((u == 2) & is_middle)
        def _():
            take(far, 0)

        @pl.when((u == 2) & is_first)
        def _():
            core_copies[2].wait_recv()

        @pl.when((u == 2) & not_first)
        def _():
            next_down.wait_recv()
            core_copies[2].start()
            core_copies[1].wait_recv()

        @pl.when((u == 3) & not_first)
        def _():
            core_copies[2].wait_recv()

        @pl.when((u == 4) & is_middle)
        def _():
            for c in range(1, AG_CHUNKS):
                take(far, c)

        @pl.when((u == 4) & is_first)
        def _():
            pl.semaphore_wait(ready.at[1], 1)

        @pl.when((u == 4) & is_first & jnp.logical_not(relayed_down))
        def _():
            next_down.start()

        @pl.when((u == 4) & relays & (on_down == 1))
        def _():
            pl.semaphore_wait(ready.at[2], 1)
            for c in range(RELAY_CHUNKS):
                pass_captions(c)

        @pl.when((u == jnp.where(is_first, 4, 6)) & is_end)
        def _():
            for c in range(AG_CHUNKS):
                take(next_near, c)

        @pl.when((u == jnp.where(is_first, 6, 9)) & is_end)
        def _():
            for c in range(AG_CHUNKS):
                take(far, c)

        @pl.when((u == 8) & is_first)
        def _():
            finish(2)

        @pl.when((u == 8) & relays & (on_up == 1))
        def _():
            for c in range(RELAY_CHUNKS):
                pass_captions(c)

        @pl.when((u == 8) & is_first)
        def _():
            next_up.wait_recv()
            core_copies[1].start()
            core_copies[1].wait_recv()

        compute(s, i)

        @pl.when(jnp.where(is_first, (u == 6) | (u == 7) | (u == 11), u > 8))
        def _():
            start = pl.multiple_of((2 * i + 1) * rows, rows)
            sums_out[i] = sums[pl.ds(start, rows), :].astype(BF16)
            sum_copy(i).start()

        @pl.when(jnp.where(is_first, (u > 7) & (u < 11), (u == 3) | (u == 8) | (u == 11)) & is_end)
        def _():
            parts_out[s] = parts[s].astype(BF16)
            for c in range(RS_CHUNKS):
                end_copy(s, c).start()

        return carry

    lax.fori_loop(0, 3 * CHIPS, step, 0)

    @pl.when(not_first)
    def _():
        finish(2)

    finish(1)

    loss_copies = [
        remote(
            loss_part.at[(y + d) % CHIPS], loss_in.at[y], loss_send.at[d - 1], loss_recv.at[y], chip(y + d)
        )
        for d in (1, 2, 3)
    ]
    for copy in loss_copies:
        copy.start()

    def pass_sums(c):
        relay_source(1, back_out.at[up_edge], c).wait_recv()
        sums_on(c).start()

    def pass_on(t, c):
        where = pl.ds(pl.multiple_of(c * rs_rows, rs_rows), rs_rows)
        end_copy(t, c).wait_recv()
        total = parts[t, where, :] + end_in[t, where, :].astype(F32)
        parts_out[t, where, :] = total.astype(BF16)
        mid_copy(t, c).start()

    @pl.when(is_middle)
    def _():
        parts_out[near] = parts[near].astype(BF16)
        for c in range(RS_CHUNKS):
            mid_copy(near, c).start()

        before = jnp.where(is_first, far, next_near)
        after = jnp.where(is_first, next_near, far)

        def pass_all(k, carry):
            pass_on(jnp.where(k < RS_CHUNKS, before, after), k % RS_CHUNKS)

            return carry

        lax.fori_loop(0, 2 * RS_CHUNKS, pass_all, 0)

    @pl.when(relays)
    def _():
        for c in range(RELAY_CHUNKS):
            pass_sums(c)

    sum_copy(0).wait_recv()
    text_sums = sums[0:rows, :] + sums_in[0].astype(F32)
    back_down.wait_recv()
    text_sums = text_sums + back_in[1].astype(F32)
    back_up.wait_recv()
    text_sums = text_sums + back_in[0].astype(F32)
    text_float, text_length = unit_rows(captions[...])
    text_out[...] = through_norm(text_sums, text_float, text_length)

    loss_total = loss_part[y]
    for d in (1, 2, 3):
        s = (y + d) % CHIPS
        remote(loss_part.at[s], loss_in.at[s], loss_send.at[0], loss_recv.at[s], chip(y + 1)).wait_recv()
        loss_total = loss_total + loss_in[s]
    loss_out[...] = loss_total

    for sender in (0, 1):

        @pl.when(y != sender + 1)
        def _():
            for c in range(RS_CHUNKS):
                where = pl.ds(c * rs_rows, rs_rows)
                part = mid_in.at[sender, where]
                remote(part, part, mid_send.at[0, c], mid_recv.at[sender, c], chip(y + 1)).wait_recv()
            parts[y] += mid_in[sender].astype(F32)

    @pl.when(is_middle)
    def _():
        for c in range(RS_CHUNKS):
            end_copy(y, c).wait_recv()
        parts[y] += end_in[y].astype(F32)

    image_float, image_length = unit_rows(images[...])
    image_out[...] = through_norm(parts[y], image_float, image_length)

    for c in range(AG_CHUNKS):

        @pl.when(y < CHIPS - 1)
        def _():
            own_copy(c, 0).wait_send()

        @pl.when(y > 0)
        def _():
            own_copy(c, 1).wait_send()

    def sent(d, carry):
        s = (y + d) % CHIPS

        @pl.when(is_middle)
        def _():
            for c in range(AG_CHUNKS):
                fwd_copy(s, c).wait_send()
            for c in range(RS_CHUNKS):
                mid_copy(s, c).wait_send()

        @pl.when(is_end)
        def _():
            for c in range(RS_CHUNKS):
                end_copy(s, c).wait_send()

        return carry

    lax.fori_loop(1, CHIPS, sent, 0)

    @pl.when(jnp.logical_not(relayed_up))
    def _():
        next_up.wait_send()
        back_up.wait_send()

    @pl.when(jnp.logical_not(relayed_down))
    def _():
        next_down.wait_send()
        back_down.wait_send()

    @pl.when(relayed)
    def _():
        for c in range(RELAY_CHUNKS):
            relay_source(0, slot(0), c).wait_send()
            relay_source(1, back_out.at[up_edge], c).wait_send()

    @pl.when(relays)
    def _():
        for c in range(RELAY_CHUNKS):
            captions_on(c).wait_send()
            sums_on(c).wait_send()

    for copy in core_copies + lab_copies + loss_copies + [sum_copy(i) for i in range(3)]:
        copy.wait_send()


def per_device(blocks, images, captions, labels, logit_scale, logit_bias):
    rows, width = images.shape
    vmem = pl.BlockSpec(memory_space=pltpu.VMEM)
    smem = pl.BlockSpec(memory_space=pltpu.SMEM)
    hbm = pl.BlockSpec(memory_space=pl.ANY)
    dma = pltpu.SemaphoreType.DMA
    loss, image_grad, text_grad = pl.pallas_call(
        functools.partial(kernel, blocks),
        out_shape=[
            jax.ShapeDtypeStruct((1, rows), F32),
            jax.ShapeDtypeStruct((rows, width), F32),
            jax.ShapeDtypeStruct((rows, width), F32),
        ],
        in_specs=[hbm, hbm, hbm, smem, smem],
        out_specs=[vmem, vmem, vmem],
        scratch_shapes=[
            pltpu.VMEM((rows, width), BF16),
            pltpu.VMEM((rows, width), BF16),
            pltpu.VMEM((CHIPS, rows, width), BF16),
            pltpu.VMEM((6 * rows, width), BF16),
            pltpu.VMEM((CHIPS, 1, rows), jnp.int32),
            pltpu.VMEM((CHIPS, 1, rows), F32),
            pltpu.VMEM((CHIPS, 1, rows), F32),
            pltpu.VMEM((CHIPS, rows, width), F32),
            pltpu.VMEM((CHIPS, rows, width), BF16),
            pltpu.VMEM((CHIPS, rows, width), BF16),
            pltpu.VMEM((2, rows, width), BF16),
            pltpu.VMEM((6 * rows, width), F32),
            pltpu.VMEM((3, rows, width), BF16),
            pltpu.VMEM((3, rows, width), BF16),
            pltpu.VMEM((2, rows, width), BF16),
            pltpu.VMEM((2, rows, width), BF16),
            pltpu.VMEM((2, rows, width), BF16),
            dma((3,)),
            dma((2, AG_CHUNKS)),
            dma((CHIPS, AG_CHUNKS)),
            dma((CHIPS, AG_CHUNKS)),
            dma((3,)),
            dma((CHIPS,)),
            dma((3,)),
            dma((CHIPS,)),
            dma((3,)),
            dma((3,)),
            dma((2,)),
            dma((2,)),
            dma((CHIPS, RS_CHUNKS)),
            dma((CHIPS, RS_CHUNKS)),
            dma((CHIPS, RS_CHUNKS)),
            dma((2, RS_CHUNKS)),
            dma((3,)),
            dma((3,)),
            dma((2,)),
            dma((2,)),
            dma((2, RELAY_CHUNKS)),
            dma((2, RELAY_CHUNKS)),
            dma((2, RELAY_CHUNKS)),
            pltpu.SemaphoreType.REGULAR((3,)),
        ],
        compiler_params=pltpu.CompilerParams(
            collective_id=0, has_side_effects=True, vmem_limit_bytes=48 * 1024 * 1024
        ),
    )(images, captions, labels.reshape(1, rows), logit_scale, logit_bias)
    return (loss.reshape(rows), image_grad, text_grad)


def solution(mesh):
    body = functools.partial(per_device, mesh.shape["blk"])
    in_specs = (P(("blk", "group"), None), P(("blk", "group"), None), P(("blk", "group")), P(), P())
    out_specs = (P(("blk", "group")), P(("blk", "group"), None), P(("blk", "group"), None))
    return jax.shard_map(body, mesh=mesh, in_specs=in_specs, out_specs=out_specs, check_vma=False)
```

```python
import functools

import jax
import jax.numpy as jnp
from jax import lax
from jax.experimental import pallas as pl
from jax.experimental.pallas import tpu as pltpu
from jax.sharding import PartitionSpec as P

EPSILON = 1e-06
CHIPS = 4
LINE = 8
VIA = (24, 8)
AG_CHUNKS = 2
RS_CHUNKS = 8
RELAY_CHUNKS = 2
MESH = pl.DeviceIdType.MESH
F32 = jnp.float32
BF16 = jnp.bfloat16


def unit_rows(values):
    wide = values.astype(F32)
    length = jnp.sqrt(jnp.sum(wide * wide, axis=-1, keepdims=True) + EPSILON)
    return (wide / length, length)


def through_norm(sums, unit_float, length):
    return (sums - unit_float * jnp.sum(unit_float * sums, axis=-1, keepdims=True)) / length


def depth_part(a, b, start, stop):
    return lax.dot_general(
        a[:, start:stop], b[:, start:stop], (((1,), (1,)), ((), ())), preferred_element_type=F32
    )


def summed_log(decay):
    pieces = [decay[i : i + 8, :] for i in range(0, decay.shape[0], 8)]
    while len(pieces) > 1:
        pieces = [a + b + a * b for a, b in zip(pieces[::2], pieces[1::2])]
    return jnp.sum(jnp.log1p(pieces[0]), axis=0, keepdims=True)


def pair_weights(raw, positive, scale, bias):
    logits = scale * raw + bias
    turned = jnp.where(positive, -logits, logits)
    decay = jnp.exp(-jnp.abs(turned))
    loss = jnp.sum(jnp.maximum(turned, 0.0), axis=0, keepdims=True) + summed_log(decay)
    share = jnp.where(turned >= 0, 1.0, decay) / (1.0 + decay)
    weights = jnp.where(positive, -scale, scale) * share
    return (loss, weights.astype(BF16))


def kernel(
    blocks,
    images_hbm,
    captions_hbm,
    labels_hbm,
    scale_ref,
    bias_ref,
    loss_out,
    image_out,
    text_out,
    images,
    captions,
    imgs,
    texts,
    labs,
    loss_part,
    loss_in,
    parts,
    parts_out,
    end_in,
    mid_in,
    sums,
    sums_out,
    sums_in,
    back_out,
    back_in,
    relay_in,
    load_sem,
    ag_own_send,
    ag_fwd_send,
    ag_recv,
    lab_send,
    lab_recv,
    loss_send,
    loss_recv,
    core_send,
    core_recv,
    next_send,
    next_recv,
    end_send,
    end_recv,
    mid_send,
    mid_recv,
    sum_send,
    sum_recv,
    back_send,
    back_recv,
    relay_src_send,
    relay_recv,
    relay_fwd_send,
    ready,
):
    rows = images.shape[0]
    ag_rows = rows // AG_CHUNKS
    rs_rows = rows // RS_CHUNKS
    relay_rows = rows // RELAY_CHUNKS
    blk = lax.axis_index("blk")
    group = lax.axis_index("group")
    y = group // 2
    core = group % 2
    other = group + 1 - 2 * core
    half = blocks // 2
    mirrored = 2 * (CHIPS - 1 - y) + core
    up_edge = (blk % half) // (half - 1)
    down_edge = (half - 1 - blk % half) // (half - 1)
    up_dev = {"blk": (blk + 1) % blocks, "group": group + up_edge * (mirrored - group)}
    down_dev = {"blk": (blk + blocks - 1) % blocks, "group": group + down_edge * (mirrored - group)}
    column = blk % half
    shift = half - LINE
    passes = [jnp.where(column == offset, 1, 0) for offset in VIA]
    on_down = passes[0] + passes[1]
    on_up = jnp.where(column == LINE - 1, 1, 0)
    offset = VIA[0] * passes[0] + VIA[1] * passes[1]

    def inner_dev(step, turned=False):
        return {"blk": (blk + 2 * blocks + step) % blocks, "group": mirrored if turned else group}

    across_dev = inner_dev(half, True)
    wrap_dev = inner_dev((half - 1) * (down_edge - up_edge))
    via_devs = [inner_dev(v) for v in VIA]
    from_devs = [inner_dev(1 + v, True) for v in VIA]
    side_dev = inner_dev(shift * (on_up - up_edge))
    late_from_dev = inner_dev(-(shift + 1), True)
    late_to_dev = inner_dev(shift + 1, True)
    caption_source_dev = inner_dev(-offset)
    caption_target_dev = inner_dev(-(offset + 1), True)
    other_dev = {"blk": blk, "group": other}

    def chip(position):
        return {"blk": blk, "group": (position + CHIPS) % CHIPS * 2 + core}

    def remote(src, dst, send, recv, device):
        return pltpu.make_async_remote_copy(
            src_ref=src, dst_ref=dst, send_sem=send, recv_sem=recv, device_id=device, device_id_type=MESH
        )

    is_end = (y == 0) | (y == CHIPS - 1)
    is_middle = (y == 1) | (y == 2)
    relayed_up = is_middle & (up_edge == 1)
    relayed_down = is_middle & (down_edge == 1)
    relayed = is_middle & (up_edge + down_edge == 1)
    relays = is_middle & (on_up + on_down == 1)
    relays_down = is_middle & (on_down == 1)
    relays_up = is_middle & (on_up == 1)
    is_first = blk % LINE == 0
    is_last = blk % LINE == LINE - 1
    not_first = jnp.logical_not(is_first)
    not_last = jnp.logical_not(is_last)

    loads = [
        pltpu.make_async_copy(captions_hbm, captions, load_sem.at[0]),
        pltpu.make_async_copy(images_hbm, images, load_sem.at[1]),
        pltpu.make_async_copy(labels_hbm, labs.at[y], load_sem.at[2]),
    ]
    for load in loads:
        load.start()

    barrier = pltpu.get_barrier_semaphore()

    def greet(device):
        pl.semaphore_signal(barrier, inc=1, device_id=device, device_id_type=MESH)

    for device in [other_dev] + [chip(y + d) for d in (1, 2, 3)]:
        greet(device)

    @pl.when(not_last)
    def _():
        greet(up_dev)

    @pl.when(is_first)
    def _():
        greet(down_dev)

    @pl.when(relayed)
    def _():
        greet(across_dev)

    @pl.when(relayed_down)
    def _():
        for device in via_devs + [wrap_dev, late_from_dev]:
            greet(device)

    @pl.when(relayed_up | relays_up)
    def _():
        greet(side_dev)

    @pl.when(relays_down)
    def _():
        greet(caption_source_dev)
        greet(caption_target_dev)

    loads[0].wait()
    text_float, _ = unit_rows(captions[...])
    texts[0:rows, :] = text_float.astype(BF16)
    loads[1].wait()
    image_float, _ = unit_rows(images[...])
    imgs[y] = image_float.astype(BF16)
    loads[2].wait()

    inner = (y * (3 - y)) // 2
    peers = 4 + jnp.where(is_first, 0, 1) + jnp.where(is_last, 1, 0)
    peers = peers + inner * (5 * up_edge + 3 * down_edge + on_down + 2 * on_up)
    pl.semaphore_wait(barrier, peers)

    def answer(index, device):
        pl.semaphore_signal(ready.at[index], inc=1, device_id=device, device_id_type=MESH)

    @pl.when(not_first)
    def _():
        answer(0, down_dev)

    @pl.when(is_last)
    def _():
        answer(1, up_dev)

    @pl.when(relayed & is_last)
    def _():
        for device in from_devs:
            answer(2, device)
        answer(3, wrap_dev)

    def own_copy(c, direction):
        part = imgs.at[y, pl.ds(c * ag_rows, ag_rows)]
        return remote(
            part, part, ag_own_send.at[direction, c], ag_recv.at[y, c], chip(y + 1 - 2 * direction)
        )

    def fwd_copy(s, c):
        part = imgs.at[s, pl.ds(c * ag_rows, ag_rows)]
        target = jnp.where(s < y, y + 1, y - 1)
        return remote(part, part, ag_fwd_send.at[s, c], ag_recv.at[s, c], chip(target))

    def slot(i):
        return texts.at[pl.ds(i * rows, rows)]

    def relay_first(kind, source, c, device):
        where = pl.ds(c * relay_rows, relay_rows)
        return remote(
            source.at[where],
            relay_in.at[kind, where],
            relay_src_send.at[kind, c],
            relay_recv.at[kind, c],
            device,
        )

    def relay_on(kind, target, start, sem, c, device):
        return remote(
            relay_in.at[kind, pl.ds(c * relay_rows, relay_rows)],
            target.at[pl.ds(start + c * relay_rows, relay_rows)],
            relay_fwd_send.at[kind, c],
            sem,
            device,
        )

    def captions_first(c):
        return [relay_first(0, slot(0), c, device) for device in (wrap_dev, via_devs[c])]

    def sums_first(c):
        up = relay_first(1, back_out.at[1], c, side_dev)
        if c == 0:
            half_rows = pl.ds(0, relay_rows)
            up = remote(
                back_out.at[1, half_rows],
                back_in.at[0, half_rows],
                relay_src_send.at[1, c],
                back_recv.at[0],
                up_dev,
            )
        return [up, relay_first(1, back_out.at[0], c, wrap_dev)]

    def captions_on(c):
        return [
            relay_on(0, texts, 2 * rows, next_recv.at[0], c, across_dev),
            relay_on(0, texts, 4 * rows, next_recv.at[1], c, caption_target_dev),
        ]

    def sums_on(c):
        return [
            relay_on(1, back_in.at[0], 0, back_recv.at[0], c, late_to_dev),
            relay_on(1, back_in.at[1], 0, back_recv.at[1], c, across_dev),
        ]

    def each(copies, conditions, act):
        for copy, condition in zip(copies, conditions):
            pl.when(condition)(functools.partial(act, copy))

    def start(copy):
        copy.start()

    def sent(copy):
        copy.wait_send()

    def arrived_start(pair):
        pair[0].wait_recv()
        pair[1].start()

    def pass_captions(c):
        ways = [(captions_first(c)[0], copy) for copy in captions_on(c)]
        each(ways, (relayed_down, is_middle & (passes[c] == 1)), arrived_start)

    def pass_sums(c):
        ways = [(sums_first(c)[1], copy) for copy in sums_on(c)]
        each(ways[c == 0 :], (relays_up, relayed_up)[c == 0 :], arrived_start)

    next_up = remote(slot(0), slot(2), next_send.at[0], next_recv.at[0], up_dev)
    next_down = remote(slot(0), slot(4), next_send.at[1], next_recv.at[1], down_dev)
    core_copies = [
        remote(slot(2 * i), slot(2 * i + 1), core_send.at[i], core_recv.at[i], other_dev) for i in range(3)
    ]
    lab_copies = [
        remote(labs.at[y], labs.at[y], lab_send.at[d - 1], lab_recv.at[y], chip(y + d)) for d in (1, 2, 3)
    ]

    for c in range(RELAY_CHUNKS):
        each(captions_first(c), (relayed_up, relayed_down), start)

    for c in range(AG_CHUNKS):

        @pl.when(y < CHIPS - 1)
        def _():
            own_copy(c, 0).start()

        @pl.when(y > 0)
        def _():
            own_copy(c, 1).start()

    core_copies[0].start()

    @pl.when(not_first)
    def _():
        next_down.start()

    for copy in lab_copies:
        copy.start()

    @pl.when(not_last)
    def _():
        pl.semaphore_wait(ready.at[0], 1)

    @pl.when(jnp.logical_not(relayed_up))
    def _():
        next_up.start()

    parts[...] = jnp.zeros_like(parts)
    sums[...] = jnp.zeros_like(sums)
    loss_part[...] = jnp.zeros_like(loss_part)

    near = jnp.where(y == 0, 1, jnp.where(y == 1, 0, jnp.where(y == 2, 3, 2)))
    next_near = jnp.where(y == 0, 2, jnp.where(y == 1, 2, 1))
    far = jnp.where(y < 2, 3, 0)

    def take(s, c):
        copy = fwd_copy(s, c)
        copy.wait_recv()

        @pl.when(is_middle)
        def _():
            copy.start()

    def take_labels(s):
        remote(labs.at[s], labs.at[s], lab_send.at[0], lab_recv.at[s], chip(y + 1)).wait_recv()

    scale = scale_ref[0]
    bias = bias_ref[0]

    def compute(s, i):
        image = imgs[s]
        where = pl.ds(pl.multiple_of(2 * i * rows, 2 * rows), 2 * rows)
        text = texts[where, :]
        raw = depth_part(text, image, 0, 512) + depth_part(text, image, 512, text.shape[1])
        label = labs[s]
        mine = label - group * rows
        theirs = label - other * rows
        theirs = jnp.where((theirs >= 0) & (theirs < rows), theirs + rows, -1)
        place = jnp.where((mine >= 0) & (mine < rows), mine, theirs)
        place = jnp.where(i == 0, place, -1)
        positive = lax.broadcasted_iota(jnp.int32, raw.shape, 0) == place
        loss, weights = pair_weights(raw, positive, scale, bias)
        sums[where, :] += jnp.dot(weights, image, preferred_element_type=F32)
        parts[s] += lax.dot_general(weights, text, (((0,), (0,)), ((), ())), preferred_element_type=F32)
        loss_part[s] += loss

    def end_copy(t, c):
        where = pl.ds(c * rs_rows, rs_rows)
        return remote(
            parts_out.at[t, where],
            end_in.at[t, where],
            end_send.at[t, c],
            end_recv.at[t, c],
            chip(1 + y // (CHIPS - 1)),
        )

    def mid_copy(t, c):
        where = pl.ds(c * rs_rows, rs_rows)
        sender = (y + 1) % 2
        return remote(
            parts_out.at[t, where], mid_in.at[sender, where], mid_send.at[t, c], mid_recv.at[sender, c], chip(t)
        )

    def sum_copy(i):
        return remote(sums_out.at[i], sums_in.at[i], sum_send.at[i], sum_recv.at[i], other_dev)

    def finish(i):
        sum_copy(i).wait_recv()
        total = sums[2 * i * rows : (2 * i + 1) * rows, :] + sums_in[i].astype(F32)
        back_out[i - 1] = total.astype(BF16)
        direct = back_down if i == 1 else back_up
        edge = relayed_down if i == 1 else relayed_up

        @pl.when(jnp.logical_not(edge))
        def _():
            direct.start()

        @pl.when(edge)
        def _():
            if i == 1:
                pl.semaphore_wait(ready.at[3], 1)
            for c in range(RELAY_CHUNKS):
                sums_first(c)[2 - i].start()

    back_down = remote(back_out.at[0], back_in.at[1], back_send.at[0], back_recv.at[1], down_dev)
    back_up = remote(back_out.at[1], back_in.at[0], back_send.at[1], back_recv.at[0], up_dev)

    def chosen(u, usual, first, late):
        value = usual[0]
        for k in range(len(usual)):
            value = jnp.where(u == k, jnp.where(is_first, first[k], usual[k]), value)
            value = jnp.where((u == k) & relayed_up, late[k], value)
        return value

    usual_order = [y, near, near, near, y, y, next_near, next_near, next_near, far, far, far]
    late_order = [y, near, near, y, next_near, next_near, near, y, next_near, far, far, far]
    first_order = [y, near, near, y, next_near, next_near, far, far, far, next_near, near, y]

    def step(u, carry):
        s = chosen(u, usual_order, first_order, late_order)
        i = chosen(u, [0, 0, 1, 2, 1, 2, 0, 1, 2, 2, 1, 0], [0, 0, 2, 2, 0, 2, 2, 0, 1, 1, 1, 1], [0, 0, 1, 1, 0, 1, 2, 2, 2, 2, 1, 0])

        @pl.when(u == 0)
        def _():
            core_copies[0].wait_recv()

        @pl.when((u == 1) & is_middle)
        def _():
            for c in range(AG_CHUNKS):
                take(near, c)
                take(next_near, c)

        @pl.when((u == 1) & is_end)
        def _():
            for c in range(AG_CHUNKS):
                take(near, c)

        @pl.when(u == 1)
        def _():
            for other_slot in (near, next_near, far):
                take_labels(other_slot)

        @pl.when((u == 2) & is_first)
        def _():
            pl.semaphore_wait(ready.at[1], 1)

        @pl.when((u == 2) & is_first & jnp.logical_not(relayed_down))
        def _():
            next_down.start()

        @pl.when((u == 2) & relays_down)
        def _():
            pl.semaphore_wait(ready.at[2], 1)
            for c in range(RELAY_CHUNKS):
                pass_captions(c)

        @pl.when((u == 2) & is_first)
        def _():
            next_down.wait_recv()
            core_copies[2].start()

        @pl.when((u == 2) & not_first)
        def _():
            next_up.wait_recv()
            core_copies[1].start()

        @pl.when((u == 2) & is_middle)
        def _():
            take(far, 0)

        @pl.when((u == 2) & is_first)
        def _():
            core_copies[2].wait_recv()

        @pl.when((u == jnp.where(relayed_up, 6, 2)) & not_first)
        def _():
            next_down.wait_recv()
            core_copies[2].start()

        @pl.when((u == 2) & not_first)
        def _():
            core_copies[1].wait_recv()

        @pl.when((u == jnp.where(relayed_up, 6, 3)) & not_first)
        def _():
            core_copies[2].wait_recv()

        @pl.when((u == 4) & is_middle)
        def _():
            for c in range(1, AG_CHUNKS):
                take(far, c)

        @pl.when((u == jnp.where(is_first, 4, 6)) & is_end)
        def _():
            for c in range(AG_CHUNKS):
                take(next_near, c)

        @pl.when((u == jnp.where(is_first, 6, 9)) & is_end)
        def _():
            for c in range(AG_CHUNKS):
                take(far, c)

        for c in range(RELAY_CHUNKS):

            @pl.when((u == 6 + 2 * c) & relayed_down)
            def _():
                pass_captions(c)

        @pl.when((u == 8) & is_first)
        def _():
            next_up.wait_recv()
            core_copies[1].start()
            core_copies[1].wait_recv()

        @pl.when((u == 9) & is_first)
        def _():
            finish(2)

        compute(s, i)

        @pl.when((u == jnp.where(is_first, 10, 9)) & is_middle)
        def _():
            parts_out[near] = parts[near].astype(BF16)
            for c in range(RS_CHUNKS):
                mid_copy(near, c).start()

        @pl.when(jnp.where(is_first, (u == 6) | (u == 7) | (u == 11), u > 8))
        def _():
            start = pl.multiple_of((2 * i + 1) * rows, rows)
            sums_out[i] = sums[pl.ds(start, rows), :].astype(BF16)
            sum_copy(i).start()

        @pl.when(jnp.where(is_first, (u > 7) & (u < 11), (u == 3) | (u == 8) | (u == 11)) & is_end)
        def _():
            parts_out[s] = parts[s].astype(BF16)
            for c in range(RS_CHUNKS):
                end_copy(s, c).start()

        return carry

    lax.fori_loop(0, 3 * CHIPS, step, 0)

    @pl.when(not_first)
    def _():
        finish(2)

    finish(1)

    loss_copies = [
        remote(
            loss_part.at[(y + d) % CHIPS], loss_in.at[y], loss_send.at[d - 1], loss_recv.at[y], chip(y + d)
        )
        for d in (1, 2, 3)
    ]
    for copy in loss_copies:
        copy.start()

    def pass_on(t, c):
        where = pl.ds(pl.multiple_of(c * rs_rows, rs_rows), rs_rows)
        end_copy(t, c).wait_recv()
        total = parts[t, where, :] + end_in[t, where, :].astype(F32)
        parts_out[t, where, :] = total.astype(BF16)
        mid_copy(t, c).start()

    @pl.when(is_middle)
    def _():
        before = jnp.where(is_first, far, next_near)
        after = jnp.where(is_first, next_near, far)

        def pass_all(k, carry):
            pass_on(jnp.where(k < RS_CHUNKS, before, after), k % RS_CHUNKS)
            for c in range(RELAY_CHUNKS):

                @pl.when(relays_up & (k == RS_CHUNKS))
                def _():
                    pass_sums(c)

            return carry

        lax.fori_loop(0, 2 * RS_CHUNKS, pass_all, 0)

    @pl.when(relayed_up)
    def _():
        for c in range(RELAY_CHUNKS):
            pass_sums(c)

    sum_copy(0).wait_recv()
    text_sums = sums[0:rows, :] + sums_in[0].astype(F32)
    back_down.wait_recv()
    text_sums = text_sums + back_in[1].astype(F32)
    back_up.wait_recv()
    text_sums = text_sums + back_in[0].astype(F32)
    text_float, text_length = unit_rows(captions[...])
    text_out[...] = through_norm(text_sums, text_float, text_length)

    loss_total = loss_part[y]
    for d in (1, 2, 3):
        s = (y + d) % CHIPS
        remote(loss_part.at[s], loss_in.at[s], loss_send.at[0], loss_recv.at[s], chip(y + 1)).wait_recv()
        loss_total = loss_total + loss_in[s]
    loss_out[...] = loss_total

    for sender in (0, 1):

        @pl.when(y != sender + 1)
        def _():
            for c in range(RS_CHUNKS):
                where = pl.ds(c * rs_rows, rs_rows)
                part = mid_in.at[sender, where]
                remote(part, part, mid_send.at[0, c], mid_recv.at[sender, c], chip(y + 1)).wait_recv()
            parts[y] += mid_in[sender].astype(F32)

    @pl.when(is_middle)
    def _():
        for c in range(RS_CHUNKS):
            end_copy(y, c).wait_recv()
        parts[y] += end_in[y].astype(F32)

    image_float, image_length = unit_rows(images[...])
    image_out[...] = through_norm(parts[y], image_float, image_length)

    for c in range(AG_CHUNKS):

        @pl.when(y < CHIPS - 1)
        def _():
            own_copy(c, 0).wait_send()

        @pl.when(y > 0)
        def _():
            own_copy(c, 1).wait_send()

    def line_sent(d, carry):
        s = (y + d) % CHIPS

        @pl.when(is_middle)
        def _():
            for c in range(AG_CHUNKS):
                fwd_copy(s, c).wait_send()
            for c in range(RS_CHUNKS):
                mid_copy(s, c).wait_send()

        @pl.when(is_end)
        def _():
            for c in range(RS_CHUNKS):
                end_copy(s, c).wait_send()

        return carry

    lax.fori_loop(1, CHIPS, line_sent, 0)

    @pl.when(jnp.logical_not(relayed_up))
    def _():
        next_up.wait_send()
        back_up.wait_send()

    @pl.when(jnp.logical_not(relayed_down))
    def _():
        next_down.wait_send()
        back_down.wait_send()

    for c in range(RELAY_CHUNKS):
        each(captions_first(c) + sums_first(c), (relayed_up, relayed_down) * 2, sent)
        each(captions_on(c), (relayed_down, is_middle & (passes[c] == 1)), sent)
        each(sums_on(c)[c == 0 :], (relays_up, relayed_up)[c == 0 :], sent)

    for copy in core_copies + lab_copies + loss_copies + [sum_copy(i) for i in range(3)]:
        copy.wait_send()


def per_device(blocks, images, captions, labels, logit_scale, logit_bias):
    rows, width = images.shape
    vmem = pl.BlockSpec(memory_space=pltpu.VMEM)
    smem = pl.BlockSpec(memory_space=pltpu.SMEM)
    hbm = pl.BlockSpec(memory_space=pl.ANY)
    dma = pltpu.SemaphoreType.DMA
    loss, image_grad, text_grad = pl.pallas_call(
        functools.partial(kernel, blocks),
        out_shape=[
            jax.ShapeDtypeStruct((1, rows), F32),
            jax.ShapeDtypeStruct((rows, width), F32),
            jax.ShapeDtypeStruct((rows, width), F32),
        ],
        in_specs=[hbm, hbm, hbm, smem, smem],
        out_specs=[vmem, vmem, vmem],
        scratch_shapes=[
            pltpu.VMEM((rows, width), BF16),
            pltpu.VMEM((rows, width), BF16),
            pltpu.VMEM((CHIPS, rows, width), BF16),
            pltpu.VMEM((6 * rows, width), BF16),
            pltpu.VMEM((CHIPS, 1, rows), jnp.int32),
            pltpu.VMEM((CHIPS, 1, rows), F32),
            pltpu.VMEM((CHIPS, 1, rows), F32),
            pltpu.VMEM((CHIPS, rows, width), F32),
            pltpu.VMEM((CHIPS, rows, width), BF16),
            pltpu.VMEM((CHIPS, rows, width), BF16),
            pltpu.VMEM((2, rows, width), BF16),
            pltpu.VMEM((6 * rows, width), F32),
            pltpu.VMEM((3, rows, width), BF16),
            pltpu.VMEM((3, rows, width), BF16),
            pltpu.VMEM((2, rows, width), BF16),
            pltpu.VMEM((2, rows, width), BF16),
            pltpu.VMEM((2, rows, width), BF16),
            dma((3,)),
            dma((2, AG_CHUNKS)),
            dma((CHIPS, AG_CHUNKS)),
            dma((CHIPS, AG_CHUNKS)),
            dma((3,)),
            dma((CHIPS,)),
            dma((3,)),
            dma((CHIPS,)),
            dma((3,)),
            dma((3,)),
            dma((2,)),
            dma((2,)),
            dma((CHIPS, RS_CHUNKS)),
            dma((CHIPS, RS_CHUNKS)),
            dma((CHIPS, RS_CHUNKS)),
            dma((2, RS_CHUNKS)),
            dma((3,)),
            dma((3,)),
            dma((2,)),
            dma((2,)),
            dma((2, RELAY_CHUNKS)),
            dma((2, RELAY_CHUNKS)),
            dma((2, RELAY_CHUNKS)),
            pltpu.SemaphoreType.REGULAR((4,)),
        ],
        compiler_params=pltpu.CompilerParams(
            collective_id=0, has_side_effects=True, vmem_limit_bytes=48 * 1024 * 1024
        ),
    )(images, captions, labels.reshape(1, rows), logit_scale, logit_bias)
    return (loss.reshape(rows), image_grad, text_grad)


def solution(mesh):
    body = functools.partial(per_device, mesh.shape["blk"])
    in_specs = (P(("blk", "group"), None), P(("blk", "group"), None), P(("blk", "group")), P(), P())
    out_specs = (P(("blk", "group")), P(("blk", "group"), None), P(("blk", "group"), None))
    return jax.shard_map(body, mesh=mesh, in_specs=in_specs, out_specs=out_specs, check_vma=False)
```

```python
import functools

import jax
import jax.numpy as jnp
from jax import lax
from jax.experimental import pallas as pl
from jax.experimental.pallas import tpu as pltpu
from jax.sharding import PartitionSpec as P

EPSILON = 1e-06
CHIPS = 4
LINE = 8
CAPTIONS_VIA = ((24, 0, 48), (8, 48, 48), (16, 96, 32))
CAPTIONS_UP_VIA = (8, 16)
SUMS_UP_VIA = (24, 16)
SUMS_DOWN_VIA = (23, 31)
AG_CHUNKS = 2
RS_CHUNKS = 8
MESH = pl.DeviceIdType.MESH
F32 = jnp.float32
BF16 = jnp.bfloat16


def unit_rows(values):
    wide = values.astype(F32)
    length = jnp.sqrt(jnp.sum(wide * wide, axis=-1, keepdims=True) + EPSILON)
    return (wide / length, length)


def through_norm(sums, unit_float, length):
    return (sums - unit_float * jnp.sum(unit_float * sums, axis=-1, keepdims=True)) / length


def depth_part(a, b, start, stop):
    return lax.dot_general(
        a[:, start:stop], b[:, start:stop], (((1,), (1,)), ((), ())), preferred_element_type=F32
    )


def summed_log(decay):
    pieces = [decay[i : i + 8, :] for i in range(0, decay.shape[0], 8)]
    while len(pieces) > 1:
        pieces = [a + b + a * b for a, b in zip(pieces[::2], pieces[1::2])]
    return jnp.sum(jnp.log1p(pieces[0]), axis=0, keepdims=True)


def pair_weights(raw, positive, scale, bias):
    logits = scale * raw + bias
    turned = jnp.where(positive, -logits, logits)
    decay = jnp.exp(-jnp.abs(turned))
    loss = jnp.sum(jnp.maximum(turned, 0.0), axis=0, keepdims=True) + summed_log(decay)
    share = jnp.where(turned >= 0, 1.0, decay) / (1.0 + decay)
    weights = jnp.where(positive, -scale, scale) * share
    return (loss, weights.astype(BF16))


def kernel(
    blocks,
    images_hbm,
    captions_hbm,
    labels_hbm,
    scale_ref,
    bias_ref,
    loss_out,
    image_out,
    text_out,
    images,
    captions,
    imgs,
    texts,
    labs,
    loss_part,
    loss_in,
    parts,
    parts_out,
    end_in,
    mid_in,
    sums,
    sums_out,
    sums_in,
    back_out,
    back_in,
    relay_in,
    load_sem,
    ag_own_send,
    ag_fwd_send,
    ag_recv,
    lab_send,
    lab_recv,
    loss_send,
    loss_recv,
    core_send,
    core_recv,
    next_send,
    next_recv,
    end_send,
    end_recv,
    mid_send,
    mid_recv,
    sum_send,
    sum_recv,
    back_send,
    back_recv,
    relay_src_send,
    relay_recv,
    relay_fwd_send,
    ready,
):
    rows = images.shape[0]
    ag_rows = rows // AG_CHUNKS
    rs_rows = rows // RS_CHUNKS
    blk = lax.axis_index("blk")
    group = lax.axis_index("group")
    y = group // 2
    core = group % 2
    other = group + 1 - 2 * core
    half = blocks // 2
    mirrored = 2 * (CHIPS - 1 - y) + core
    up_edge = (blk % half) // (half - 1)
    down_edge = (half - 1 - blk % half) // (half - 1)
    up_dev = {"blk": (blk + 1) % blocks, "group": group + up_edge * (mirrored - group)}
    down_dev = {"blk": (blk + blocks - 1) % blocks, "group": group + down_edge * (mirrored - group)}
    column = blk % half

    def inner_dev(step, turned=False):
        return {"blk": (blk + 2 * blocks + step) % blocks, "group": mirrored if turned else group}

    across_dev = inner_dev(half, True)
    wrap_dev = inner_dev((half - 1) * (down_edge - up_edge))
    other_dev = {"blk": blk, "group": other}

    def chip(position):
        return {"blk": blk, "group": (position + CHIPS) % CHIPS * 2 + core}

    def remote(src, dst, send, recv, device):
        return pltpu.make_async_remote_copy(
            src_ref=src, dst_ref=dst, send_sem=send, recv_sem=recv, device_id=device, device_id_type=MESH
        )

    is_end = (y == 0) | (y == CHIPS - 1)
    is_middle = (y == 1) | (y == 2)
    relayed_up = is_middle & (up_edge == 1)
    relayed_down = is_middle & (down_edge == 1)
    relayed = is_middle & (up_edge + down_edge == 1)
    in_column = {offset: is_middle & (column == offset) for offset in (7, 8, 15, 16, 23, 24)}
    is_first = blk % LINE == 0
    is_last = blk % LINE == LINE - 1
    not_first = jnp.logical_not(is_first)
    not_last = jnp.logical_not(is_last)

    loads = [
        pltpu.make_async_copy(captions_hbm, captions, load_sem.at[0]),
        pltpu.make_async_copy(images_hbm, images, load_sem.at[1]),
        pltpu.make_async_copy(labels_hbm, labs.at[y], load_sem.at[2]),
    ]
    for load in loads:
        load.start()

    barrier = pltpu.get_barrier_semaphore()

    def greet(device):
        pl.semaphore_signal(barrier, inc=1, device_id=device, device_id_type=MESH)

    for device in [other_dev] + [chip(y + d) for d in (1, 2, 3)]:
        greet(device)

    @pl.when(not_last)
    def _():
        greet(up_dev)

    @pl.when(is_first)
    def _():
        greet(down_dev)

    @pl.when(relayed_down)
    def _():
        greet(wrap_dev)
        for offset in CAPTIONS_UP_VIA:
            greet(inner_dev(offset - half, True))
        greet(inner_dev(SUMS_DOWN_VIA[0]))
        for offset, _, _ in CAPTIONS_VIA:
            greet(inner_dev(offset))
        for offset in SUMS_UP_VIA:
            greet(inner_dev(-offset - 1, True))

    for offset in CAPTIONS_UP_VIA:

        @pl.when(in_column[offset])
        def _():
            greet(inner_dev(half - 1 - offset))
            greet(inner_dev(half - offset, True))

    @pl.when(relayed_up)
    def _():
        greet(across_dev)
        greet(inner_dev(SUMS_DOWN_VIA[0] + 1 - blocks, True))
        for offset in SUMS_UP_VIA:
            greet(inner_dev(-offset))

    for offset, _, _ in CAPTIONS_VIA:

        @pl.when(in_column[offset])
        def _():
            greet(inner_dev(-offset))
            greet(inner_dev(-offset - 1, True))

    for offset in SUMS_UP_VIA:

        @pl.when(in_column[half - 1 - offset])
        def _():
            greet(inner_dev(offset))

    @pl.when(in_column[SUMS_DOWN_VIA[0]])
    def _():
        greet(inner_dev(blocks - 1 - SUMS_DOWN_VIA[0], True))

    loads[0].wait()
    text_float, _ = unit_rows(captions[...])
    texts[0:rows, :] = text_float.astype(BF16)
    loads[1].wait()
    image_float, _ = unit_rows(images[...])
    imgs[y] = image_float.astype(BF16)
    loads[2].wait()

    inner = (y * (3 - y)) // 2
    peers = 4 + jnp.where(is_first, 0, 1) + jnp.where(is_last, 1, 0)
    inner_peers = 10 * up_edge + 5 * down_edge
    for offset, count in ((24, 1), (8, 2), (16, 2), (7, 2), (15, 2), (23, 2)):
        inner_peers = inner_peers + jnp.where(column == offset, count, 0)
    peers = peers + inner * inner_peers
    pl.semaphore_wait(barrier, peers)

    def answer(index, device):
        pl.semaphore_signal(ready.at[index], inc=1, device_id=device, device_id_type=MESH)

    @pl.when(not_first)
    def _():
        answer(0, down_dev)

    @pl.when(is_last)
    def _():
        answer(1, up_dev)

    @pl.when(relayed & is_last)
    def _():
        for offset, _, _ in CAPTIONS_VIA:
            answer(2, inner_dev(offset + 1, True))
        answer(4, wrap_dev)

    @pl.when(in_column[SUMS_DOWN_VIA[0]])
    def _():
        answer(3, inner_dev(-SUMS_DOWN_VIA[0]))

    def own_copy(c, direction):
        part = imgs.at[y, pl.ds(c * ag_rows, ag_rows)]
        return remote(
            part, part, ag_own_send.at[direction, c], ag_recv.at[y, c], chip(y + 1 - 2 * direction)
        )

    def fwd_copy(s, c):
        part = imgs.at[s, pl.ds(c * ag_rows, ag_rows)]
        target = jnp.where(s < y, y + 1, y - 1)
        return remote(part, part, ag_fwd_send.at[s, c], ag_recv.at[s, c], chip(target))

    def slot(i):
        return texts.at[pl.ds(i * rows, rows)]

    def flow(kind, c):
        if kind == 0:
            offset = CAPTIONS_UP_VIA[c]
            begin, size, source = c * 64, 64, slot(0)
            near_dev, far_dev = inner_dev(offset + 1 - half), inner_dev(half - offset, True)
            target, base, sem, sends, passes = texts, 2 * rows, next_recv.at[0], relayed_up, in_column[offset]
        elif kind == 1:
            offset, begin, size = CAPTIONS_VIA[c]
            source, near_dev, far_dev = slot(0), inner_dev(offset), inner_dev(-offset - 1, True)
            target, base, sem, sends, passes = texts, 4 * rows, next_recv.at[1], relayed_down, in_column[offset]
        elif kind == 2:
            offset = SUMS_UP_VIA[c]
            begin, size, source = c * 64, 64, back_out.at[1]
            near_dev, far_dev = inner_dev(-offset), inner_dev(offset + 1, True)
            target, base, sem = back_in.at[0], 0, back_recv.at[0]
            sends, passes = relayed_up, in_column[half - 1 - offset]
        else:
            offset = SUMS_DOWN_VIA[c]
            begin, size, source = c * 64, 64, back_out.at[0]
            near_dev, far_dev = inner_dev(offset), inner_dev(blocks - 1 - offset, True)
            target, base, sem = back_in.at[1], 0, back_recv.at[1]
            sends, passes = relayed_down, in_column[offset] if c == 0 else relayed_up
        held = relay_in.at[kind, pl.ds(begin, size)]
        first = remote(
            source.at[pl.ds(begin, size)], held, relay_src_send.at[kind, c], relay_recv.at[kind, c], near_dev
        )
        second = remote(
            held, target.at[pl.ds(base + begin, size)], relay_fwd_send.at[kind, c], sem, far_dev
        )
        return first, second, sends, passes

    flow_parts = [(0, 0), (0, 1), (1, 0), (1, 1), (1, 2), (2, 0), (2, 1), (3, 0), (3, 1)]

    def send_flow(kind, c):
        first, _, sends, _ = flow(kind, c)

        @pl.when(sends)
        def _():
            first.start()

    def pass_flow(kind, c):
        first, second, _, passes = flow(kind, c)

        @pl.when(passes)
        def _():
            first.wait_recv()
            second.start()

    next_up = remote(slot(0), slot(2), next_send.at[0], next_recv.at[0], up_dev)
    next_down = remote(slot(0), slot(4), next_send.at[1], next_recv.at[1], down_dev)
    core_copies = [
        remote(slot(2 * i), slot(2 * i + 1), core_send.at[i], core_recv.at[i], other_dev) for i in range(3)
    ]
    lab_copies = [
        remote(labs.at[y], labs.at[y], lab_send.at[d - 1], lab_recv.at[y], chip(y + d)) for d in (1, 2, 3)
    ]

    for kind, c in flow_parts[:5]:
        send_flow(kind, c)

    for c in range(AG_CHUNKS):

        @pl.when(y < CHIPS - 1)
        def _():
            own_copy(c, 0).start()

        @pl.when(y > 0)
        def _():
            own_copy(c, 1).start()

    core_copies[0].start()

    @pl.when(not_first)
    def _():
        next_down.start()

    for copy in lab_copies:
        copy.start()

    @pl.when(not_last)
    def _():
        pl.semaphore_wait(ready.at[0], 1)

    @pl.when(jnp.logical_not(relayed_up))
    def _():
        next_up.start()

    parts[...] = jnp.zeros_like(parts)
    sums[...] = jnp.zeros_like(sums)
    loss_part[...] = jnp.zeros_like(loss_part)

    near = jnp.where(y == 0, 1, jnp.where(y == 1, 0, jnp.where(y == 2, 3, 2)))
    next_near = jnp.where(y == 0, 2, jnp.where(y == 1, 2, 1))
    far = jnp.where(y < 2, 3, 0)

    def take(s, c):
        copy = fwd_copy(s, c)
        copy.wait_recv()

        @pl.when(is_middle)
        def _():
            copy.start()

    def take_labels(s):
        remote(labs.at[s], labs.at[s], lab_send.at[0], lab_recv.at[s], chip(y + 1)).wait_recv()

    scale = scale_ref[0]
    bias = bias_ref[0]

    def compute(s, i):
        image = imgs[s]
        where = pl.ds(pl.multiple_of(2 * i * rows, 2 * rows), 2 * rows)
        text = texts[where, :]
        raw = depth_part(text, image, 0, 512) + depth_part(text, image, 512, text.shape[1])
        label = labs[s]
        mine = label - group * rows
        theirs = label - other * rows
        theirs = jnp.where((theirs >= 0) & (theirs < rows), theirs + rows, -1)
        place = jnp.where((mine >= 0) & (mine < rows), mine, theirs)
        place = jnp.where(i == 0, place, -1)
        positive = lax.broadcasted_iota(jnp.int32, raw.shape, 0) == place
        loss, weights = pair_weights(raw, positive, scale, bias)
        sums[where, :] += jnp.dot(weights, image, preferred_element_type=F32)
        parts[s] += lax.dot_general(weights, text, (((0,), (0,)), ((), ())), preferred_element_type=F32)
        loss_part[s] += loss

    def end_copy(t, c):
        where = pl.ds(c * rs_rows, rs_rows)
        return remote(
            parts_out.at[t, where],
            end_in.at[t, where],
            end_send.at[t, c],
            end_recv.at[t, c],
            chip(1 + y // (CHIPS - 1)),
        )

    def mid_copy(t, c):
        where = pl.ds(c * rs_rows, rs_rows)
        sender = (y + 1) % 2
        return remote(
            parts_out.at[t, where], mid_in.at[sender, where], mid_send.at[t, c], mid_recv.at[sender, c], chip(t)
        )

    def sum_copy(i):
        return remote(sums_out.at[i], sums_in.at[i], sum_send.at[i], sum_recv.at[i], other_dev)

    def finish(i):
        sum_copy(i).wait_recv()
        total = sums[2 * i * rows : (2 * i + 1) * rows, :] + sums_in[i].astype(F32)
        back_out[i - 1] = total.astype(BF16)
        direct = back_down if i == 1 else back_up
        edge = relayed_down if i == 1 else relayed_up

        @pl.when(jnp.logical_not(edge))
        def _():
            direct.start()

        if i == 1:

            @pl.when(edge)
            def _():
                pl.semaphore_wait(ready.at[3], 1)
                pl.semaphore_wait(ready.at[4], 1)

        for c in range(2):
            send_flow(4 - i, c)

    back_down = remote(back_out.at[0], back_in.at[1], back_send.at[0], back_recv.at[1], down_dev)
    back_up = remote(back_out.at[1], back_in.at[0], back_send.at[1], back_recv.at[0], up_dev)

    first_ends = is_first & is_end
    end_step = jnp.where(is_end, 1, 0)

    def chosen(u, usual, first, first_end, late):
        value = usual[0]
        for k in range(len(usual)):
            value = jnp.where(u == k, jnp.where(is_first, first[k], usual[k]), value)
            value = jnp.where((u == k) & relayed_up, late[k], value)
            value = jnp.where((u == k) & first_ends, first_end[k], value)
        return value

    usual_order = [y, near, near, near, y, y, next_near, next_near, next_near, far, far, far]
    late_order = [y, near, near, y, next_near, next_near, near, y, next_near, far, far, far]
    first_end_order = [y, near, near, y, next_near, next_near, next_near, far, far, far, near, y]
    first_order = [y, near, near, y, next_near, next_near, far, far, far, next_near, near, y]

    def step(u, carry):
        s = chosen(u, usual_order, first_order, first_end_order, late_order)
        i = chosen(u, [0, 0, 1, 2, 1, 2, 0, 1, 2, 2, 1, 0], [0, 0, 2, 2, 0, 2, 2, 0, 1, 1, 1, 1], [0, 0, 2, 2, 0, 2, 1, 2, 0, 1, 1, 1], [0, 0, 1, 1, 0, 1, 2, 2, 2, 2, 1, 0])

        @pl.when(u == 0)
        def _():
            core_copies[0].wait_recv()

        @pl.when((u == 1) & is_middle)
        def _():
            for c in range(AG_CHUNKS):
                take(near, c)
                take(next_near, c)

        @pl.when((u == 1) & is_end)
        def _():
            for c in range(AG_CHUNKS):
                take(near, c)

        @pl.when(u == 1)
        def _():
            for other_slot in (near, next_near, far):
                take_labels(other_slot)

        @pl.when((u == 2) & is_first)
        def _():
            pl.semaphore_wait(ready.at[1], 1)

        @pl.when((u == 2) & is_first & jnp.logical_not(relayed_down))
        def _():
            next_down.start()

        @pl.when((u == 2) & (in_column[8] | in_column[16] | in_column[24]))
        def _():
            pl.semaphore_wait(ready.at[2], 1)
            for c in range(3):
                pass_flow(1, c)

        @pl.when((u == 2) & is_first)
        def _():
            next_down.wait_recv()
            core_copies[2].start()

        @pl.when((u == 2) & not_first)
        def _():
            next_up.wait_recv()
            core_copies[1].start()

        @pl.when((u == 2) & is_middle)
        def _():
            take(far, 0)

        @pl.when((u == 2) & is_first)
        def _():
            core_copies[2].wait_recv()

        @pl.when((u == jnp.where(relayed_up, 6, 2)) & not_first)
        def _():
            next_down.wait_recv()
            core_copies[2].start()

        @pl.when((u == 2) & not_first)
        def _():
            core_copies[1].wait_recv()

        @pl.when((u == jnp.where(relayed_up, 6, 3)) & not_first)
        def _():
            core_copies[2].wait_recv()

        @pl.when((u == 4) & is_middle)
        def _():
            for c in range(1, AG_CHUNKS):
                take(far, c)

        @pl.when((u == jnp.where(is_first, 4, 6)) & is_end)
        def _():
            for c in range(AG_CHUNKS):
                take(next_near, c)

        @pl.when((u == jnp.where(is_first, 7, 9)) & is_end)
        def _():
            for c in range(AG_CHUNKS):
                take(far, c)

        @pl.when((u == 6) & (in_column[8] | in_column[16]))
        def _():
            pass_flow(0, 0)
            pass_flow(0, 1)

        @pl.when((u == jnp.where(is_end, 6, 8)) & is_first)
        def _():
            next_up.wait_recv()
            core_copies[1].start()
            core_copies[1].wait_recv()

        @pl.when((u == jnp.where(is_end, 11, 9)) & is_first)
        def _():
            finish(2)

        compute(s, i)

        @pl.when((u == jnp.where(is_first, 10, 9)) & is_middle)
        def _():
            parts_out[near] = parts[near].astype(BF16)
            for c in range(RS_CHUNKS):
                mid_copy(near, c).start()

        @pl.when(jnp.where(is_first, (u == 6 + end_step) | (u == 7 + end_step) | (u == 11), u > 8))
        def _():
            start = pl.multiple_of((2 * i + 1) * rows, rows)
            sums_out[i] = sums[pl.ds(start, rows), :].astype(BF16)
            sum_copy(i).start()

        @pl.when(jnp.where(is_first, (u == 6) | (u == 9) | (u == 10), (u == 3) | (u == 8) | (u == 11)) & is_end)
        def _():
            parts_out[s] = parts[s].astype(BF16)
            for c in range(RS_CHUNKS):
                end_copy(s, c).start()

        return carry

    lax.fori_loop(0, 3 * CHIPS, step, 0)

    @pl.when(not_first)
    def _():
        finish(2)

    @pl.when(jnp.logical_not(is_first & is_middle))
    def _():
        finish(1)

    loss_copies = [
        remote(
            loss_part.at[(y + d) % CHIPS], loss_in.at[y], loss_send.at[d - 1], loss_recv.at[y], chip(y + d)
        )
        for d in (1, 2, 3)
    ]
    for copy in loss_copies:
        copy.start()

    def pass_on(t, c):
        where = pl.ds(pl.multiple_of(c * rs_rows, rs_rows), rs_rows)
        end_copy(t, c).wait_recv()
        total = parts[t, where, :] + end_in[t, where, :].astype(F32)
        parts_out[t, where, :] = total.astype(BF16)
        mid_copy(t, c).start()

    @pl.when(is_middle)
    def _():
        def pass_all(k, carry):
            pass_on(jnp.where(k < RS_CHUNKS, next_near, far), k % RS_CHUNKS)

            @pl.when(is_first & (k == RS_CHUNKS - 1))
            def _():
                finish(1)

            @pl.when((in_column[7] | in_column[15]) & (k == 1))
            def _():
                pass_flow(2, 0)
                pass_flow(2, 1)

            @pl.when(in_column[23] & (k == RS_CHUNKS + RS_CHUNKS // 2))
            def _():
                pass_flow(3, 0)

            return carry

        lax.fori_loop(0, 2 * RS_CHUNKS, pass_all, 0)

    pass_flow(3, 1)

    sum_copy(0).wait_recv()
    text_sums = sums[0:rows, :] + sums_in[0].astype(F32)
    back_down.wait_recv()
    text_sums = text_sums + back_in[1].astype(F32)
    back_up.wait_recv()
    text_sums = text_sums + back_in[0].astype(F32)
    text_float, text_length = unit_rows(captions[...])
    text_out[...] = through_norm(text_sums, text_float, text_length)

    loss_total = loss_part[y]
    for d in (1, 2, 3):
        s = (y + d) % CHIPS
        remote(loss_part.at[s], loss_in.at[s], loss_send.at[0], loss_recv.at[s], chip(y + 1)).wait_recv()
        loss_total = loss_total + loss_in[s]
    loss_out[...] = loss_total

    for sender in (0, 1):

        @pl.when(y != sender + 1)
        def _():
            for c in range(RS_CHUNKS):
                where = pl.ds(c * rs_rows, rs_rows)
                part = mid_in.at[sender, where]
                remote(part, part, mid_send.at[0, c], mid_recv.at[sender, c], chip(y + 1)).wait_recv()
            parts[y] += mid_in[sender].astype(F32)

    @pl.when(is_middle)
    def _():
        for c in range(RS_CHUNKS):
            end_copy(y, c).wait_recv()
        parts[y] += end_in[y].astype(F32)

    image_float, image_length = unit_rows(images[...])
    image_out[...] = through_norm(parts[y], image_float, image_length)

    for c in range(AG_CHUNKS):

        @pl.when(y < CHIPS - 1)
        def _():
            own_copy(c, 0).wait_send()

        @pl.when(y > 0)
        def _():
            own_copy(c, 1).wait_send()

    def line_sent(d, carry):
        s = (y + d) % CHIPS

        @pl.when(is_middle)
        def _():
            for c in range(AG_CHUNKS):
                fwd_copy(s, c).wait_send()
            for c in range(RS_CHUNKS):
                mid_copy(s, c).wait_send()

        @pl.when(is_end)
        def _():
            for c in range(RS_CHUNKS):
                end_copy(s, c).wait_send()

        return carry

    lax.fori_loop(1, CHIPS, line_sent, 0)

    @pl.when(jnp.logical_not(relayed_up))
    def _():
        next_up.wait_send()
        back_up.wait_send()

    @pl.when(jnp.logical_not(relayed_down))
    def _():
        next_down.wait_send()
        back_down.wait_send()

    for kind, c in flow_parts:
        first, second, sends, passes = flow(kind, c)
        pl.when(sends)(first.wait_send)
        pl.when(passes)(second.wait_send)

    for copy in core_copies + lab_copies + loss_copies + [sum_copy(i) for i in range(3)]:
        copy.wait_send()


def per_device(blocks, images, captions, labels, logit_scale, logit_bias):
    rows, width = images.shape
    vmem = pl.BlockSpec(memory_space=pltpu.VMEM)
    smem = pl.BlockSpec(memory_space=pltpu.SMEM)
    hbm = pl.BlockSpec(memory_space=pl.ANY)
    dma = pltpu.SemaphoreType.DMA
    loss, image_grad, text_grad = pl.pallas_call(
        functools.partial(kernel, blocks),
        out_shape=[
            jax.ShapeDtypeStruct((1, rows), F32),
            jax.ShapeDtypeStruct((rows, width), F32),
            jax.ShapeDtypeStruct((rows, width), F32),
        ],
        in_specs=[hbm, hbm, hbm, smem, smem],
        out_specs=[vmem, vmem, vmem],
        scratch_shapes=[
            pltpu.VMEM((rows, width), BF16),
            pltpu.VMEM((rows, width), BF16),
            pltpu.VMEM((CHIPS, rows, width), BF16),
            pltpu.VMEM((6 * rows, width), BF16),
            pltpu.VMEM((CHIPS, 1, rows), jnp.int32),
            pltpu.VMEM((CHIPS, 1, rows), F32),
            pltpu.VMEM((CHIPS, 1, rows), F32),
            pltpu.VMEM((CHIPS, rows, width), F32),
            pltpu.VMEM((CHIPS, rows, width), BF16),
            pltpu.VMEM((CHIPS, rows, width), BF16),
            pltpu.VMEM((2, rows, width), BF16),
            pltpu.VMEM((6 * rows, width), F32),
            pltpu.VMEM((3, rows, width), BF16),
            pltpu.VMEM((3, rows, width), BF16),
            pltpu.VMEM((2, rows, width), BF16),
            pltpu.VMEM((2, rows, width), BF16),
            pltpu.VMEM((4, rows, width), BF16),
            dma((3,)),
            dma((2, AG_CHUNKS)),
            dma((CHIPS, AG_CHUNKS)),
            dma((CHIPS, AG_CHUNKS)),
            dma((3,)),
            dma((CHIPS,)),
            dma((3,)),
            dma((CHIPS,)),
            dma((3,)),
            dma((3,)),
            dma((2,)),
            dma((2,)),
            dma((CHIPS, RS_CHUNKS)),
            dma((CHIPS, RS_CHUNKS)),
            dma((CHIPS, RS_CHUNKS)),
            dma((2, RS_CHUNKS)),
            dma((3,)),
            dma((3,)),
            dma((2,)),
            dma((2,)),
            dma((4, 3)),
            dma((4, 3)),
            dma((4, 3)),
            pltpu.SemaphoreType.REGULAR((5,)),
        ],
        compiler_params=pltpu.CompilerParams(
            collective_id=0, has_side_effects=True, vmem_limit_bytes=48 * 1024 * 1024
        ),
    )(images, captions, labels.reshape(1, rows), logit_scale, logit_bias)
    return (loss.reshape(rows), image_grad, text_grad)


def solution(mesh):
    body = functools.partial(per_device, mesh.shape["blk"])
    in_specs = (P(("blk", "group"), None), P(("blk", "group"), None), P(("blk", "group")), P(), P())
    out_specs = (P(("blk", "group")), P(("blk", "group"), None), P(("blk", "group"), None))
    return jax.shard_map(body, mesh=mesh, in_specs=in_specs, out_specs=out_specs, check_vma=False)
```

```python
import functools

import jax
import jax.numpy as jnp
from jax import lax
from jax.experimental import pallas as pl
from jax.experimental.pallas import tpu as pltpu
from jax.sharding import PartitionSpec as P

EPSILON = 1e-06
CHIPS = 4
LINE = 8
CAPTIONS_VIA = ((24, 0, 48), (8, 48, 48), (16, 96, 32))
CAPTIONS_UP_VIA = (8, 16)
SUMS_UP_VIA = ((24, 0, 48), (16, 48, 48), (8, 96, 32))
SUMS_DOWN_VIA = (23, 31)
AG_CHUNKS = 2
RS_CHUNKS = 4
MESH = pl.DeviceIdType.MESH
F32 = jnp.float32
BF16 = jnp.bfloat16


def unit_rows(values):
    wide = values.astype(F32)
    length = jnp.sqrt(jnp.sum(wide * wide, axis=-1, keepdims=True) + EPSILON)
    return (wide / length, length)


def through_norm(sums, unit_float, length):
    return (sums - unit_float * jnp.sum(unit_float * sums, axis=-1, keepdims=True)) / length


def depth_part(a, b, start, stop):
    return lax.dot_general(
        a[:, start:stop], b[:, start:stop], (((1,), (1,)), ((), ())), preferred_element_type=F32
    )


def summed_log(decay):
    pieces = [decay[i : i + 8, :] for i in range(0, decay.shape[0], 8)]
    while len(pieces) > 1:
        pieces = [a + b + a * b for a, b in zip(pieces[::2], pieces[1::2])]
    return jnp.sum(jnp.log1p(pieces[0]), axis=0, keepdims=True)


def pair_weights(raw, positive, scale, bias):
    logits = scale * raw + bias
    turned = jnp.where(positive, -logits, logits)
    decay = jnp.exp(-jnp.abs(turned))
    loss = jnp.sum(jnp.maximum(turned, 0.0), axis=0, keepdims=True) + summed_log(decay)
    share = jnp.where(turned >= 0, 1.0, decay) / (1.0 + decay)
    weights = jnp.where(positive, -scale, scale) * share
    return (loss, weights.astype(BF16))


def kernel(
    blocks,
    images_hbm,
    captions_hbm,
    labels_hbm,
    scale_ref,
    bias_ref,
    loss_out,
    image_out,
    text_out,
    images,
    captions,
    imgs,
    texts,
    labs,
    loss_part,
    loss_in,
    parts,
    parts_out,
    end_in,
    mid_in,
    sums,
    sums_out,
    sums_in,
    back_out,
    back_in,
    relay_in,
    load_sem,
    ag_own_send,
    ag_fwd_send,
    ag_recv,
    lab_send,
    lab_recv,
    loss_send,
    loss_recv,
    core_send,
    core_recv,
    next_send,
    next_recv,
    end_send,
    end_recv,
    mid_send,
    mid_recv,
    sum_send,
    sum_recv,
    back_send,
    back_recv,
    relay_src_send,
    relay_recv,
    relay_fwd_send,
    ready,
):
    rows = images.shape[0]
    ag_rows = rows // AG_CHUNKS
    rs_rows = rows // RS_CHUNKS
    blk = lax.axis_index("blk")
    group = lax.axis_index("group")
    y = group // 2
    core = group % 2
    other = group + 1 - 2 * core
    half = blocks // 2
    mirrored = 2 * (CHIPS - 1 - y) + core
    up_edge = (blk % half) // (half - 1)
    down_edge = (half - 1 - blk % half) // (half - 1)
    up_dev = {"blk": (blk + 1) % blocks, "group": group + up_edge * (mirrored - group)}
    down_dev = {"blk": (blk + blocks - 1) % blocks, "group": group + down_edge * (mirrored - group)}
    column = blk % half

    def inner_dev(step, turned=False):
        return {"blk": (blk + 2 * blocks + step) % blocks, "group": mirrored if turned else group}

    across_dev = inner_dev(half, True)
    wrap_dev = inner_dev((half - 1) * (down_edge - up_edge))
    other_dev = {"blk": blk, "group": other}

    def chip(position):
        return {"blk": blk, "group": (position + CHIPS) % CHIPS * 2 + core}

    def remote(src, dst, send, recv, device):
        return pltpu.make_async_remote_copy(
            src_ref=src, dst_ref=dst, send_sem=send, recv_sem=recv, device_id=device, device_id_type=MESH
        )

    is_end = (y == 0) | (y == CHIPS - 1)
    is_middle = (y == 1) | (y == 2)
    relayed_up = is_middle & (up_edge == 1)
    relayed_down = is_middle & (down_edge == 1)
    relayed = is_middle & (up_edge + down_edge == 1)
    in_column = {offset: is_middle & (column == offset) for offset in (7, 8, 15, 16, 23, 24)}
    is_first = blk % LINE == 0
    is_last = blk % LINE == LINE - 1
    not_first = jnp.logical_not(is_first)
    not_last = jnp.logical_not(is_last)

    loads = [
        pltpu.make_async_copy(captions_hbm, captions, load_sem.at[0]),
        pltpu.make_async_copy(images_hbm, images, load_sem.at[1]),
        pltpu.make_async_copy(labels_hbm, labs.at[y], load_sem.at[2]),
    ]
    for load in loads:
        load.start()

    barrier = pltpu.get_barrier_semaphore()

    def greet(device):
        pl.semaphore_signal(barrier, inc=1, device_id=device, device_id_type=MESH)

    for device in [other_dev] + [chip(y + d) for d in (1, 2, 3)]:
        greet(device)

    @pl.when(not_last)
    def _():
        greet(up_dev)

    @pl.when(is_first)
    def _():
        greet(down_dev)

    @pl.when(relayed_down)
    def _():
        greet(wrap_dev)
        for offset in CAPTIONS_UP_VIA:
            greet(inner_dev(offset - half, True))
        greet(inner_dev(SUMS_DOWN_VIA[0]))
        for offset, _, _ in CAPTIONS_VIA:
            greet(inner_dev(offset))
        for offset, _, _ in SUMS_UP_VIA:
            greet(inner_dev(-offset - 1, True))

    for offset in CAPTIONS_UP_VIA:

        @pl.when(in_column[offset])
        def _():
            greet(inner_dev(half - 1 - offset))
            greet(inner_dev(half - offset, True))

    @pl.when(relayed_up)
    def _():
        greet(across_dev)
        greet(inner_dev(SUMS_DOWN_VIA[0] + 1 - blocks, True))
        for offset, _, _ in SUMS_UP_VIA:
            greet(inner_dev(-offset))

    for offset, _, _ in CAPTIONS_VIA:

        @pl.when(in_column[offset])
        def _():
            greet(inner_dev(-offset))
            greet(inner_dev(-offset - 1, True))

    for offset, _, _ in SUMS_UP_VIA:

        @pl.when(in_column[half - 1 - offset])
        def _():
            greet(inner_dev(offset))

    @pl.when(in_column[SUMS_DOWN_VIA[0]])
    def _():
        greet(inner_dev(blocks - 1 - SUMS_DOWN_VIA[0], True))

    loads[0].wait()
    text_float, _ = unit_rows(captions[...])
    texts[0:rows, :] = text_float.astype(BF16)
    loads[1].wait()
    image_float, _ = unit_rows(images[...])
    imgs[y] = image_float.astype(BF16)
    loads[2].wait()

    inner = (y * (3 - y)) // 2
    peers = 4 + jnp.where(is_first, 0, 1) + jnp.where(is_last, 1, 0)
    inner_peers = 11 * up_edge + 5 * down_edge
    for offset, count in ((24, 1), (8, 2), (16, 2), (7, 2), (15, 2), (23, 4)):
        inner_peers = inner_peers + jnp.where(column == offset, count, 0)
    peers = peers + inner * inner_peers
    pl.semaphore_wait(barrier, peers)

    def answer(index, device):
        pl.semaphore_signal(ready.at[index], inc=1, device_id=device, device_id_type=MESH)

    @pl.when(not_first)
    def _():
        answer(0, down_dev)

    @pl.when(is_last)
    def _():
        answer(1, up_dev)

    @pl.when(relayed & is_last)
    def _():
        for offset, _, _ in CAPTIONS_VIA:
            answer(2, inner_dev(offset + 1, True))
        answer(4, wrap_dev)

    @pl.when(in_column[SUMS_DOWN_VIA[0]])
    def _():
        answer(3, inner_dev(-SUMS_DOWN_VIA[0]))

    def own_copy(c, direction):
        part = imgs.at[y, pl.ds(c * ag_rows, ag_rows)]
        return remote(
            part, part, ag_own_send.at[direction, c], ag_recv.at[y, c], chip(y + 1 - 2 * direction)
        )

    def fwd_copy(s, c):
        part = imgs.at[s, pl.ds(c * ag_rows, ag_rows)]
        target = jnp.where(s < y, y + 1, y - 1)
        return remote(part, part, ag_fwd_send.at[s, c], ag_recv.at[s, c], chip(target))

    def slot(i):
        return texts.at[pl.ds(i * rows, rows)]

    def flow(kind, c):
        if kind == 0:
            offset = CAPTIONS_UP_VIA[c]
            begin, size, source = c * 64, 64, slot(0)
            near_dev, far_dev = inner_dev(offset + 1 - half), inner_dev(half - offset, True)
            target, base, sem, sends, passes = texts, 2 * rows, next_recv.at[0], relayed_up, in_column[offset]
        elif kind == 1:
            offset, begin, size = CAPTIONS_VIA[c]
            source, near_dev, far_dev = slot(0), inner_dev(offset), inner_dev(-offset - 1, True)
            target, base, sem, sends, passes = texts, 4 * rows, next_recv.at[1], relayed_down, in_column[offset]
        elif kind == 2:
            offset, begin, size = SUMS_UP_VIA[c]
            source = back_out.at[1]
            near_dev, far_dev = inner_dev(-offset), inner_dev(offset + 1, True)
            target, base, sem = back_in.at[0], 0, back_recv.at[0]
            sends, passes = relayed_up, in_column[half - 1 - offset]
        else:
            offset = SUMS_DOWN_VIA[c]
            begin, size, source = c * 64, 64, back_out.at[0]
            near_dev, far_dev = inner_dev(offset), inner_dev(blocks - 1 - offset, True)
            target, base, sem = back_in.at[1], 0, back_recv.at[1]
            sends, passes = relayed_down, in_column[offset] if c == 0 else relayed_up
        held = relay_in.at[kind, pl.ds(begin, size)]
        first = remote(
            source.at[pl.ds(begin, size)], held, relay_src_send.at[kind, c], relay_recv.at[kind, c], near_dev
        )
        second = remote(
            held, target.at[pl.ds(base + begin, size)], relay_fwd_send.at[kind, c], sem, far_dev
        )
        return first, second, sends, passes

    flow_parts = [(0, 0), (0, 1), (1, 0), (1, 1), (1, 2), (2, 0), (2, 1), (2, 2), (3, 0), (3, 1)]

    def send_flow(kind, c):
        first, _, sends, _ = flow(kind, c)

        @pl.when(sends)
        def _():
            first.start()

    def pass_flow(kind, c):
        first, second, _, passes = flow(kind, c)

        @pl.when(passes)
        def _():
            first.wait_recv()
            second.start()

    next_up = remote(slot(0), slot(2), next_send.at[0], next_recv.at[0], up_dev)
    next_down = remote(slot(0), slot(4), next_send.at[1], next_recv.at[1], down_dev)
    core_copies = [
        remote(slot(2 * i), slot(2 * i + 1), core_send.at[i], core_recv.at[i], other_dev) for i in range(3)
    ]
    lab_copies = [
        remote(labs.at[y], labs.at[y], lab_send.at[d - 1], lab_recv.at[y], chip(y + d)) for d in (1, 2, 3)
    ]

    for kind, c in flow_parts[:5]:
        send_flow(kind, c)

    for c in range(AG_CHUNKS):

        @pl.when(y < CHIPS - 1)
        def _():
            own_copy(c, 0).start()

        @pl.when(y > 0)
        def _():
            own_copy(c, 1).start()

    core_copies[0].start()

    @pl.when(not_first)
    def _():
        next_down.start()

    for copy in lab_copies:
        copy.start()

    @pl.when(not_last)
    def _():
        pl.semaphore_wait(ready.at[0], 1)

    @pl.when(jnp.logical_not(relayed_up))
    def _():
        next_up.start()

    parts[...] = jnp.zeros_like(parts)
    sums[...] = jnp.zeros_like(sums)
    loss_part[...] = jnp.zeros_like(loss_part)

    near = jnp.where(y == 0, 1, jnp.where(y == 1, 0, jnp.where(y == 2, 3, 2)))
    next_near = jnp.where(y == 0, 2, jnp.where(y == 1, 2, 1))
    far = jnp.where(y < 2, 3, 0)

    def take(s, c):
        copy = fwd_copy(s, c)
        copy.wait_recv()

        @pl.when(is_middle)
        def _():
            copy.start()

    def take_labels(s):
        remote(labs.at[s], labs.at[s], lab_send.at[0], lab_recv.at[s], chip(y + 1)).wait_recv()

    scale = scale_ref[0]
    bias = bias_ref[0]

    def compute(s, i):
        image = imgs[s]
        where = pl.ds(pl.multiple_of(2 * i * rows, 2 * rows), 2 * rows)
        text = texts[where, :]
        raw = depth_part(text, image, 0, 512) + depth_part(text, image, 512, text.shape[1])
        label = labs[s]
        mine = label - group * rows
        theirs = label - other * rows
        theirs = jnp.where((theirs >= 0) & (theirs < rows), theirs + rows, -1)
        place = jnp.where((mine >= 0) & (mine < rows), mine, theirs)
        place = jnp.where(i == 0, place, -1)
        positive = lax.broadcasted_iota(jnp.int32, raw.shape, 0) == place
        loss, weights = pair_weights(raw, positive, scale, bias)
        sums[where, :] += jnp.dot(weights, image, preferred_element_type=F32)
        parts[s] += lax.dot_general(weights, text, (((0,), (0,)), ((), ())), preferred_element_type=F32)
        loss_part[s] += loss

    def end_copy(t, c):
        where = pl.ds(c * rs_rows, rs_rows)
        return remote(
            parts_out.at[t, where],
            end_in.at[t, where],
            end_send.at[t, c],
            end_recv.at[t, c],
            chip(1 + y // (CHIPS - 1)),
        )

    def mid_copy(t, c):
        where = pl.ds(c * rs_rows, rs_rows)
        sender = (y + 1) % 2
        return remote(
            parts_out.at[t, where], mid_in.at[sender, where], mid_send.at[t, c], mid_recv.at[sender, c], chip(t)
        )

    def sum_copy(i):
        return remote(sums_out.at[i], sums_in.at[i], sum_send.at[i], sum_recv.at[i], other_dev)

    def finish(i):
        sum_copy(i).wait_recv()
        total = sums[2 * i * rows : (2 * i + 1) * rows, :] + sums_in[i].astype(F32)
        back_out[i - 1] = total.astype(BF16)
        direct = back_down if i == 1 else back_up
        edge = relayed_down if i == 1 else relayed_up

        @pl.when(jnp.logical_not(edge))
        def _():
            direct.start()

        if i == 1:

            @pl.when(edge)
            def _():
                pl.semaphore_wait(ready.at[3], 1)
                pl.semaphore_wait(ready.at[4], 1)

        for c in range(1 + i):
            send_flow(4 - i, c)

    back_down = remote(back_out.at[0], back_in.at[1], back_send.at[0], back_recv.at[1], down_dev)
    back_up = remote(back_out.at[1], back_in.at[0], back_send.at[1], back_recv.at[0], up_dev)

    first_ends = is_first & is_end
    end_step = jnp.where(is_end, 1, 0)

    def chosen(u, usual, first, first_end, late):
        value = usual[0]
        for k in range(len(usual)):
            value = jnp.where(u == k, jnp.where(is_first, first[k], usual[k]), value)
            value = jnp.where((u == k) & relayed_up, late[k], value)
            value = jnp.where((u == k) & first_ends, first_end[k], value)
        return value

    usual_order = [y, near, near, near, y, y, next_near, next_near, next_near, far, far, far]
    late_order = [y, near, near, y, next_near, next_near, near, y, next_near, far, far, far]
    first_end_order = [y, near, near, y, next_near, next_near, next_near, far, far, far, near, y]
    first_order = [y, near, near, y, next_near, next_near, far, far, far, next_near, near, y]

    def step(u, carry):
        s = chosen(u, usual_order, first_order, first_end_order, late_order)
        i = chosen(u, [0, 0, 1, 2, 1, 2, 0, 1, 2, 2, 1, 0], [0, 0, 2, 2, 0, 2, 2, 0, 1, 1, 1, 1], [0, 0, 2, 2, 0, 2, 1, 2, 0, 1, 1, 1], [0, 0, 1, 1, 0, 1, 2, 2, 2, 2, 1, 0])

        @pl.when(u == 0)
        def _():
            core_copies[0].wait_recv()

        @pl.when((u == 1) & is_middle)
        def _():
            for c in range(AG_CHUNKS):
                take(near, c)
                take(next_near, c)

        @pl.when((u == 1) & is_end)
        def _():
            for c in range(AG_CHUNKS):
                take(near, c)

        @pl.when(u == 1)
        def _():
            for other_slot in (near, next_near, far):
                take_labels(other_slot)

        @pl.when((u == 2) & is_first)
        def _():
            pl.semaphore_wait(ready.at[1], 1)

        @pl.when((u == 2) & is_first & jnp.logical_not(relayed_down))
        def _():
            next_down.start()

        @pl.when((u == 2) & (in_column[8] | in_column[16] | in_column[24]))
        def _():
            pl.semaphore_wait(ready.at[2], 1)
            for c in range(3):
                pass_flow(1, c)

        @pl.when((u == 2) & is_first)
        def _():
            next_down.wait_recv()
            core_copies[2].start()

        @pl.when((u == 2) & not_first)
        def _():
            next_up.wait_recv()
            core_copies[1].start()

        @pl.when((u == 2) & is_middle)
        def _():
            take(far, 0)

        @pl.when((u == 2) & is_first)
        def _():
            core_copies[2].wait_recv()

        @pl.when((u == jnp.where(relayed_up, 6, 2)) & not_first)
        def _():
            next_down.wait_recv()
            core_copies[2].start()

        @pl.when((u == 2) & not_first)
        def _():
            core_copies[1].wait_recv()

        @pl.when((u == jnp.where(relayed_up, 6, 3)) & not_first)
        def _():
            core_copies[2].wait_recv()

        @pl.when((u == 4) & is_middle)
        def _():
            for c in range(1, AG_CHUNKS):
                take(far, c)

        @pl.when((u == jnp.where(is_first, 4, 6)) & is_end)
        def _():
            for c in range(AG_CHUNKS):
                take(next_near, c)

        @pl.when((u == jnp.where(is_first, 7, 9)) & is_end)
        def _():
            for c in range(AG_CHUNKS):
                take(far, c)

        @pl.when((u == 5) & (in_column[8] | in_column[16]))
        def _():
            pass_flow(0, 0)
            pass_flow(0, 1)

        @pl.when((u == jnp.where(is_end, 6, 8)) & is_first)
        def _():
            next_up.wait_recv()
            core_copies[1].start()
            core_copies[1].wait_recv()

        @pl.when((u == jnp.where(is_end, 11, 9)) & is_first)
        def _():
            finish(2)

        compute(s, i)

        @pl.when((u == jnp.where(is_first, 10, 9)) & is_middle)
        def _():
            parts_out[near] = parts[near].astype(BF16)
            for c in range(RS_CHUNKS):
                mid_copy(near, c).start()

        @pl.when(jnp.where(is_first, (u == 6 + end_step) | (u == 7 + end_step) | (u == 11), u > 8))
        def _():
            start = pl.multiple_of((2 * i + 1) * rows, rows)
            sums_out[i] = sums[pl.ds(start, rows), :].astype(BF16)
            sum_copy(i).start()

        @pl.when(jnp.where(is_first, (u == 6) | (u == 9) | (u == 10), (u == 3) | (u == 8) | (u == 11)) & is_end)
        def _():
            parts_out[s] = parts[s].astype(BF16)
            for c in range(RS_CHUNKS):
                end_copy(s, c).start()

        return carry

    lax.fori_loop(0, 3 * CHIPS, step, 0)

    @pl.when(not_first)
    def _():
        finish(2)

    @pl.when(jnp.logical_not(is_first & is_middle))
    def _():
        finish(1)

    loss_copies = [
        remote(
            loss_part.at[(y + d) % CHIPS], loss_in.at[y], loss_send.at[d - 1], loss_recv.at[y], chip(y + d)
        )
        for d in (1, 2, 3)
    ]
    for copy in loss_copies:
        copy.start()

    def pass_on(t, c):
        where = pl.ds(pl.multiple_of(c * rs_rows, rs_rows), rs_rows)
        end_copy(t, c).wait_recv()
        total = parts[t, where, :] + end_in[t, where, :].astype(F32)
        parts_out[t, where, :] = total.astype(BF16)
        mid_copy(t, c).start()

    @pl.when(is_middle)
    def _():
        def pass_all(k, carry):
            pass_on(jnp.where(k < RS_CHUNKS, next_near, far), k % RS_CHUNKS)

            @pl.when(is_first & (k == RS_CHUNKS - 1))
            def _():
                finish(1)

            @pl.when((in_column[7] | in_column[15] | in_column[23]) & (k == 1))
            def _():
                for c in range(3):
                    pass_flow(2, c)

            @pl.when(in_column[23] & (k == RS_CHUNKS + RS_CHUNKS // 2))
            def _():
                pass_flow(3, 0)

            return carry

        lax.fori_loop(0, 2 * RS_CHUNKS, pass_all, 0)

    pass_flow(3, 1)

    sum_copy(0).wait_recv()
    text_sums = sums[0:rows, :] + sums_in[0].astype(F32)
    back_down.wait_recv()
    text_sums = text_sums + back_in[1].astype(F32)
    back_up.wait_recv()
    text_sums = text_sums + back_in[0].astype(F32)
    text_float, text_length = unit_rows(captions[...])
    text_out[...] = through_norm(text_sums, text_float, text_length).astype(BF16)

    loss_total = loss_part[y]
    for d in (1, 2, 3):
        s = (y + d) % CHIPS
        remote(loss_part.at[s], loss_in.at[s], loss_send.at[0], loss_recv.at[s], chip(y + 1)).wait_recv()
        loss_total = loss_total + loss_in[s]
    loss_out[...] = loss_total

    for sender in (0, 1):

        @pl.when(y != sender + 1)
        def _():
            for c in range(RS_CHUNKS):
                where = pl.ds(c * rs_rows, rs_rows)
                part = mid_in.at[sender, where]
                remote(part, part, mid_send.at[0, c], mid_recv.at[sender, c], chip(y + 1)).wait_recv()
            parts[y] += mid_in[sender].astype(F32)

    @pl.when(is_middle)
    def _():
        for c in range(RS_CHUNKS):
            end_copy(y, c).wait_recv()
        parts[y] += end_in[y].astype(F32)

    image_float, image_length = unit_rows(images[...])
    image_out[...] = through_norm(parts[y], image_float, image_length).astype(BF16)

    for c in range(AG_CHUNKS):

        @pl.when(y < CHIPS - 1)
        def _():
            own_copy(c, 0).wait_send()

        @pl.when(y > 0)
        def _():
            own_copy(c, 1).wait_send()

    def line_sent(d, carry):
        s = (y + d) % CHIPS

        @pl.when(is_middle)
        def _():
            for c in range(AG_CHUNKS):
                fwd_copy(s, c).wait_send()
            for c in range(RS_CHUNKS):
                mid_copy(s, c).wait_send()

        @pl.when(is_end)
        def _():
            for c in range(RS_CHUNKS):
                end_copy(s, c).wait_send()

        return carry

    lax.fori_loop(1, CHIPS, line_sent, 0)

    @pl.when(jnp.logical_not(relayed_up))
    def _():
        next_up.wait_send()
        back_up.wait_send()

    @pl.when(jnp.logical_not(relayed_down))
    def _():
        next_down.wait_send()
        back_down.wait_send()

    for kind, c in flow_parts:
        first, second, sends, passes = flow(kind, c)
        pl.when(sends)(first.wait_send)
        pl.when(passes)(second.wait_send)

    for copy in core_copies + lab_copies + loss_copies + [sum_copy(i) for i in range(3)]:
        copy.wait_send()


def per_device(blocks, images, captions, labels, logit_scale, logit_bias):
    rows, width = images.shape
    vmem = pl.BlockSpec(memory_space=pltpu.VMEM)
    smem = pl.BlockSpec(memory_space=pltpu.SMEM)
    hbm = pl.BlockSpec(memory_space=pl.ANY)
    dma = pltpu.SemaphoreType.DMA
    loss, image_grad, text_grad = pl.pallas_call(
        functools.partial(kernel, blocks),
        out_shape=[
            jax.ShapeDtypeStruct((1, rows), F32),
            jax.ShapeDtypeStruct((rows, width), BF16),
            jax.ShapeDtypeStruct((rows, width), BF16),
        ],
        in_specs=[hbm, hbm, hbm, smem, smem],
        out_specs=[vmem, vmem, vmem],
        scratch_shapes=[
            pltpu.VMEM((rows, width), BF16),
            pltpu.VMEM((rows, width), BF16),
            pltpu.VMEM((CHIPS, rows, width), BF16),
            pltpu.VMEM((6 * rows, width), BF16),
            pltpu.VMEM((CHIPS, 1, rows), jnp.int32),
            pltpu.VMEM((CHIPS, 1, rows), F32),
            pltpu.VMEM((CHIPS, 1, rows), F32),
            pltpu.VMEM((CHIPS, rows, width), F32),
            pltpu.VMEM((CHIPS, rows, width), BF16),
            pltpu.VMEM((CHIPS, rows, width), BF16),
            pltpu.VMEM((2, rows, width), BF16),
            pltpu.VMEM((6 * rows, width), F32),
            pltpu.VMEM((3, rows, width), BF16),
            pltpu.VMEM((3, rows, width), BF16),
            pltpu.VMEM((2, rows, width), BF16),
            pltpu.VMEM((2, rows, width), BF16),
            pltpu.VMEM((4, rows, width), BF16),
            dma((3,)),
            dma((2, AG_CHUNKS)),
            dma((CHIPS, AG_CHUNKS)),
            dma((CHIPS, AG_CHUNKS)),
            dma((3,)),
            dma((CHIPS,)),
            dma((3,)),
            dma((CHIPS,)),
            dma((3,)),
            dma((3,)),
            dma((2,)),
            dma((2,)),
            dma((CHIPS, RS_CHUNKS)),
            dma((CHIPS, RS_CHUNKS)),
            dma((CHIPS, RS_CHUNKS)),
            dma((2, RS_CHUNKS)),
            dma((3,)),
            dma((3,)),
            dma((2,)),
            dma((2,)),
            dma((4, 3)),
            dma((4, 3)),
            dma((4, 3)),
            pltpu.SemaphoreType.REGULAR((5,)),
        ],
        compiler_params=pltpu.CompilerParams(
            collective_id=0, has_side_effects=True, vmem_limit_bytes=60 * 1024 * 1024
        ),
    )(images, captions, labels.reshape(1, rows), logit_scale, logit_bias)
    return (loss.reshape(rows), image_grad.astype(F32), text_grad.astype(F32))


def solution(mesh):
    body = functools.partial(per_device, mesh.shape["blk"])
    in_specs = (P(("blk", "group"), None), P(("blk", "group"), None), P(("blk", "group")), P(), P())
    out_specs = (P(("blk", "group")), P(("blk", "group"), None), P(("blk", "group"), None))
    return jax.shard_map(body, mesh=mesh, in_specs=in_specs, out_specs=out_specs, check_vma=False)
```

```python
import functools

import jax
import jax.numpy as jnp
from jax import lax
from jax.experimental import pallas as pl
from jax.experimental.pallas import tpu as pltpu
from jax.sharding import PartitionSpec as P

EPSILON = 1e-06
CHIPS = 4
LINE = 8
CAPTIONS_VIA = ((24, 0, 48), (8, 48, 48), (16, 96, 32))
CAPTIONS_UP_VIA = (8, 16)
SUMS_UP_VIA = ((24, 0, 48), (16, 48, 48), (8, 96, 32))
SUMS_DOWN_VIA = (23, 31)
AG_CHUNKS = 2
RS_CHUNKS = 4
MESH = pl.DeviceIdType.MESH
F32 = jnp.float32
BF16 = jnp.bfloat16


def unit_rows(values):
    wide = values.astype(F32)
    length = jnp.sqrt(jnp.sum(wide * wide, axis=-1, keepdims=True) + EPSILON)
    return (wide / length, length)


def through_norm(sums, unit_float, length):
    return (sums - unit_float * jnp.sum(unit_float * sums, axis=-1, keepdims=True)) / length


def depth_part(a, b, start, stop):
    return lax.dot_general(
        a[:, start:stop], b[:, start:stop], (((1,), (1,)), ((), ())), preferred_element_type=F32
    )


def summed_log(decay):
    pieces = [decay[i : i + 8, :] for i in range(0, decay.shape[0], 8)]
    while len(pieces) > 1:
        pieces = [a + b + a * b for a, b in zip(pieces[::2], pieces[1::2])]
    return jnp.sum(jnp.log1p(pieces[0]), axis=0, keepdims=True)


def pair_weights(raw, positive, scale, bias):
    logits = scale * raw + bias
    turned = jnp.where(positive, -logits, logits)
    decay = jnp.exp(-jnp.abs(turned))
    loss = jnp.sum(jnp.maximum(turned, 0.0), axis=0, keepdims=True) + summed_log(decay)
    share = jnp.where(turned >= 0, 1.0, decay) / (1.0 + decay)
    weights = jnp.where(positive, -scale, scale) * share
    return (loss, weights.astype(BF16))


def kernel(
    blocks,
    images_hbm,
    captions_hbm,
    labels_hbm,
    scale_ref,
    bias_ref,
    loss_out,
    image_out,
    text_out,
    images,
    captions,
    imgs,
    texts,
    labs,
    loss_part,
    loss_in,
    parts,
    parts_out,
    end_in,
    mid_in,
    sums,
    sums_out,
    sums_in,
    back_out,
    back_in,
    relay_in,
    load_sem,
    ag_own_send,
    ag_fwd_send,
    ag_recv,
    lab_send,
    lab_recv,
    loss_send,
    loss_recv,
    core_send,
    core_recv,
    next_send,
    next_recv,
    end_send,
    end_recv,
    mid_send,
    mid_recv,
    sum_send,
    sum_recv,
    back_send,
    back_recv,
    relay_src_send,
    relay_recv,
    relay_fwd_send,
    ready,
):
    rows = images.shape[0]
    ag_rows = rows // AG_CHUNKS
    rs_rows = rows // RS_CHUNKS
    blk = lax.axis_index("blk")
    group = lax.axis_index("group")
    y = group // 2
    core = group % 2
    other = group + 1 - 2 * core
    half = blocks // 2
    mirrored = 2 * (CHIPS - 1 - y) + core
    up_edge = (blk % half) // (half - 1)
    down_edge = (half - 1 - blk % half) // (half - 1)
    up_dev = {"blk": (blk + 1) % blocks, "group": group + up_edge * (mirrored - group)}
    down_dev = {"blk": (blk + blocks - 1) % blocks, "group": group + down_edge * (mirrored - group)}
    column = blk % half

    def inner_dev(step, turned=False):
        return {"blk": (blk + 2 * blocks + step) % blocks, "group": mirrored if turned else group}

    across_dev = inner_dev(half, True)
    wrap_dev = inner_dev((half - 1) * (down_edge - up_edge))
    other_dev = {"blk": blk, "group": other}

    def chip(position):
        return {"blk": blk, "group": (position + CHIPS) % CHIPS * 2 + core}

    def remote(src, dst, send, recv, device):
        return pltpu.make_async_remote_copy(
            src_ref=src, dst_ref=dst, send_sem=send, recv_sem=recv, device_id=device, device_id_type=MESH
        )

    is_end = (y == 0) | (y == CHIPS - 1)
    is_middle = (y == 1) | (y == 2)
    relayed_up = is_middle & (up_edge == 1)
    relayed_down = is_middle & (down_edge == 1)
    relayed = is_middle & (up_edge + down_edge == 1)
    in_column = {offset: is_middle & (column == offset) for offset in (7, 8, 15, 16, 23, 24)}
    is_first = blk % LINE == 0
    is_last = blk % LINE == LINE - 1
    not_first = jnp.logical_not(is_first)
    not_last = jnp.logical_not(is_last)

    loads = [
        pltpu.make_async_copy(captions_hbm, captions, load_sem.at[0]),
        pltpu.make_async_copy(images_hbm, images, load_sem.at[1]),
        pltpu.make_async_copy(labels_hbm, labs.at[y], load_sem.at[2]),
    ]
    for load in loads:
        load.start()

    barrier = pltpu.get_barrier_semaphore()

    def greet(device):
        pl.semaphore_signal(barrier, inc=1, device_id=device, device_id_type=MESH)

    for device in [other_dev] + [chip(y + d) for d in (1, 2, 3)]:
        greet(device)

    @pl.when(not_last)
    def _():
        greet(up_dev)

    @pl.when(is_first)
    def _():
        greet(down_dev)

    @pl.when(relayed_down)
    def _():
        greet(wrap_dev)
        for offset in CAPTIONS_UP_VIA:
            greet(inner_dev(offset - half, True))
        greet(inner_dev(SUMS_DOWN_VIA[0]))
        for offset, _, _ in CAPTIONS_VIA:
            greet(inner_dev(offset))
        for offset, _, _ in SUMS_UP_VIA:
            greet(inner_dev(-offset - 1, True))

    for offset in CAPTIONS_UP_VIA:

        @pl.when(in_column[offset])
        def _():
            greet(inner_dev(half - 1 - offset))
            greet(inner_dev(half - offset, True))

    @pl.when(relayed_up)
    def _():
        greet(across_dev)
        greet(inner_dev(SUMS_DOWN_VIA[0] + 1 - blocks, True))
        for offset, _, _ in SUMS_UP_VIA:
            greet(inner_dev(-offset))

    for offset, _, _ in CAPTIONS_VIA:

        @pl.when(in_column[offset])
        def _():
            greet(inner_dev(-offset))
            greet(inner_dev(-offset - 1, True))

    for offset, _, _ in SUMS_UP_VIA:

        @pl.when(in_column[half - 1 - offset])
        def _():
            greet(inner_dev(offset))

    @pl.when(in_column[SUMS_DOWN_VIA[0]])
    def _():
        greet(inner_dev(blocks - 1 - SUMS_DOWN_VIA[0], True))

    loads[0].wait()
    text_float, _ = unit_rows(captions[...])
    texts[0:rows, :] = text_float.astype(BF16)
    loads[1].wait()
    image_float, _ = unit_rows(images[...])
    imgs[y] = image_float.astype(BF16)
    loads[2].wait()

    inner = (y * (3 - y)) // 2
    peers = 4 + jnp.where(is_first, 0, 1) + jnp.where(is_last, 1, 0)
    inner_peers = 11 * up_edge + 5 * down_edge
    for offset, count in ((24, 1), (8, 2), (16, 2), (7, 2), (15, 2), (23, 4)):
        inner_peers = inner_peers + jnp.where(column == offset, count, 0)
    peers = peers + inner * inner_peers
    pl.semaphore_wait(barrier, peers)

    def answer(index, device):
        pl.semaphore_signal(ready.at[index], inc=1, device_id=device, device_id_type=MESH)

    @pl.when(not_first)
    def _():
        answer(0, down_dev)

    @pl.when(is_last)
    def _():
        answer(1, up_dev)

    @pl.when(relayed & is_last)
    def _():
        for offset, _, _ in CAPTIONS_VIA:
            answer(2, inner_dev(offset + 1, True))
        answer(4, wrap_dev)

    @pl.when(in_column[SUMS_DOWN_VIA[0]])
    def _():
        answer(3, inner_dev(-SUMS_DOWN_VIA[0]))

    def own_copy(c, direction):
        part = imgs.at[y, pl.ds(c * ag_rows, ag_rows)]
        return remote(
            part, part, ag_own_send.at[direction, c], ag_recv.at[y, c], chip(y + 1 - 2 * direction)
        )

    def fwd_copy(s, c):
        part = imgs.at[s, pl.ds(c * ag_rows, ag_rows)]
        target = jnp.where(s < y, y + 1, y - 1)
        return remote(part, part, ag_fwd_send.at[s, c], ag_recv.at[s, c], chip(target))

    def slot(i):
        return texts.at[pl.ds(i * rows, rows)]

    def flow(kind, c):
        if kind == 0:
            offset = CAPTIONS_UP_VIA[c]
            begin, size, source = c * 64, 64, slot(0)
            near_dev, far_dev = inner_dev(offset + 1 - half), inner_dev(half - offset, True)
            target, base, sem, sends, passes = texts, 2 * rows, next_recv.at[0], relayed_up, in_column[offset]
        elif kind == 1:
            offset, begin, size = CAPTIONS_VIA[c]
            source, near_dev, far_dev = slot(0), inner_dev(offset), inner_dev(-offset - 1, True)
            target, base, sem, sends, passes = texts, 4 * rows, next_recv.at[1], relayed_down, in_column[offset]
        elif kind == 2:
            offset, begin, size = SUMS_UP_VIA[c]
            source = back_out.at[1]
            near_dev, far_dev = inner_dev(-offset), inner_dev(offset + 1, True)
            target, base, sem = back_in.at[0], 0, back_recv.at[0]
            sends, passes = relayed_up, in_column[half - 1 - offset]
        else:
            offset = SUMS_DOWN_VIA[c]
            begin, size, source = c * 64, 64, back_out.at[0]
            near_dev, far_dev = inner_dev(offset), inner_dev(blocks - 1 - offset, True)
            target, base, sem = back_in.at[1], 0, back_recv.at[1]
            sends, passes = relayed_down, in_column[offset] if c == 0 else relayed_up
        held = relay_in.at[kind, pl.ds(begin, size)]
        first = remote(
            source.at[pl.ds(begin, size)], held, relay_src_send.at[kind, c], relay_recv.at[kind, c], near_dev
        )
        second = remote(
            held, target.at[pl.ds(base + begin, size)], relay_fwd_send.at[kind, c], sem, far_dev
        )
        return first, second, sends, passes

    flow_parts = [(0, 0), (0, 1), (1, 0), (1, 1), (1, 2), (2, 0), (2, 1), (2, 2), (3, 0), (3, 1)]

    def send_flow(kind, c):
        first, _, sends, _ = flow(kind, c)

        @pl.when(sends)
        def _():
            first.start()

    def pass_flow(kind, c):
        first, second, _, passes = flow(kind, c)

        @pl.when(passes)
        def _():
            first.wait_recv()
            second.start()

    next_up = remote(slot(0), slot(2), next_send.at[0], next_recv.at[0], up_dev)
    next_down = remote(slot(0), slot(4), next_send.at[1], next_recv.at[1], down_dev)
    core_copies = [
        remote(slot(2 * i), slot(2 * i + 1), core_send.at[i], core_recv.at[i], other_dev) for i in range(3)
    ]
    lab_copies = [
        remote(labs.at[y], labs.at[y], lab_send.at[d - 1], lab_recv.at[y], chip(y + d)) for d in (1, 2, 3)
    ]

    for kind, c in flow_parts[:5]:
        send_flow(kind, c)

    for c in range(AG_CHUNKS):

        @pl.when(y < CHIPS - 1)
        def _():
            own_copy(c, 0).start()

        @pl.when(y > 0)
        def _():
            own_copy(c, 1).start()

    core_copies[0].start()

    @pl.when(not_first)
    def _():
        next_down.start()

    for copy in lab_copies:
        copy.start()

    @pl.when(not_last)
    def _():
        pl.semaphore_wait(ready.at[0], 1)

    @pl.when(jnp.logical_not(relayed_up))
    def _():
        next_up.start()

    parts[...] = jnp.zeros_like(parts)
    sums[...] = jnp.zeros_like(sums)
    loss_part[...] = jnp.zeros_like(loss_part)

    near = jnp.where(y == 0, 1, jnp.where(y == 1, 0, jnp.where(y == 2, 3, 2)))
    next_near = jnp.where(y == 0, 2, jnp.where(y == 1, 2, 1))
    far = jnp.where(y < 2, 3, 0)

    def take(s, c):
        copy = fwd_copy(s, c)
        copy.wait_recv()

        @pl.when(is_middle)
        def _():
            copy.start()

    def take_labels(s):
        remote(labs.at[s], labs.at[s], lab_send.at[0], lab_recv.at[s], chip(y + 1)).wait_recv()

    scale = scale_ref[0]
    bias = bias_ref[0]

    def compute(s, i):
        image = imgs[s]
        where = pl.ds(pl.multiple_of(2 * i * rows, 2 * rows), 2 * rows)
        text = texts[where, :]
        raw = depth_part(text, image, 0, 512) + depth_part(text, image, 512, text.shape[1])
        label = labs[s]
        mine = label - group * rows
        theirs = label - other * rows
        theirs = jnp.where((theirs >= 0) & (theirs < rows), theirs + rows, -1)
        place = jnp.where((mine >= 0) & (mine < rows), mine, theirs)
        place = jnp.where(i == 0, place, -1)
        positive = lax.broadcasted_iota(jnp.int32, raw.shape, 0) == place
        loss, weights = pair_weights(raw, positive, scale, bias)
        sums[where, :] += jnp.dot(weights, image, preferred_element_type=F32)
        parts[s] += lax.dot_general(weights, text, (((0,), (0,)), ((), ())), preferred_element_type=F32)
        loss_part[s] += loss

    def end_copy(t, c):
        where = pl.ds(c * rs_rows, rs_rows)
        return remote(
            parts_out.at[t, where],
            end_in.at[t, where],
            end_send.at[t, c],
            end_recv.at[t, c],
            chip(1 + y // (CHIPS - 1)),
        )

    def mid_copy(t, c):
        where = pl.ds(c * rs_rows, rs_rows)
        sender = (y + 1) % 2
        return remote(
            parts_out.at[t, where], mid_in.at[sender, where], mid_send.at[t, c], mid_recv.at[sender, c], chip(t)
        )

    def sum_copy(i):
        return remote(sums_out.at[i], sums_in.at[i], sum_send.at[i], sum_recv.at[i], other_dev)

    def finish(i):
        sum_copy(i).wait_recv()
        total = sums[2 * i * rows : (2 * i + 1) * rows, :] + sums_in[i].astype(F32)
        back_out[i - 1] = total.astype(BF16)
        direct = back_down if i == 1 else back_up
        edge = relayed_down if i == 1 else relayed_up

        @pl.when(jnp.logical_not(edge))
        def _():
            direct.start()

        if i == 1:

            @pl.when(edge)
            def _():
                pl.semaphore_wait(ready.at[3], 1)
                pl.semaphore_wait(ready.at[4], 1)

        for c in range(1 + i):
            send_flow(4 - i, c)

    back_down = remote(back_out.at[0], back_in.at[1], back_send.at[0], back_recv.at[1], down_dev)
    back_up = remote(back_out.at[1], back_in.at[0], back_send.at[1], back_recv.at[0], up_dev)

    first_ends = is_first & is_end
    end_step = jnp.where(is_end, 1, 0)

    def chosen(u, usual, first, first_end, late):
        value = usual[0]
        for k in range(len(usual)):
            value = jnp.where(u == k, jnp.where(is_first, first[k], usual[k]), value)
            value = jnp.where((u == k) & relayed_up, late[k], value)
            value = jnp.where((u == k) & first_ends, first_end[k], value)
        return value

    usual_order = [y, near, near, near, y, y, next_near, next_near, next_near, far, far, far]
    late_order = [y, near, near, y, next_near, next_near, near, y, next_near, far, far, far]
    first_end_order = [y, near, near, y, next_near, next_near, next_near, far, far, far, near, y]
    first_order = [y, near, near, y, next_near, next_near, far, far, next_near, far, near, y]

    def step(u, carry):
        s = chosen(u, usual_order, first_order, first_end_order, late_order)
        i = chosen(u, [0, 0, 1, 2, 1, 2, 0, 1, 2, 2, 1, 0], [0, 0, 2, 2, 0, 2, 2, 0, 1, 1, 1, 1], [0, 0, 2, 2, 0, 2, 1, 2, 0, 1, 1, 1], [0, 0, 1, 1, 0, 1, 2, 2, 2, 2, 1, 0])

        @pl.when(u == 0)
        def _():
            core_copies[0].wait_recv()

        @pl.when((u == 1) & is_middle)
        def _():
            for c in range(AG_CHUNKS):
                take(near, c)
                take(next_near, c)

        @pl.when((u == 1) & is_end)
        def _():
            for c in range(AG_CHUNKS):
                take(near, c)

        @pl.when(u == 1)
        def _():
            for other_slot in (near, next_near, far):
                take_labels(other_slot)

        @pl.when((u == 2) & is_first)
        def _():
            pl.semaphore_wait(ready.at[1], 1)

        @pl.when((u == 2) & is_first & jnp.logical_not(relayed_down))
        def _():
            next_down.start()

        @pl.when((u == 2) & (in_column[8] | in_column[16] | in_column[24]))
        def _():
            pl.semaphore_wait(ready.at[2], 1)
            for c in range(3):
                pass_flow(1, c)

        @pl.when((u == 2) & is_first)
        def _():
            next_down.wait_recv()
            core_copies[2].start()

        @pl.when((u == 2) & not_first)
        def _():
            next_up.wait_recv()
            core_copies[1].start()

        @pl.when((u == 2) & is_middle)
        def _():
            take(far, 0)

        @pl.when((u == 2) & is_first)
        def _():
            core_copies[2].wait_recv()

        @pl.when((u == jnp.where(relayed_up, 6, 2)) & not_first)
        def _():
            next_down.wait_recv()
            core_copies[2].start()

        @pl.when((u == 2) & not_first)
        def _():
            core_copies[1].wait_recv()

        @pl.when((u == jnp.where(relayed_up, 6, 3)) & not_first)
        def _():
            core_copies[2].wait_recv()

        @pl.when((u == 4) & (in_column[8] | in_column[16]))
        def _():
            pass_flow(0, 0)
            pass_flow(0, 1)

        @pl.when((u == 4) & is_middle)
        def _():
            for c in range(1, AG_CHUNKS):
                take(far, c)

        @pl.when((u == jnp.where(is_first, 4, 6)) & is_end)
        def _():
            for c in range(AG_CHUNKS):
                take(next_near, c)

        @pl.when((u == jnp.where(is_first, 7, 9)) & is_end)
        def _():
            for c in range(AG_CHUNKS):
                take(far, c)

        @pl.when((u == jnp.where(is_end, 6, 8)) & is_first)
        def _():
            next_up.wait_recv()
            core_copies[1].start()
            core_copies[1].wait_recv()

        @pl.when(((u == jnp.where(is_end, 11, 9)) & is_first) | ((u == 11) & relayed_up))
        def _():
            finish(2)

        compute(s, i)

        @pl.when((u == jnp.where(is_first, 10, 9)) & is_middle)
        def _():
            parts_out[near] = parts[near].astype(BF16)
            for c in range(RS_CHUNKS):
                mid_copy(near, c).start()

        @pl.when(jnp.where(is_first, (u == 6 + end_step) | (u == 7 + end_step) | (u == 11), u > 8))
        def _():
            start = pl.multiple_of((2 * i + 1) * rows, rows)
            sums_out[i] = sums[pl.ds(start, rows), :].astype(BF16)
            sum_copy(i).start()

        @pl.when(jnp.where(is_first, (u == 6) | (u == 9) | (u == 10), (u == 3) | (u == 8) | (u == 11)) & is_end)
        def _():
            parts_out[s] = parts[s].astype(BF16)
            for c in range(RS_CHUNKS):
                end_copy(s, c).start()

        return carry

    lax.fori_loop(0, 3 * CHIPS, step, 0)

    @pl.when(not_first & jnp.logical_not(relayed_up))
    def _():
        finish(2)

    @pl.when(jnp.logical_not(is_first & is_middle))
    def _():
        finish(1)

    loss_copies = [
        remote(
            loss_part.at[(y + d) % CHIPS], loss_in.at[y], loss_send.at[d - 1], loss_recv.at[y], chip(y + d)
        )
        for d in (1, 2, 3)
    ]
    for copy in loss_copies:
        copy.start()

    def pass_on(t, c):
        where = pl.ds(pl.multiple_of(c * rs_rows, rs_rows), rs_rows)
        end_copy(t, c).wait_recv()
        total = parts[t, where, :] + end_in[t, where, :].astype(F32)
        parts_out[t, where, :] = total.astype(BF16)
        mid_copy(t, c).start()

    @pl.when(is_middle)
    def _():
        for c in range(3):
            pass_flow(2, c)

        def pass_all(k, carry):
            pass_on(jnp.where(k < RS_CHUNKS, next_near, far), k % RS_CHUNKS)

            @pl.when(is_first & (k == RS_CHUNKS - 1))
            def _():
                finish(1)

            @pl.when(in_column[23] & (k == RS_CHUNKS + RS_CHUNKS // 2))
            def _():
                pass_flow(3, 0)

            return carry

        lax.fori_loop(0, 2 * RS_CHUNKS, pass_all, 0)

    pass_flow(3, 1)

    loss_total = loss_part[y]
    for d in (1, 2, 3):
        s = (y + d) % CHIPS
        remote(loss_part.at[s], loss_in.at[s], loss_send.at[0], loss_recv.at[s], chip(y + 1)).wait_recv()
        loss_total = loss_total + loss_in[s]
    loss_out[...] = loss_total

    for sender in (0, 1):

        @pl.when(y != sender + 1)
        def _():
            for c in range(RS_CHUNKS):
                where = pl.ds(c * rs_rows, rs_rows)
                part = mid_in.at[sender, where]
                remote(part, part, mid_send.at[0, c], mid_recv.at[sender, c], chip(y + 1)).wait_recv()
            parts[y] += mid_in[sender].astype(F32)

    @pl.when(is_middle)
    def _():
        for c in range(RS_CHUNKS):
            end_copy(y, c).wait_recv()
        parts[y] += end_in[y].astype(F32)

    image_float, image_length = unit_rows(images[...])
    image_out[...] = through_norm(parts[y], image_float, image_length).astype(BF16)

    sum_copy(0).wait_recv()
    text_sums = sums[0:rows, :] + sums_in[0].astype(F32)
    back_down.wait_recv()
    text_sums = text_sums + back_in[1].astype(F32)
    text_float, text_length = unit_rows(captions[...])
    back_up.wait_recv()
    text_sums = text_sums + back_in[0].astype(F32)
    text_out[...] = through_norm(text_sums, text_float, text_length).astype(BF16)

    for c in range(AG_CHUNKS):

        @pl.when(y < CHIPS - 1)
        def _():
            own_copy(c, 0).wait_send()

        @pl.when(y > 0)
        def _():
            own_copy(c, 1).wait_send()

    def line_sent(d, carry):
        s = (y + d) % CHIPS

        @pl.when(is_middle)
        def _():
            for c in range(AG_CHUNKS):
                fwd_copy(s, c).wait_send()
            for c in range(RS_CHUNKS):
                mid_copy(s, c).wait_send()

        @pl.when(is_end)
        def _():
            for c in range(RS_CHUNKS):
                end_copy(s, c).wait_send()

        return carry

    lax.fori_loop(1, CHIPS, line_sent, 0)

    @pl.when(jnp.logical_not(relayed_up))
    def _():
        next_up.wait_send()
        back_up.wait_send()

    @pl.when(jnp.logical_not(relayed_down))
    def _():
        next_down.wait_send()
        back_down.wait_send()

    for kind, c in flow_parts:
        first, second, sends, passes = flow(kind, c)
        pl.when(sends)(first.wait_send)
        pl.when(passes)(second.wait_send)

    for copy in core_copies + lab_copies + loss_copies + [sum_copy(i) for i in range(3)]:
        copy.wait_send()


def per_device(blocks, images, captions, labels, logit_scale, logit_bias):
    rows, width = images.shape
    vmem = pl.BlockSpec(memory_space=pltpu.VMEM)
    smem = pl.BlockSpec(memory_space=pltpu.SMEM)
    hbm = pl.BlockSpec(memory_space=pl.ANY)
    dma = pltpu.SemaphoreType.DMA
    loss, image_grad, text_grad = pl.pallas_call(
        functools.partial(kernel, blocks),
        out_shape=[
            jax.ShapeDtypeStruct((1, rows), F32),
            jax.ShapeDtypeStruct((rows, width), BF16),
            jax.ShapeDtypeStruct((rows, width), BF16),
        ],
        in_specs=[hbm, hbm, hbm, smem, smem],
        out_specs=[vmem, vmem, vmem],
        scratch_shapes=[
            pltpu.VMEM((rows, width), BF16),
            pltpu.VMEM((rows, width), BF16),
            pltpu.VMEM((CHIPS, rows, width), BF16),
            pltpu.VMEM((6 * rows, width), BF16),
            pltpu.VMEM((CHIPS, 1, rows), jnp.int32),
            pltpu.VMEM((CHIPS, 1, rows), F32),
            pltpu.VMEM((CHIPS, 1, rows), F32),
            pltpu.VMEM((CHIPS, rows, width), F32),
            pltpu.VMEM((CHIPS, rows, width), BF16),
            pltpu.VMEM((CHIPS, rows, width), BF16),
            pltpu.VMEM((2, rows, width), BF16),
            pltpu.VMEM((6 * rows, width), F32),
            pltpu.VMEM((3, rows, width), BF16),
            pltpu.VMEM((3, rows, width), BF16),
            pltpu.VMEM((2, rows, width), BF16),
            pltpu.VMEM((2, rows, width), BF16),
            pltpu.VMEM((4, rows, width), BF16),
            dma((3,)),
            dma((2, AG_CHUNKS)),
            dma((CHIPS, AG_CHUNKS)),
            dma((CHIPS, AG_CHUNKS)),
            dma((3,)),
            dma((CHIPS,)),
            dma((3,)),
            dma((CHIPS,)),
            dma((3,)),
            dma((3,)),
            dma((2,)),
            dma((2,)),
            dma((CHIPS, RS_CHUNKS)),
            dma((CHIPS, RS_CHUNKS)),
            dma((CHIPS, RS_CHUNKS)),
            dma((2, RS_CHUNKS)),
            dma((3,)),
            dma((3,)),
            dma((2,)),
            dma((2,)),
            dma((4, 3)),
            dma((4, 3)),
            dma((4, 3)),
            pltpu.SemaphoreType.REGULAR((5,)),
        ],
        compiler_params=pltpu.CompilerParams(
            collective_id=0, has_side_effects=True, vmem_limit_bytes=60 * 1024 * 1024
        ),
    )(images, captions, labels.reshape(1, rows), logit_scale, logit_bias)
    return (loss.reshape(rows), image_grad.astype(F32), text_grad.astype(F32))


def solution(mesh):
    body = functools.partial(per_device, mesh.shape["blk"])
    in_specs = (P(("blk", "group"), None), P(("blk", "group"), None), P(("blk", "group")), P(), P())
    out_specs = (P(("blk", "group")), P(("blk", "group"), None), P(("blk", "group"), None))
    return jax.shard_map(body, mesh=mesh, in_specs=in_specs, out_specs=out_specs, check_vma=False)
```

```python
import functools

import jax
import jax.numpy as jnp
from jax import lax
from jax.experimental import pallas as pl
from jax.experimental.pallas import tpu as pltpu
from jax.sharding import PartitionSpec as P

EPSILON = 1e-06
CHIPS = 4
LINE = 8
CAPTIONS_VIA = ((24, 0, 48), (8, 48, 48), (16, 96, 32))
CAPTIONS_UP_VIA = (8, 16)
SUMS_UP_VIA = ((24, 0, 64), (16, 64, 32), (8, 96, 32))
SUMS_DOWN_VIA = (23, 31)
AG_CHUNKS = 2
RS_CHUNKS = 4
MESH = pl.DeviceIdType.MESH
F32 = jnp.float32
BF16 = jnp.bfloat16


def unit_rows(values):
    wide = values.astype(F32)
    length = jnp.sqrt(jnp.sum(wide * wide, axis=-1, keepdims=True) + EPSILON)
    return (wide / length, length)


def through_norm(sums, unit_float, length):
    return (sums - unit_float * jnp.sum(unit_float * sums, axis=-1, keepdims=True)) / length


def depth_part(a, b, start, stop):
    return lax.dot_general(
        a[:, start:stop], b[:, start:stop], (((1,), (1,)), ((), ())), preferred_element_type=F32
    )


def summed_log(decay):
    pieces = [decay[i : i + 8, :] for i in range(0, decay.shape[0], 8)]
    while len(pieces) > 1:
        pieces = [a + b + a * b for a, b in zip(pieces[::2], pieces[1::2])]
    return jnp.sum(jnp.log1p(pieces[0]), axis=0, keepdims=True)


def pair_weights(raw, positive, scale, bias):
    logits = scale * raw + bias
    turned = jnp.where(positive, -logits, logits)
    decay = jnp.exp(-jnp.abs(turned))
    loss = jnp.sum(jnp.maximum(turned, 0.0), axis=0, keepdims=True) + summed_log(decay)
    share = jnp.where(turned >= 0, 1.0, decay) / (1.0 + decay)
    weights = jnp.where(positive, -scale, scale) * share
    return (loss, weights.astype(BF16))


def kernel(
    blocks,
    images_hbm,
    captions_hbm,
    labels_hbm,
    scale_ref,
    bias_ref,
    loss_out,
    image_out,
    text_out,
    images,
    captions,
    imgs,
    texts,
    labs,
    loss_part,
    loss_in,
    parts,
    parts_out,
    end_in,
    mid_in,
    sums,
    sums_out,
    sums_in,
    back_out,
    back_in,
    relay_in,
    load_sem,
    ag_own_send,
    ag_fwd_send,
    ag_recv,
    lab_send,
    lab_recv,
    loss_send,
    loss_recv,
    core_send,
    core_recv,
    next_send,
    next_recv,
    end_send,
    end_recv,
    mid_send,
    mid_recv,
    sum_send,
    sum_recv,
    back_send,
    back_recv,
    relay_src_send,
    relay_recv,
    relay_fwd_send,
    ready,
):
    rows = images.shape[0]
    ag_rows = rows // AG_CHUNKS
    rs_rows = rows // RS_CHUNKS
    blk = lax.axis_index("blk")
    group = lax.axis_index("group")
    y = group // 2
    core = group % 2
    other = group + 1 - 2 * core
    half = blocks // 2
    mirrored = 2 * (CHIPS - 1 - y) + core
    up_edge = (blk % half) // (half - 1)
    down_edge = (half - 1 - blk % half) // (half - 1)
    up_dev = {"blk": (blk + 1) % blocks, "group": group + up_edge * (mirrored - group)}
    down_dev = {"blk": (blk + blocks - 1) % blocks, "group": group + down_edge * (mirrored - group)}
    column = blk % half

    def inner_dev(step, turned=False):
        return {"blk": (blk + 2 * blocks + step) % blocks, "group": mirrored if turned else group}

    across_dev = inner_dev(half, True)
    wrap_dev = inner_dev((half - 1) * (down_edge - up_edge))
    other_dev = {"blk": blk, "group": other}

    def chip(position):
        return {"blk": blk, "group": (position + CHIPS) % CHIPS * 2 + core}

    def remote(src, dst, send, recv, device):
        return pltpu.make_async_remote_copy(
            src_ref=src, dst_ref=dst, send_sem=send, recv_sem=recv, device_id=device, device_id_type=MESH
        )

    is_end = (y == 0) | (y == CHIPS - 1)
    is_middle = (y == 1) | (y == 2)
    relayed_up = is_middle & (up_edge == 1)
    relayed_down = is_middle & (down_edge == 1)
    relayed = is_middle & (up_edge + down_edge == 1)
    in_column = {offset: is_middle & (column == offset) for offset in (7, 8, 15, 16, 23, 24)}
    is_first = blk % LINE == 0
    is_last = blk % LINE == LINE - 1
    not_first = jnp.logical_not(is_first)
    not_last = jnp.logical_not(is_last)

    loads = [
        pltpu.make_async_copy(captions_hbm, captions, load_sem.at[0]),
        pltpu.make_async_copy(images_hbm, images, load_sem.at[1]),
        pltpu.make_async_copy(labels_hbm, labs.at[y], load_sem.at[2]),
    ]
    for load in loads:
        load.start()

    barrier = pltpu.get_barrier_semaphore()

    def greet(device):
        pl.semaphore_signal(barrier, inc=1, device_id=device, device_id_type=MESH)

    for device in [other_dev] + [chip(y + d) for d in (1, 2, 3)]:
        greet(device)

    @pl.when(not_last)
    def _():
        greet(up_dev)

    @pl.when(is_first)
    def _():
        greet(down_dev)

    @pl.when(relayed_down)
    def _():
        greet(wrap_dev)
        for offset in CAPTIONS_UP_VIA:
            greet(inner_dev(offset - half, True))
        greet(inner_dev(SUMS_DOWN_VIA[0]))
        for offset, _, _ in CAPTIONS_VIA:
            greet(inner_dev(offset))
        for offset, _, _ in SUMS_UP_VIA:
            greet(inner_dev(-offset - 1, True))

    for offset in CAPTIONS_UP_VIA:

        @pl.when(in_column[offset])
        def _():
            greet(inner_dev(half - 1 - offset))
            greet(inner_dev(half - offset, True))

    @pl.when(relayed_up)
    def _():
        greet(across_dev)
        greet(inner_dev(SUMS_DOWN_VIA[0] + 1 - blocks, True))
        for offset, _, _ in SUMS_UP_VIA:
            greet(inner_dev(-offset))

    for offset, _, _ in CAPTIONS_VIA:

        @pl.when(in_column[offset])
        def _():
            greet(inner_dev(-offset))
            greet(inner_dev(-offset - 1, True))

    for offset, _, _ in SUMS_UP_VIA:

        @pl.when(in_column[half - 1 - offset])
        def _():
            greet(inner_dev(offset))

    @pl.when(in_column[SUMS_DOWN_VIA[0]])
    def _():
        greet(inner_dev(blocks - 1 - SUMS_DOWN_VIA[0], True))

    loads[0].wait()
    text_float, _ = unit_rows(captions[...])
    texts[0:rows, :] = text_float.astype(BF16)
    loads[1].wait()
    image_float, _ = unit_rows(images[...])
    imgs[y] = image_float.astype(BF16)
    loads[2].wait()

    inner = (y * (3 - y)) // 2
    peers = 4 + jnp.where(is_first, 0, 1) + jnp.where(is_last, 1, 0)
    inner_peers = 11 * up_edge + 5 * down_edge
    for offset, count in ((24, 1), (8, 2), (16, 2), (7, 2), (15, 2), (23, 4)):
        inner_peers = inner_peers + jnp.where(column == offset, count, 0)
    peers = peers + inner * inner_peers
    pl.semaphore_wait(barrier, peers)

    def answer(index, device):
        pl.semaphore_signal(ready.at[index], inc=1, device_id=device, device_id_type=MESH)

    @pl.when(not_first)
    def _():
        answer(0, down_dev)

    @pl.when(is_last)
    def _():
        answer(1, up_dev)

    @pl.when(relayed & is_last)
    def _():
        for offset, _, _ in CAPTIONS_VIA:
            answer(2, inner_dev(offset + 1, True))
        answer(4, wrap_dev)

    @pl.when(in_column[SUMS_DOWN_VIA[0]])
    def _():
        answer(3, inner_dev(-SUMS_DOWN_VIA[0]))

    def own_copy(c, direction):
        part = imgs.at[y, pl.ds(c * ag_rows, ag_rows)]
        return remote(
            part, part, ag_own_send.at[direction, c], ag_recv.at[y, c], chip(y + 1 - 2 * direction)
        )

    def fwd_copy(s, c):
        part = imgs.at[s, pl.ds(c * ag_rows, ag_rows)]
        target = jnp.where(s < y, y + 1, y - 1)
        return remote(part, part, ag_fwd_send.at[s, c], ag_recv.at[s, c], chip(target))

    def slot(i):
        return texts.at[pl.ds(i * rows, rows)]

    def flow(kind, c):
        if kind == 0:
            offset = CAPTIONS_UP_VIA[c]
            begin, size, source = c * 64, 64, slot(0)
            near_dev, far_dev = inner_dev(offset + 1 - half), inner_dev(half - offset, True)
            target, base, sem, sends, passes = texts, 2 * rows, next_recv.at[0], relayed_up, in_column[offset]
        elif kind == 1:
            offset, begin, size = CAPTIONS_VIA[c]
            source, near_dev, far_dev = slot(0), inner_dev(offset), inner_dev(-offset - 1, True)
            target, base, sem, sends, passes = texts, 4 * rows, next_recv.at[1], relayed_down, in_column[offset]
        elif kind == 2:
            offset, begin, size = SUMS_UP_VIA[c]
            source = back_out.at[1]
            near_dev, far_dev = inner_dev(-offset), inner_dev(offset + 1, True)
            target, base, sem = back_in.at[0], 0, back_recv.at[0]
            sends, passes = relayed_up, in_column[half - 1 - offset]
        else:
            offset = SUMS_DOWN_VIA[c]
            begin, size, source = c * 64, 64, back_out.at[0]
            near_dev, far_dev = inner_dev(offset), inner_dev(blocks - 1 - offset, True)
            target, base, sem = back_in.at[1], 0, back_recv.at[1]
            sends, passes = relayed_down, in_column[offset] if c == 0 else relayed_up
        held = relay_in.at[kind, pl.ds(begin, size)]
        first = remote(
            source.at[pl.ds(begin, size)], held, relay_src_send.at[kind, c], relay_recv.at[kind, c], near_dev
        )
        second = remote(
            held, target.at[pl.ds(base + begin, size)], relay_fwd_send.at[kind, c], sem, far_dev
        )
        return first, second, sends, passes

    flow_parts = [(0, 0), (0, 1), (1, 0), (1, 1), (1, 2), (2, 0), (2, 1), (2, 2), (3, 0), (3, 1)]

    def send_flow(kind, c):
        first, _, sends, _ = flow(kind, c)

        @pl.when(sends)
        def _():
            first.start()

    def pass_flow(kind, c):
        first, second, _, passes = flow(kind, c)

        @pl.when(passes)
        def _():
            first.wait_recv()
            second.start()

    next_up = remote(slot(0), slot(2), next_send.at[0], next_recv.at[0], up_dev)
    next_down = remote(slot(0), slot(4), next_send.at[1], next_recv.at[1], down_dev)
    core_copies = [
        remote(slot(2 * i), slot(2 * i + 1), core_send.at[i], core_recv.at[i], other_dev) for i in range(3)
    ]
    lab_copies = [
        remote(labs.at[y], labs.at[y], lab_send.at[d - 1], lab_recv.at[y], chip(y + d)) for d in (1, 2, 3)
    ]

    for kind, c in flow_parts[:5]:
        send_flow(kind, c)

    for c in range(AG_CHUNKS):

        @pl.when(y < CHIPS - 1)
        def _():
            own_copy(c, 0).start()

        @pl.when(y > 0)
        def _():
            own_copy(c, 1).start()

    core_copies[0].start()

    @pl.when(not_first)
    def _():
        next_down.start()

    for copy in lab_copies:
        copy.start()

    @pl.when(not_last)
    def _():
        pl.semaphore_wait(ready.at[0], 1)

    @pl.when(jnp.logical_not(relayed_up))
    def _():
        next_up.start()

    parts[...] = jnp.zeros_like(parts)
    sums[...] = jnp.zeros_like(sums)
    loss_part[...] = jnp.zeros_like(loss_part)

    near = jnp.where(y == 0, 1, jnp.where(y == 1, 0, jnp.where(y == 2, 3, 2)))
    next_near = jnp.where(y == 0, 2, jnp.where(y == 1, 2, 1))
    far = jnp.where(y < 2, 3, 0)

    def take(s, c):
        copy = fwd_copy(s, c)
        copy.wait_recv()

        @pl.when(is_middle)
        def _():
            copy.start()

    def take_labels(s):
        remote(labs.at[s], labs.at[s], lab_send.at[0], lab_recv.at[s], chip(y + 1)).wait_recv()

    scale = scale_ref[0]
    bias = bias_ref[0]

    def compute(s, i):
        image = imgs[s]
        where = pl.ds(pl.multiple_of(2 * i * rows, 2 * rows), 2 * rows)
        text = texts[where, :]
        raw = depth_part(text, image, 0, 512) + depth_part(text, image, 512, text.shape[1])
        label = labs[s]
        mine = label - group * rows
        theirs = label - other * rows
        theirs = jnp.where((theirs >= 0) & (theirs < rows), theirs + rows, -1)
        place = jnp.where((mine >= 0) & (mine < rows), mine, theirs)
        place = jnp.where(i == 0, place, -1)
        positive = lax.broadcasted_iota(jnp.int32, raw.shape, 0) == place
        loss, weights = pair_weights(raw, positive, scale, bias)
        sums[where, :] += jnp.dot(weights, image, preferred_element_type=F32)
        parts[s] += lax.dot_general(weights, text, (((0,), (0,)), ((), ())), preferred_element_type=F32)
        loss_part[s] += loss

    def end_copy(t, c):
        where = pl.ds(c * rs_rows, rs_rows)
        return remote(
            parts_out.at[t, where],
            end_in.at[t, where],
            end_send.at[t, c],
            end_recv.at[t, c],
            chip(1 + y // (CHIPS - 1)),
        )

    def mid_copy(t, c):
        where = pl.ds(c * rs_rows, rs_rows)
        sender = (y + 1) % 2
        return remote(
            parts_out.at[t, where], mid_in.at[sender, where], mid_send.at[t, c], mid_recv.at[sender, c], chip(t)
        )

    def sum_copy(i):
        return remote(sums_out.at[i], sums_in.at[i], sum_send.at[i], sum_recv.at[i], other_dev)

    def finish(i):
        sum_copy(i).wait_recv()
        total = sums[2 * i * rows : (2 * i + 1) * rows, :] + sums_in[i].astype(F32)
        back_out[i - 1] = total.astype(BF16)
        direct = back_down if i == 1 else back_up
        edge = relayed_down if i == 1 else relayed_up

        @pl.when(jnp.logical_not(edge))
        def _():
            direct.start()

        if i == 1:

            @pl.when(edge)
            def _():
                pl.semaphore_wait(ready.at[3], 1)
                pl.semaphore_wait(ready.at[4], 1)

        for c in range(1 + i):
            send_flow(4 - i, c)

    back_down = remote(back_out.at[0], back_in.at[1], back_send.at[0], back_recv.at[1], down_dev)
    back_up = remote(back_out.at[1], back_in.at[0], back_send.at[1], back_recv.at[0], up_dev)

    first_ends = is_first & is_end
    end_step = jnp.where(is_end, 1, 0)

    def chosen(u, usual, first, first_end, late):
        value = usual[0]
        for k in range(len(usual)):
            value = jnp.where(u == k, jnp.where(is_first, first[k], usual[k]), value)
            value = jnp.where((u == k) & relayed_up, late[k], value)
            value = jnp.where((u == k) & first_ends, first_end[k], value)
        return value

    usual_order = [y, near, near, near, y, y, next_near, next_near, next_near, far, far, far]
    late_order = [y, near, near, y, next_near, next_near, near, y, next_near, far, far, far]
    first_end_order = [y, near, near, y, next_near, next_near, next_near, far, far, far, near, y]
    first_order = [y, near, near, y, next_near, next_near, far, far, next_near, far, near, y]

    def step(u, carry):
        s = chosen(u, usual_order, first_order, first_end_order, late_order)
        i = chosen(u, [0, 0, 1, 2, 1, 2, 0, 1, 2, 2, 1, 0], [0, 0, 2, 2, 0, 2, 2, 0, 1, 1, 1, 1], [0, 0, 2, 2, 0, 2, 1, 2, 0, 1, 1, 1], [0, 0, 1, 1, 0, 1, 2, 2, 2, 2, 1, 0])

        @pl.when(u == 0)
        def _():
            core_copies[0].wait_recv()

        @pl.when((u == 1) & is_middle)
        def _():
            for c in range(AG_CHUNKS):
                take(near, c)
                take(next_near, c)

        @pl.when((u == 1) & is_end)
        def _():
            for c in range(AG_CHUNKS):
                take(near, c)

        @pl.when(u == 1)
        def _():
            for other_slot in (near, next_near, far):
                take_labels(other_slot)

        @pl.when((u == 2) & is_first)
        def _():
            pl.semaphore_wait(ready.at[1], 1)

        @pl.when((u == 2) & is_first & jnp.logical_not(relayed_down))
        def _():
            next_down.start()

        @pl.when((u == 2) & (in_column[8] | in_column[16] | in_column[24]))
        def _():
            pl.semaphore_wait(ready.at[2], 1)
            for c in range(3):
                pass_flow(1, c)

        @pl.when((u == 2) & is_first)
        def _():
            next_down.wait_recv()
            core_copies[2].start()

        @pl.when((u == 2) & not_first)
        def _():
            next_up.wait_recv()
            core_copies[1].start()

        @pl.when((u == 2) & is_middle)
        def _():
            take(far, 0)

        @pl.when((u == 2) & is_first)
        def _():
            core_copies[2].wait_recv()

        @pl.when((u == jnp.where(relayed_up, 6, 2)) & not_first)
        def _():
            next_down.wait_recv()
            core_copies[2].start()

        @pl.when((u == 2) & not_first)
        def _():
            core_copies[1].wait_recv()

        @pl.when((u == jnp.where(relayed_up, 6, 3)) & not_first)
        def _():
            core_copies[2].wait_recv()

        @pl.when((u == 4) & (in_column[8] | in_column[16]))
        def _():
            pass_flow(0, 0)
            pass_flow(0, 1)

        @pl.when((u == 4) & is_middle)
        def _():
            for c in range(1, AG_CHUNKS):
                take(far, c)

        @pl.when((u == jnp.where(is_first, 4, 6)) & is_end)
        def _():
            for c in range(AG_CHUNKS):
                take(next_near, c)

        @pl.when((u == jnp.where(is_first, 7, 9)) & is_end)
        def _():
            for c in range(AG_CHUNKS):
                take(far, c)

        @pl.when((u == jnp.where(is_end, 6, 8)) & is_first)
        def _():
            next_up.wait_recv()
            core_copies[1].start()
            core_copies[1].wait_recv()

        @pl.when(((u == jnp.where(is_end, 11, 9)) & is_first) | ((u == 11) & relayed_up))
        def _():
            finish(2)

        compute(s, i)

        @pl.when((u == jnp.where(is_first, 10, 9)) & is_middle)
        def _():
            parts_out[near] = parts[near].astype(BF16)
            for c in range(RS_CHUNKS):
                mid_copy(near, c).start()

        @pl.when(jnp.where(is_first, (u == 6 + end_step) | (u == 7 + end_step) | (u == 11), u > 8))
        def _():
            start = pl.multiple_of((2 * i + 1) * rows, rows)
            sums_out[i] = sums[pl.ds(start, rows), :].astype(BF16)
            sum_copy(i).start()

        @pl.when(jnp.where(is_first, (u == 6) | (u == 9) | (u == 10), (u == 3) | (u == 8) | (u == 11)) & is_end)
        def _():
            parts_out[s] = parts[s].astype(BF16)
            for c in range(RS_CHUNKS):
                end_copy(s, c).start()

        return carry

    lax.fori_loop(0, 3 * CHIPS, step, 0)

    @pl.when(not_first & jnp.logical_not(relayed_up))
    def _():
        finish(2)

    @pl.when(jnp.logical_not(is_first & is_middle))
    def _():
        finish(1)

    loss_copies = [
        remote(
            loss_part.at[(y + d) % CHIPS], loss_in.at[y], loss_send.at[d - 1], loss_recv.at[y], chip(y + d)
        )
        for d in (1, 2, 3)
    ]
    for copy in loss_copies:
        copy.start()

    def pass_on(t, c):
        where = pl.ds(pl.multiple_of(c * rs_rows, rs_rows), rs_rows)
        end_copy(t, c).wait_recv()
        total = parts[t, where, :] + end_in[t, where, :].astype(F32)
        parts_out[t, where, :] = total.astype(BF16)
        mid_copy(t, c).start()

    @pl.when(is_middle)
    def _():
        for c in range(3):
            pass_flow(2, c)

        def pass_all(k, carry):
            pass_on(jnp.where(k < RS_CHUNKS, next_near, far), k % RS_CHUNKS)

            @pl.when(is_first & (k == RS_CHUNKS - 1))
            def _():
                finish(1)

            @pl.when(in_column[23] & (k == RS_CHUNKS + RS_CHUNKS // 2))
            def _():
                pass_flow(3, 0)

            return carry

        lax.fori_loop(0, 2 * RS_CHUNKS, pass_all, 0)

    pass_flow(3, 1)

    loss_total = loss_part[y]
    for d in (1, 2, 3):
        s = (y + d) % CHIPS
        remote(loss_part.at[s], loss_in.at[s], loss_send.at[0], loss_recv.at[s], chip(y + 1)).wait_recv()
        loss_total = loss_total + loss_in[s]
    loss_out[...] = loss_total

    for sender in (0, 1):

        @pl.when(y != sender + 1)
        def _():
            for c in range(RS_CHUNKS):
                where = pl.ds(c * rs_rows, rs_rows)
                part = mid_in.at[sender, where]
                remote(part, part, mid_send.at[0, c], mid_recv.at[sender, c], chip(y + 1)).wait_recv()
            parts[y] += mid_in[sender].astype(F32)

    @pl.when(is_middle)
    def _():
        for c in range(RS_CHUNKS):
            end_copy(y, c).wait_recv()
        parts[y] += end_in[y].astype(F32)

    image_float, image_length = unit_rows(images[...])
    image_out[...] = through_norm(parts[y], image_float, image_length).astype(BF16)

    sum_copy(0).wait_recv()
    text_sums = sums[0:rows, :] + sums_in[0].astype(F32)
    back_down.wait_recv()
    text_sums = text_sums + back_in[1].astype(F32)
    text_float, text_length = unit_rows(captions[...])
    back_up.wait_recv()
    text_sums = text_sums + back_in[0].astype(F32)
    text_out[...] = through_norm(text_sums, text_float, text_length).astype(BF16)

    for c in range(AG_CHUNKS):

        @pl.when(y < CHIPS - 1)
        def _():
            own_copy(c, 0).wait_send()

        @pl.when(y > 0)
        def _():
            own_copy(c, 1).wait_send()

    def line_sent(d, carry):
        s = (y + d) % CHIPS

        @pl.when(is_middle)
        def _():
            for c in range(AG_CHUNKS):
                fwd_copy(s, c).wait_send()
            for c in range(RS_CHUNKS):
                mid_copy(s, c).wait_send()

        @pl.when(is_end)
        def _():
            for c in range(RS_CHUNKS):
                end_copy(s, c).wait_send()

        return carry

    lax.fori_loop(1, CHIPS, line_sent, 0)

    @pl.when(jnp.logical_not(relayed_up))
    def _():
        next_up.wait_send()
        back_up.wait_send()

    @pl.when(jnp.logical_not(relayed_down))
    def _():
        next_down.wait_send()
        back_down.wait_send()

    for kind, c in flow_parts:
        first, second, sends, passes = flow(kind, c)
        pl.when(sends)(first.wait_send)
        pl.when(passes)(second.wait_send)

    for copy in core_copies + lab_copies + loss_copies + [sum_copy(i) for i in range(3)]:
        copy.wait_send()


def per_device(blocks, images, captions, labels, logit_scale, logit_bias):
    rows, width = images.shape
    vmem = pl.BlockSpec(memory_space=pltpu.VMEM)
    smem = pl.BlockSpec(memory_space=pltpu.SMEM)
    hbm = pl.BlockSpec(memory_space=pl.ANY)
    dma = pltpu.SemaphoreType.DMA
    loss, image_grad, text_grad = pl.pallas_call(
        functools.partial(kernel, blocks),
        out_shape=[
            jax.ShapeDtypeStruct((1, rows), F32),
            jax.ShapeDtypeStruct((rows, width), BF16),
            jax.ShapeDtypeStruct((rows, width), BF16),
        ],
        in_specs=[hbm, hbm, hbm, smem, smem],
        out_specs=[vmem, vmem, vmem],
        scratch_shapes=[
            pltpu.VMEM((rows, width), BF16),
            pltpu.VMEM((rows, width), BF16),
            pltpu.VMEM((CHIPS, rows, width), BF16),
            pltpu.VMEM((6 * rows, width), BF16),
            pltpu.VMEM((CHIPS, 1, rows), jnp.int32),
            pltpu.VMEM((CHIPS, 1, rows), F32),
            pltpu.VMEM((CHIPS, 1, rows), F32),
            pltpu.VMEM((CHIPS, rows, width), F32),
            pltpu.VMEM((CHIPS, rows, width), BF16),
            pltpu.VMEM((CHIPS, rows, width), BF16),
            pltpu.VMEM((2, rows, width), BF16),
            pltpu.VMEM((6 * rows, width), F32),
            pltpu.VMEM((3, rows, width), BF16),
            pltpu.VMEM((3, rows, width), BF16),
            pltpu.VMEM((2, rows, width), BF16),
            pltpu.VMEM((2, rows, width), BF16),
            pltpu.VMEM((4, rows, width), BF16),
            dma((3,)),
            dma((2, AG_CHUNKS)),
            dma((CHIPS, AG_CHUNKS)),
            dma((CHIPS, AG_CHUNKS)),
            dma((3,)),
            dma((CHIPS,)),
            dma((3,)),
            dma((CHIPS,)),
            dma((3,)),
            dma((3,)),
            dma((2,)),
            dma((2,)),
            dma((CHIPS, RS_CHUNKS)),
            dma((CHIPS, RS_CHUNKS)),
            dma((CHIPS, RS_CHUNKS)),
            dma((2, RS_CHUNKS)),
            dma((3,)),
            dma((3,)),
            dma((2,)),
            dma((2,)),
            dma((4, 3)),
            dma((4, 3)),
            dma((4, 3)),
            pltpu.SemaphoreType.REGULAR((5,)),
        ],
        compiler_params=pltpu.CompilerParams(
            collective_id=0, has_side_effects=True, vmem_limit_bytes=60 * 1024 * 1024
        ),
    )(images, captions, labels.reshape(1, rows), logit_scale, logit_bias)
    return (loss.reshape(rows), image_grad.astype(F32), text_grad.astype(F32))


def solution(mesh):
    body = functools.partial(per_device, mesh.shape["blk"])
    in_specs = (P(("blk", "group"), None), P(("blk", "group"), None), P(("blk", "group")), P(), P())
    out_specs = (P(("blk", "group")), P(("blk", "group"), None), P(("blk", "group"), None))
    return jax.shard_map(body, mesh=mesh, in_specs=in_specs, out_specs=out_specs, check_vma=False)
```

```python
import functools

import jax
import jax.numpy as jnp
from jax import lax
from jax.experimental import pallas as pl
from jax.experimental.pallas import tpu as pltpu
from jax.sharding import PartitionSpec as P

EPSILON = 1e-06
CHIPS = 4
LINE = 8
CAPTIONS_VIA = ((24, 0, 48), (8, 48, 48), (16, 96, 32))
CAPTIONS_UP_VIA = (8, 16)
SUMS_UP_VIA = ((24, 0, 80), (16, 80, 32), (8, 112, 16))
SUMS_DOWN_VIA = (23, 31)
AG_CHUNKS = 2
RS_CHUNKS = 4
MESH = pl.DeviceIdType.MESH
F32 = jnp.float32
BF16 = jnp.bfloat16


def unit_rows(values):
    wide = values.astype(F32)
    length = jnp.sqrt(jnp.sum(wide * wide, axis=-1, keepdims=True) + EPSILON)
    return (wide / length, length)


def through_norm(sums, unit_float, length):
    return (sums - unit_float * jnp.sum(unit_float * sums, axis=-1, keepdims=True)) / length


def depth_part(a, b, start, stop):
    return lax.dot_general(
        a[:, start:stop], b[:, start:stop], (((1,), (1,)), ((), ())), preferred_element_type=F32
    )


def summed_log(decay):
    pieces = [decay[i : i + 8, :] for i in range(0, decay.shape[0], 8)]
    while len(pieces) > 1:
        pieces = [a + b + a * b for a, b in zip(pieces[::2], pieces[1::2])]
    return jnp.sum(jnp.log1p(pieces[0]), axis=0, keepdims=True)


def pair_weights(raw, positive, scale, bias):
    logits = scale * raw + bias
    turned = jnp.where(positive, -logits, logits)
    decay = jnp.exp(-jnp.abs(turned))
    loss = jnp.sum(jnp.maximum(turned, 0.0), axis=0, keepdims=True) + summed_log(decay)
    share = jnp.where(turned >= 0, 1.0, decay) / (1.0 + decay)
    weights = jnp.where(positive, -scale, scale) * share
    return (loss, weights.astype(BF16))


def kernel(
    blocks,
    images_hbm,
    captions_hbm,
    labels_hbm,
    scale_ref,
    bias_ref,
    loss_out,
    image_out,
    text_out,
    images,
    captions,
    imgs,
    texts,
    labs,
    loss_part,
    loss_in,
    parts,
    parts_out,
    end_in,
    mid_in,
    sums,
    sums_out,
    sums_in,
    back_out,
    back_in,
    relay_in,
    load_sem,
    ag_own_send,
    ag_fwd_send,
    ag_recv,
    lab_send,
    lab_recv,
    loss_send,
    loss_recv,
    core_send,
    core_recv,
    next_send,
    next_recv,
    end_send,
    end_recv,
    mid_send,
    mid_recv,
    sum_send,
    sum_recv,
    back_send,
    back_recv,
    relay_src_send,
    relay_recv,
    relay_fwd_send,
    ready,
):
    rows = images.shape[0]
    ag_rows = rows // AG_CHUNKS
    rs_rows = rows // RS_CHUNKS
    blk = lax.axis_index("blk")
    group = lax.axis_index("group")
    y = group // 2
    core = group % 2
    other = group + 1 - 2 * core
    half = blocks // 2
    mirrored = 2 * (CHIPS - 1 - y) + core
    up_edge = (blk % half) // (half - 1)
    down_edge = (half - 1 - blk % half) // (half - 1)
    up_dev = {"blk": (blk + 1) % blocks, "group": group + up_edge * (mirrored - group)}
    down_dev = {"blk": (blk + blocks - 1) % blocks, "group": group + down_edge * (mirrored - group)}
    column = blk % half

    def inner_dev(step, turned=False):
        return {"blk": (blk + 2 * blocks + step) % blocks, "group": mirrored if turned else group}

    across_dev = inner_dev(half, True)
    wrap_dev = inner_dev((half - 1) * (down_edge - up_edge))
    other_dev = {"blk": blk, "group": other}

    def chip(position):
        return {"blk": blk, "group": (position + CHIPS) % CHIPS * 2 + core}

    def remote(src, dst, send, recv, device):
        return pltpu.make_async_remote_copy(
            src_ref=src, dst_ref=dst, send_sem=send, recv_sem=recv, device_id=device, device_id_type=MESH
        )

    is_end = (y == 0) | (y == CHIPS - 1)
    is_middle = (y == 1) | (y == 2)
    relayed_up = is_middle & (up_edge == 1)
    relayed_down = is_middle & (down_edge == 1)
    relayed = is_middle & (up_edge + down_edge == 1)
    in_column = {offset: is_middle & (column == offset) for offset in (7, 8, 15, 16, 23, 24)}
    is_first = blk % LINE == 0
    is_last = blk % LINE == LINE - 1
    not_first = jnp.logical_not(is_first)
    not_last = jnp.logical_not(is_last)

    loads = [
        pltpu.make_async_copy(captions_hbm, captions, load_sem.at[0]),
        pltpu.make_async_copy(images_hbm, images, load_sem.at[1]),
        pltpu.make_async_copy(labels_hbm, labs.at[y], load_sem.at[2]),
    ]
    for load in loads:
        load.start()

    barrier = pltpu.get_barrier_semaphore()

    def greet(device):
        pl.semaphore_signal(barrier, inc=1, device_id=device, device_id_type=MESH)

    for device in [other_dev] + [chip(y + d) for d in (1, 2, 3)]:
        greet(device)

    @pl.when(not_last)
    def _():
        greet(up_dev)

    @pl.when(is_first)
    def _():
        greet(down_dev)

    @pl.when(relayed_down)
    def _():
        greet(wrap_dev)
        for offset in CAPTIONS_UP_VIA:
            greet(inner_dev(offset - half, True))
        greet(inner_dev(SUMS_DOWN_VIA[0]))
        for offset, _, _ in CAPTIONS_VIA:
            greet(inner_dev(offset))
        for offset, _, _ in SUMS_UP_VIA:
            greet(inner_dev(-offset - 1, True))

    for offset in CAPTIONS_UP_VIA:

        @pl.when(in_column[offset])
        def _():
            greet(inner_dev(half - 1 - offset))
            greet(inner_dev(half - offset, True))

    @pl.when(relayed_up)
    def _():
        greet(across_dev)
        greet(inner_dev(SUMS_DOWN_VIA[0] + 1 - blocks, True))
        for offset, _, _ in SUMS_UP_VIA:
            greet(inner_dev(-offset))

    for offset, _, _ in CAPTIONS_VIA:

        @pl.when(in_column[offset])
        def _():
            greet(inner_dev(-offset))
            greet(inner_dev(-offset - 1, True))

    for offset, _, _ in SUMS_UP_VIA:

        @pl.when(in_column[half - 1 - offset])
        def _():
            greet(inner_dev(offset))

    @pl.when(in_column[SUMS_DOWN_VIA[0]])
    def _():
        greet(inner_dev(blocks - 1 - SUMS_DOWN_VIA[0], True))

    loads[0].wait()
    text_float, _ = unit_rows(captions[...])
    texts[0:rows, :] = text_float.astype(BF16)
    loads[1].wait()
    image_float, _ = unit_rows(images[...])
    imgs[y] = image_float.astype(BF16)
    loads[2].wait()

    inner = (y * (3 - y)) // 2
    peers = 4 + jnp.where(is_first, 0, 1) + jnp.where(is_last, 1, 0)
    inner_peers = 11 * up_edge + 5 * down_edge
    for offset, count in ((24, 1), (8, 2), (16, 2), (7, 2), (15, 2), (23, 4)):
        inner_peers = inner_peers + jnp.where(column == offset, count, 0)
    peers = peers + inner * inner_peers
    pl.semaphore_wait(barrier, peers)

    def answer(index, device):
        pl.semaphore_signal(ready.at[index], inc=1, device_id=device, device_id_type=MESH)

    @pl.when(not_first)
    def _():
        answer(0, down_dev)

    @pl.when(is_last)
    def _():
        answer(1, up_dev)

    @pl.when(relayed & is_last)
    def _():
        for offset, _, _ in CAPTIONS_VIA:
            answer(2, inner_dev(offset + 1, True))
        answer(4, wrap_dev)

    @pl.when(in_column[SUMS_DOWN_VIA[0]])
    def _():
        answer(3, inner_dev(-SUMS_DOWN_VIA[0]))

    def own_copy(c, direction):
        part = imgs.at[y, pl.ds(c * ag_rows, ag_rows)]
        return remote(
            part, part, ag_own_send.at[direction, c], ag_recv.at[y, c], chip(y + 1 - 2 * direction)
        )

    def fwd_copy(s, c):
        part = imgs.at[s, pl.ds(c * ag_rows, ag_rows)]
        target = jnp.where(s < y, y + 1, y - 1)
        return remote(part, part, ag_fwd_send.at[s, c], ag_recv.at[s, c], chip(target))

    def slot(i):
        return texts.at[pl.ds(i * rows, rows)]

    def flow(kind, c):
        if kind == 0:
            offset = CAPTIONS_UP_VIA[c]
            begin, size, source = c * 64, 64, slot(0)
            near_dev, far_dev = inner_dev(offset + 1 - half), inner_dev(half - offset, True)
            target, base, sem, sends, passes = texts, 2 * rows, next_recv.at[0], relayed_up, in_column[offset]
        elif kind == 1:
            offset, begin, size = CAPTIONS_VIA[c]
            source, near_dev, far_dev = slot(0), inner_dev(offset), inner_dev(-offset - 1, True)
            target, base, sem, sends, passes = texts, 4 * rows, next_recv.at[1], relayed_down, in_column[offset]
        elif kind == 2:
            offset, begin, size = SUMS_UP_VIA[c]
            source = back_out.at[1]
            near_dev, far_dev = inner_dev(-offset), inner_dev(offset + 1, True)
            target, base, sem = back_in.at[0], 0, back_recv.at[0]
            sends, passes = relayed_up, in_column[half - 1 - offset]
        else:
            offset = SUMS_DOWN_VIA[c]
            begin, size, source = c * 64, 64, back_out.at[0]
            near_dev, far_dev = inner_dev(offset), inner_dev(blocks - 1 - offset, True)
            target, base, sem = back_in.at[1], 0, back_recv.at[1]
            sends, passes = relayed_down, in_column[offset] if c == 0 else relayed_up
        held = relay_in.at[kind, pl.ds(begin, size)]
        first = remote(
            source.at[pl.ds(begin, size)], held, relay_src_send.at[kind, c], relay_recv.at[kind, c], near_dev
        )
        second = remote(
            held, target.at[pl.ds(base + begin, size)], relay_fwd_send.at[kind, c], sem, far_dev
        )
        return first, second, sends, passes

    flow_parts = [(0, 0), (0, 1), (1, 0), (1, 1), (1, 2), (2, 0), (2, 1), (2, 2), (3, 0), (3, 1)]

    def send_flow(kind, c):
        first, _, sends, _ = flow(kind, c)

        @pl.when(sends)
        def _():
            first.start()

    def pass_flow(kind, c):
        first, second, _, passes = flow(kind, c)

        @pl.when(passes)
        def _():
            first.wait_recv()
            second.start()

    next_up = remote(slot(0), slot(2), next_send.at[0], next_recv.at[0], up_dev)
    next_down = remote(slot(0), slot(4), next_send.at[1], next_recv.at[1], down_dev)
    core_copies = [
        remote(slot(2 * i), slot(2 * i + 1), core_send.at[i], core_recv.at[i], other_dev) for i in range(3)
    ]
    lab_copies = [
        remote(labs.at[y], labs.at[y], lab_send.at[d - 1], lab_recv.at[y], chip(y + d)) for d in (1, 2, 3)
    ]

    for kind, c in flow_parts[:5]:
        send_flow(kind, c)

    for c in range(AG_CHUNKS):

        @pl.when(y < CHIPS - 1)
        def _():
            own_copy(c, 0).start()

        @pl.when(y > 0)
        def _():
            own_copy(c, 1).start()

    core_copies[0].start()

    @pl.when(not_first)
    def _():
        next_down.start()

    for copy in lab_copies:
        copy.start()

    @pl.when(not_last)
    def _():
        pl.semaphore_wait(ready.at[0], 1)

    @pl.when(jnp.logical_not(relayed_up))
    def _():
        next_up.start()

    parts[...] = jnp.zeros_like(parts)
    sums[...] = jnp.zeros_like(sums)
    loss_part[...] = jnp.zeros_like(loss_part)

    near = jnp.where(y == 0, 1, jnp.where(y == 1, 0, jnp.where(y == 2, 3, 2)))
    next_near = jnp.where(y == 0, 2, jnp.where(y == 1, 2, 1))
    far = jnp.where(y < 2, 3, 0)

    def take(s, c):
        copy = fwd_copy(s, c)
        copy.wait_recv()

        @pl.when(is_middle)
        def _():
            copy.start()

    def take_labels(s):
        remote(labs.at[s], labs.at[s], lab_send.at[0], lab_recv.at[s], chip(y + 1)).wait_recv()

    scale = scale_ref[0]
    bias = bias_ref[0]

    def compute(s, i):
        image = imgs[s]
        where = pl.ds(pl.multiple_of(2 * i * rows, 2 * rows), 2 * rows)
        text = texts[where, :]
        raw = depth_part(text, image, 0, 512) + depth_part(text, image, 512, text.shape[1])
        label = labs[s]
        mine = label - group * rows
        theirs = label - other * rows
        theirs = jnp.where((theirs >= 0) & (theirs < rows), theirs + rows, -1)
        place = jnp.where((mine >= 0) & (mine < rows), mine, theirs)
        place = jnp.where(i == 0, place, -1)
        positive = lax.broadcasted_iota(jnp.int32, raw.shape, 0) == place
        loss, weights = pair_weights(raw, positive, scale, bias)
        sums[where, :] += jnp.dot(weights, image, preferred_element_type=F32)
        parts[s] += lax.dot_general(weights, text, (((0,), (0,)), ((), ())), preferred_element_type=F32)
        loss_part[s] += loss

    def end_copy(t, c):
        where = pl.ds(c * rs_rows, rs_rows)
        return remote(
            parts_out.at[t, where],
            end_in.at[t, where],
            end_send.at[t, c],
            end_recv.at[t, c],
            chip(1 + y // (CHIPS - 1)),
        )

    def mid_copy(t, c):
        where = pl.ds(c * rs_rows, rs_rows)
        sender = (y + 1) % 2
        return remote(
            parts_out.at[t, where], mid_in.at[sender, where], mid_send.at[t, c], mid_recv.at[sender, c], chip(t)
        )

    def sum_copy(i):
        return remote(sums_out.at[i], sums_in.at[i], sum_send.at[i], sum_recv.at[i], other_dev)

    def finish(i):
        sum_copy(i).wait_recv()
        total = sums[2 * i * rows : (2 * i + 1) * rows, :] + sums_in[i].astype(F32)
        back_out[i - 1] = total.astype(BF16)
        direct = back_down if i == 1 else back_up
        edge = relayed_down if i == 1 else relayed_up

        @pl.when(jnp.logical_not(edge))
        def _():
            direct.start()

        if i == 1:

            @pl.when(edge)
            def _():
                pl.semaphore_wait(ready.at[3], 1)
                pl.semaphore_wait(ready.at[4], 1)

        for c in range(1 + i):
            send_flow(4 - i, c)

    back_down = remote(back_out.at[0], back_in.at[1], back_send.at[0], back_recv.at[1], down_dev)
    back_up = remote(back_out.at[1], back_in.at[0], back_send.at[1], back_recv.at[0], up_dev)

    first_ends = is_first & is_end
    end_step = jnp.where(is_end, 1, 0)

    def chosen(u, usual, first, first_end, late):
        value = usual[0]
        for k in range(len(usual)):
            value = jnp.where(u == k, jnp.where(is_first, first[k], usual[k]), value)
            value = jnp.where((u == k) & relayed_up, late[k], value)
            value = jnp.where((u == k) & first_ends, first_end[k], value)
        return value

    usual_order = [y, near, near, near, y, y, next_near, next_near, next_near, far, far, far]
    late_order = [y, near, near, y, next_near, next_near, near, y, next_near, far, far, far]
    first_end_order = [y, near, near, y, next_near, next_near, next_near, far, far, far, near, y]
    first_order = [y, near, near, y, next_near, next_near, far, far, next_near, far, near, y]

    def step(u, carry):
        s = chosen(u, usual_order, first_order, first_end_order, late_order)
        i = chosen(u, [0, 0, 1, 2, 1, 2, 0, 1, 2, 2, 1, 0], [0, 0, 2, 2, 0, 2, 2, 0, 1, 1, 1, 1], [0, 0, 2, 2, 0, 2, 1, 2, 0, 1, 1, 1], [0, 0, 1, 1, 0, 1, 2, 2, 2, 2, 1, 0])

        @pl.when(u == 0)
        def _():
            core_copies[0].wait_recv()

        @pl.when((u == 1) & is_middle)
        def _():
            for c in range(AG_CHUNKS):
                take(near, c)
                take(next_near, c)

        @pl.when((u == 1) & is_end)
        def _():
            for c in range(AG_CHUNKS):
                take(near, c)

        @pl.when(u == 1)
        def _():
            for other_slot in (near, next_near, far):
                take_labels(other_slot)

        @pl.when((u == 2) & is_first)
        def _():
            pl.semaphore_wait(ready.at[1], 1)

        @pl.when((u == 2) & is_first & jnp.logical_not(relayed_down))
        def _():
            next_down.start()

        @pl.when((u == 2) & (in_column[8] | in_column[16] | in_column[24]))
        def _():
            pl.semaphore_wait(ready.at[2], 1)
            for c in range(3):
                pass_flow(1, c)

        @pl.when((u == 2) & is_first)
        def _():
            next_down.wait_recv()
            core_copies[2].start()

        @pl.when((u == 2) & not_first)
        def _():
            next_up.wait_recv()
            core_copies[1].start()

        @pl.when((u == 2) & is_middle)
        def _():
            take(far, 0)

        @pl.when((u == 2) & is_first)
        def _():
            core_copies[2].wait_recv()

        @pl.when((u == jnp.where(relayed_up, 6, 2)) & not_first)
        def _():
            next_down.wait_recv()
            core_copies[2].start()

        @pl.when((u == 2) & not_first)
        def _():
            core_copies[1].wait_recv()

        @pl.when((u == jnp.where(relayed_up, 6, 3)) & not_first)
        def _():
            core_copies[2].wait_recv()

        @pl.when((u == 4) & (in_column[8] | in_column[16]))
        def _():
            pass_flow(0, 0)
            pass_flow(0, 1)

        @pl.when((u == 4) & is_middle)
        def _():
            for c in range(1, AG_CHUNKS):
                take(far, c)

        @pl.when((u == jnp.where(is_first, 4, 6)) & is_end)
        def _():
            for c in range(AG_CHUNKS):
                take(next_near, c)

        @pl.when((u == jnp.where(is_first, 7, 9)) & is_end)
        def _():
            for c in range(AG_CHUNKS):
                take(far, c)

        @pl.when((u == jnp.where(is_end, 6, 8)) & is_first)
        def _():
            next_up.wait_recv()
            core_copies[1].start()
            core_copies[1].wait_recv()

        @pl.when(((u == jnp.where(is_end, 11, 9)) & is_first) | ((u == 11) & relayed_up))
        def _():
            finish(2)

        compute(s, i)

        @pl.when((u == jnp.where(is_first, 10, 9)) & is_middle)
        def _():
            parts_out[near] = parts[near].astype(BF16)
            for c in range(RS_CHUNKS):
                mid_copy(near, c).start()

        @pl.when(jnp.where(is_first, (u == 6 + end_step) | (u == 7 + end_step) | (u == 11), u > 8))
        def _():
            start = pl.multiple_of((2 * i + 1) * rows, rows)
            sums_out[i] = sums[pl.ds(start, rows), :].astype(BF16)
            sum_copy(i).start()

        @pl.when(jnp.where(is_first, (u == 6) | (u == 9) | (u == 10), (u == 3) | (u == 8) | (u == 11)) & is_end)
        def _():
            parts_out[s] = parts[s].astype(BF16)
            for c in range(RS_CHUNKS):
                end_copy(s, c).start()

        return carry

    lax.fori_loop(0, 3 * CHIPS, step, 0)

    @pl.when(not_first & jnp.logical_not(relayed_up))
    def _():
        finish(2)

    @pl.when(jnp.logical_not(is_first & is_middle))
    def _():
        finish(1)

    loss_copies = [
        remote(
            loss_part.at[(y + d) % CHIPS], loss_in.at[y], loss_send.at[d - 1], loss_recv.at[y], chip(y + d)
        )
        for d in (1, 2, 3)
    ]
    for copy in loss_copies:
        copy.start()

    def pass_on(t, c):
        where = pl.ds(pl.multiple_of(c * rs_rows, rs_rows), rs_rows)
        end_copy(t, c).wait_recv()
        total = parts[t, where, :] + end_in[t, where, :].astype(F32)
        parts_out[t, where, :] = total.astype(BF16)
        mid_copy(t, c).start()

    @pl.when(is_middle)
    def _():
        for c in range(3):
            pass_flow(2, c)

        def pass_all(k, carry):
            pass_on(jnp.where(k < RS_CHUNKS, next_near, far), k % RS_CHUNKS)

            @pl.when(is_first & (k == RS_CHUNKS - 1))
            def _():
                finish(1)

            @pl.when(in_column[23] & (k == RS_CHUNKS + RS_CHUNKS // 2))
            def _():
                pass_flow(3, 0)

            return carry

        lax.fori_loop(0, 2 * RS_CHUNKS, pass_all, 0)

    pass_flow(3, 1)

    loss_total = loss_part[y]
    for d in (1, 2, 3):
        s = (y + d) % CHIPS
        remote(loss_part.at[s], loss_in.at[s], loss_send.at[0], loss_recv.at[s], chip(y + 1)).wait_recv()
        loss_total = loss_total + loss_in[s]
    loss_out[...] = loss_total

    for sender in (0, 1):

        @pl.when(y != sender + 1)
        def _():
            for c in range(RS_CHUNKS):
                where = pl.ds(c * rs_rows, rs_rows)
                part = mid_in.at[sender, where]
                remote(part, part, mid_send.at[0, c], mid_recv.at[sender, c], chip(y + 1)).wait_recv()
            parts[y] += mid_in[sender].astype(F32)

    @pl.when(is_middle)
    def _():
        for c in range(RS_CHUNKS):
            end_copy(y, c).wait_recv()
        parts[y] += end_in[y].astype(F32)

    image_float, image_length = unit_rows(images[...])
    image_out[...] = through_norm(parts[y], image_float, image_length).astype(BF16)

    sum_copy(0).wait_recv()
    text_sums = sums[0:rows, :] + sums_in[0].astype(F32)
    back_down.wait_recv()
    text_sums = text_sums + back_in[1].astype(F32)
    text_float, text_length = unit_rows(captions[...])
    back_up.wait_recv()
    text_sums = text_sums + back_in[0].astype(F32)
    text_out[...] = through_norm(text_sums, text_float, text_length).astype(BF16)

    for c in range(AG_CHUNKS):

        @pl.when(y < CHIPS - 1)
        def _():
            own_copy(c, 0).wait_send()

        @pl.when(y > 0)
        def _():
            own_copy(c, 1).wait_send()

    def line_sent(d, carry):
        s = (y + d) % CHIPS

        @pl.when(is_middle)
        def _():
            for c in range(AG_CHUNKS):
                fwd_copy(s, c).wait_send()
            for c in range(RS_CHUNKS):
                mid_copy(s, c).wait_send()

        @pl.when(is_end)
        def _():
            for c in range(RS_CHUNKS):
                end_copy(s, c).wait_send()

        return carry

    lax.fori_loop(1, CHIPS, line_sent, 0)

    @pl.when(jnp.logical_not(relayed_up))
    def _():
        next_up.wait_send()
        back_up.wait_send()

    @pl.when(jnp.logical_not(relayed_down))
    def _():
        next_down.wait_send()
        back_down.wait_send()

    for kind, c in flow_parts:
        first, second, sends, passes = flow(kind, c)
        pl.when(sends)(first.wait_send)
        pl.when(passes)(second.wait_send)

    for copy in core_copies + lab_copies + loss_copies + [sum_copy(i) for i in range(3)]:
        copy.wait_send()


def per_device(blocks, images, captions, labels, logit_scale, logit_bias):
    rows, width = images.shape
    vmem = pl.BlockSpec(memory_space=pltpu.VMEM)
    smem = pl.BlockSpec(memory_space=pltpu.SMEM)
    hbm = pl.BlockSpec(memory_space=pl.ANY)
    dma = pltpu.SemaphoreType.DMA
    loss, image_grad, text_grad = pl.pallas_call(
        functools.partial(kernel, blocks),
        out_shape=[
            jax.ShapeDtypeStruct((1, rows), F32),
            jax.ShapeDtypeStruct((rows, width), BF16),
            jax.ShapeDtypeStruct((rows, width), BF16),
        ],
        in_specs=[hbm, hbm, hbm, smem, smem],
        out_specs=[vmem, vmem, vmem],
        scratch_shapes=[
            pltpu.VMEM((rows, width), BF16),
            pltpu.VMEM((rows, width), BF16),
            pltpu.VMEM((CHIPS, rows, width), BF16),
            pltpu.VMEM((6 * rows, width), BF16),
            pltpu.VMEM((CHIPS, 1, rows), jnp.int32),
            pltpu.VMEM((CHIPS, 1, rows), F32),
            pltpu.VMEM((CHIPS, 1, rows), F32),
            pltpu.VMEM((CHIPS, rows, width), F32),
            pltpu.VMEM((CHIPS, rows, width), BF16),
            pltpu.VMEM((CHIPS, rows, width), BF16),
            pltpu.VMEM((2, rows, width), BF16),
            pltpu.VMEM((6 * rows, width), F32),
            pltpu.VMEM((3, rows, width), BF16),
            pltpu.VMEM((3, rows, width), BF16),
            pltpu.VMEM((2, rows, width), BF16),
            pltpu.VMEM((2, rows, width), BF16),
            pltpu.VMEM((4, rows, width), BF16),
            dma((3,)),
            dma((2, AG_CHUNKS)),
            dma((CHIPS, AG_CHUNKS)),
            dma((CHIPS, AG_CHUNKS)),
            dma((3,)),
            dma((CHIPS,)),
            dma((3,)),
            dma((CHIPS,)),
            dma((3,)),
            dma((3,)),
            dma((2,)),
            dma((2,)),
            dma((CHIPS, RS_CHUNKS)),
            dma((CHIPS, RS_CHUNKS)),
            dma((CHIPS, RS_CHUNKS)),
            dma((2, RS_CHUNKS)),
            dma((3,)),
            dma((3,)),
            dma((2,)),
            dma((2,)),
            dma((4, 3)),
            dma((4, 3)),
            dma((4, 3)),
            pltpu.SemaphoreType.REGULAR((5,)),
        ],
        compiler_params=pltpu.CompilerParams(
            collective_id=0, has_side_effects=True, vmem_limit_bytes=60 * 1024 * 1024
        ),
    )(images, captions, labels.reshape(1, rows), logit_scale, logit_bias)
    return (loss.reshape(rows), image_grad.astype(F32), text_grad.astype(F32))


def solution(mesh):
    body = functools.partial(per_device, mesh.shape["blk"])
    in_specs = (P(("blk", "group"), None), P(("blk", "group"), None), P(("blk", "group")), P(), P())
    out_specs = (P(("blk", "group")), P(("blk", "group"), None), P(("blk", "group"), None))
    return jax.shard_map(body, mesh=mesh, in_specs=in_specs, out_specs=out_specs, check_vma=False)
```
